32 devices in a mesh: dp: 8 (over z, x), tensor: 4 (over y, core).
Axes of the slice: x: 2, y: 2, z: 4, core: 2. Of those that a mesh axis runs over, the one named last changes fastest.
Arguments:
- layer_in: bfloat16 [4096, 1024], P(('dp', 'tensor')), may hold values from -6 to 6
- mixer_gain: float32 [1024], replicated, may hold values from 0.5 to 1.5
- w_mix: bfloat16 [1024, 8, 768], P('dp', 'tensor'), may hold values from -0.1875 to 0.1875
- w_rates: bfloat16 [1024, 8, 2], P('dp', 'tensor'), may hold values from -0.1875 to 0.1875
- conv_taps: bfloat16 [4, 8, 512], P(None, 'tensor', 'dp'), may hold values from -3 to 3
- a_log: float32 [8], replicated, may hold values from 0 to 2.77
- dt_bias: float32 [8], replicated, may hold values from -6.9 to -2.3
- head_gain: float32 [256], replicated, may hold values from 0.5 to 1.5
- w_out: bfloat16 [2048, 1024], P('tensor', 'dp'), may hold values from -0.25 to 0.25
- ffn_gain: float32 [1024], replicated, may hold values from 0.5 to 1.5
- w_gate_up: bfloat16 [1024, 2, 2816], P('dp', None, 'tensor'), may hold values from -0.1875 to 0.1875
- w_down: bfloat16 [2816, 1024], P('tensor', 'dp'), may hold values from -0.15625 to 0.15625
- out_grad: bfloat16 [4096, 1024], P(('dp', 'tensor')), may hold values from -6 to 6
Outputs:
- layer_out: bfloat16 [4096, 1024], P(('dp', 'tensor'))
- in_grad: float32 [4096, 1024], P(('dp', 'tensor'))
- grad_mixer_gain: float32 [1024], replicated
- grad_w_mix: float32 [1024, 8, 768], P('dp', 'tensor')
- grad_w_rates: float32 [1024, 8, 2], P('dp', 'tensor')
- grad_conv_taps: float32 [4, 8, 512], P(None, 'tensor', 'dp')
- grad_a_log: float32 [8], replicated
- grad_dt_bias: float32 [8], replicated
- grad_head_gain: float32 [256], replicated
- grad_w_out: float32 [2048, 1024], P('tensor', 'dp')
- grad_ffn_gain: float32 [1024], replicated
- grad_w_gate_up: float32 [1024, 2, 2816], P('dp', None, 'tensor')
- grad_w_down: float32 [2816, 1024], P('tensor', 'dp')
The draws below stay inside these ranges and needn't reach their ends.
All inputs are finite; a program needn't handle non-finite values.
Results may differ from the reference program's by a relative error of at most 0.017.
Values may be sent and summed in bfloat16 or wider, within the bound.
No kernel may reach another device: no remote copies, remote signals or barrier semaphores. Data moves between devices by JAX's collectives and lax.ppermute only.
A program may use at most 128 MiB of HBM per device.

```python
import math
import jax
import jax.numpy as jnp
from jax import lax

D = 1024
H = 8
DK = 128
DV = 256
FF = 2816
CONV = 4
GROUP = 64
SEQ = 512
TOKENS = 4096
N_DP = 8


def spiked(values, own_key, source, target, parts, factor):
    def block_of(axis_at):
        return (jnp.arange(values.shape[axis_at]) // (values.shape[axis_at] // parts)).reshape((-1,) + (1,) * (values.ndim - 1 - axis_at))

    first = jax.random.permutation(own_key, parts)[block_of(target)]
    other_side = (block_of(target) + parts // 2) % parts
    return jnp.where((block_of(source) == first) | (block_of(source) == other_side), factor * values, values)


def levels(rng, shape, shards, smallest, largest):
    def one(dim, parts):
        steps = jax.random.uniform(jax.random.fold_in(jax.random.fold_in(rng, 6), dim), (parts,), jnp.float32, smallest / len(shards), largest / len(shards))
        return jnp.repeat(jnp.exp(steps), shape[dim] // parts).reshape((-1,) + (1,) * (len(shape) - dim - 1))

    loudness = one(*shards[0])
    for cut in shards[1:]:
        loudness = loudness * one(*cut)
    return loudness


def scatter_about(stream_key, shape, scale, bound, cuts=(), kind=jnp.bfloat16):
    gain = levels(stream_key, shape, cuts, -0.22, 0.18) if cuts else 1.0
    values = jax.random.normal(stream_key, shape, jnp.float32) * scale * gain
    return jnp.minimum(jnp.maximum(values, -bound), bound).astype(kind)


def gaussian_with(own_key, extent, scale, reach, split, heavy, held_as=jnp.bfloat16):
    drawn = scale * jax.random.normal(own_key, extent, jnp.float32)
    if split:
        drawn = drawn * levels(own_key, extent, split, -0.22, 0.18)
    return jnp.clip(spiked(drawn, jax.random.fold_in(own_key, 3), *heavy), -reach, reach).astype(held_as)


def setup_inputs(seed: int = 0) -> dict:
    streams_of = jax.random.split(jax.random.key(seed), 14)
    return {
        "layer_in": gaussian_with(streams_of[0], (TOKENS, D), 1.0, 6.0, ((0, 32),), (0, 1, 32, 2.75)),
        "mixer_gain": jnp.clip(1.0 + 0.1 * jax.random.normal(streams_of[1], (D,), jnp.float32), 0.5, 1.5),
        "w_mix": scatter_about(streams_of[2], (D, H, 2 * DK + 2 * DV), D ** -0.5, 0.1875, ((0, 8), (1, 4))),
        "w_rates": scatter_about(streams_of[3], (D, H, 2), D ** -0.5, 0.1875, ((0, 8), (1, 4))),
        "conv_taps": scatter_about(streams_of[4], (CONV, H, 2 * DK + DV), CONV ** -0.5, 3.0, ((1, 4), (2, 8))),
        "a_log": jnp.clip(jax.random.uniform(streams_of[5], (H,), jnp.float32, 0.0, 2.77), 0.0, 2.77),
        "dt_bias": jnp.clip(jax.random.uniform(streams_of[6], (H,), jnp.float32, -6.9, -2.3), -6.9, -2.3),
        "head_gain": jnp.clip(1.0 + 0.1 * jax.random.normal(streams_of[7], (DV,), jnp.float32), 0.5, 1.5),
        "w_out": scatter_about(streams_of[8], (H * DV, D), (H * DV // 4) ** -0.5, 0.25, ((0, 4), (1, 8))),
        "ffn_gain": jnp.clip(1.0 + 0.1 * jax.random.normal(streams_of[9], (D,), jnp.float32), 0.5, 1.5),
        "w_gate_up": scatter_about(streams_of[10], (D, 2, FF), D ** -0.5, 0.1875, ((0, 8), (2, 4))),
        "w_down": scatter_about(streams_of[11], (FF, D), (FF // 2) ** -0.5, 0.15625, ((0, 4), (1, 8))),
        "out_grad": gaussian_with(streams_of[12], (TOKENS, D), 1.0, 6.0, ((0, 32),), (0, 1, 32, 2.75)),
    }


highest = lax.Precision.HIGHEST
NORM_EPS = 1e-05
UNIT_EPS = 1e-06

@jax.custom_vjp
def low(v):
    return lax.optimization_barrier(v.astype(jnp.bfloat16)).astype(jnp.float32)

@jax.custom_vjp
def low_back(v):
    return v

def low_keep(v):
    return (low(v), None)

def low_pass(kept, grad):
    return (grad,)

def back_keep(v):
    return (v, None)

def back_low(kept, grad):
    return (low(grad),)
low.defvjp(low_keep, low_pass)
low_back.defvjp(back_keep, back_low)

def scale_norm(matrix, scale_gain):
    return matrix * lax.rsqrt(lax.optimization_barrier(jnp.mean(matrix * matrix, axis=-1, keepdims=True)) + NORM_EPS) * scale_gain

def unit_rows(matrix):
    return matrix * lax.rsqrt(lax.optimization_barrier(jnp.sum(matrix * matrix, axis=-1, keepdims=True)) + UNIT_EPS)

def group_step(state_now, block):
    queries, key_rows, val_rows, log_decay, strength = block
    width = log_decay.shape[1]
    cumulative = jnp.cumsum(log_decay, axis=1)
    row_ids = lax.broadcasted_iota(jnp.int32, (width, width), 0)
    col_ids = lax.broadcasted_iota(jnp.int32, (width, width), 1)
    lower_mask = row_ids >= col_ids
    strict_mask = row_ids > col_ids
    spread = cumulative[:, :, None] - cumulative[:, None, :]
    decay_map = jnp.where(lower_mask, jnp.exp(jnp.where(lower_mask, spread, 0.0)), 0.0)
    key_dots = jnp.einsum('hid,hjd->hij', key_rows, key_rows, precision=highest)
    system = jnp.where(strict_mask, strength[:, :, None] * key_dots * decay_map, 0.0) + jnp.eye(width, dtype=jnp.float32)
    start_decay = jnp.exp(cumulative)
    right_side = jnp.concatenate([(strength * start_decay)[:, :, None] * key_rows, strength[:, :, None] * val_rows], axis=2)
    solved = jax.scipy.linalg.solve_triangular(system, right_side, lower=True)
    key_width = key_rows.shape[2]
    carried = solved[:, :, key_width:] - jnp.einsum('hcd,hde->hce', solved[:, :, :key_width], state_now, precision=highest)
    scores = jnp.einsum('hid,hjd->hij', queries, key_rows, precision=highest) * decay_map
    output = start_decay[:, :, None] * jnp.einsum('hcd,hde->hce', queries, state_now, precision=highest)
    output = output + jnp.einsum('hij,hje->hie', scores, carried, precision=highest)
    final_decay = cumulative[:, -1:]
    remaining = jnp.exp(final_decay - cumulative)
    state_next = jnp.exp(final_decay)[:, :, None] * state_now
    state_next = state_next + jnp.einsum('hjd,hje->hde', key_rows * remaining[:, :, None], carried, precision=highest)
    return (state_next, output)

def to_blocks(matrix):
    length = matrix.shape[0]
    shaped = matrix.reshape((length // GROUP, GROUP) + matrix.shape[1:])
    return jnp.moveaxis(shaped, 2, 1)

def mixer_core(project, rates, taps, a_log, dt_bias, head_gain, first_head):
    heads_here = project.shape[1]
    channels = taps.shape[2]
    value_width = head_gain.shape[0]
    key_width = (channels - value_width) // 2
    length = project.shape[0]
    padded = jnp.pad(project[:, :, :channels], ((CONV - 1, 0), (0, 0), (0, 0)))
    mixed = taps[0] * padded[0:length]
    for offset in range(1, CONV):
        mixed = mixed + taps[offset] * padded[offset:offset + length]
    mixed = jax.nn.silu(mixed)
    queries = unit_rows(mixed[:, :, :key_width]) * key_width ** (-0.5)
    key_rows = unit_rows(mixed[:, :, key_width:2 * key_width])
    val_rows = mixed[:, :, 2 * key_width:]
    log_rate = lax.dynamic_slice_in_dim(a_log, first_head, heads_here)
    bias_here = lax.dynamic_slice_in_dim(dt_bias, first_head, heads_here)
    log_decay = -jnp.exp(log_rate) * jax.nn.softplus(rates[:, :, 0] + bias_here)
    strength = jax.nn.sigmoid(rates[:, :, 1])
    initial = jnp.zeros((heads_here, key_width, value_width), jnp.float32)
    blocks = (to_blocks(queries), to_blocks(key_rows), to_blocks(val_rows), to_blocks(log_decay), to_blocks(strength))
    final_state, outputs = lax.scan(jax.checkpoint(group_step), initial, blocks)
    outputs = jnp.moveaxis(outputs, 1, 2).reshape(length, heads_here, value_width)
    gated = scale_norm(outputs, head_gain) * jax.nn.silu(project[:, :, channels:])
    return gated.reshape(length, heads_here * value_width)

def layer(resid_in, mixer_gain, w_mix, w_rates, conv_taps, a_log, dt_bias, head_gain, w_out, ffn_gain, w_gate_up, w_down):
    normed = low(scale_norm(resid_in, mixer_gain))
    project = low_back(jnp.einsum('bsd,dhc->bshc', normed, w_mix, precision=highest))
    rates = low_back(jnp.einsum('bsd,dhc->bshc', normed, w_rates, precision=highest))

    def core_one(project_one, rates_one):
        return mixer_core(project_one, rates_one, conv_taps, a_log, dt_bias, head_gain, jnp.int32(0))
    gated = low(jax.vmap(core_one)(project, rates))
    mixer_out = low_back(jnp.einsum('bsc,cd->bsd', gated, w_out, precision=highest))
    resid = resid_in + mixer_out
    ffn_in = low(scale_norm(resid, ffn_gain))
    gate_up = low_back(jnp.einsum('bsd,dgf->bsgf', ffn_in, w_gate_up, precision=highest))
    hidden = low(jax.nn.silu(gate_up[:, :, 0]) * gate_up[:, :, 1])
    ffn_out = low_back(jnp.einsum('bsf,fd->bsd', hidden, w_down, precision=highest))
    return resid + ffn_out

def reference(layer_in, mixer_gain, w_mix, w_rates, conv_taps, a_log, dt_bias, head_gain, w_out, ffn_gain, w_gate_up, w_down, out_grad):
    batch_seqs = math.gcd(N_DP, max(1, 4096 // SEQ))
    turns = N_DP // batch_seqs
    params = tuple((p_item.astype(jnp.float32) for p_item in (mixer_gain, w_mix, w_rates, conv_taps, a_log, dt_bias, head_gain, w_out, ffn_gain, w_gate_up, w_down)))
    inputs = layer_in.astype(jnp.float32).reshape(turns, batch_seqs, SEQ, D)
    cotangents = out_grad.astype(jnp.float32).reshape(turns, batch_seqs, SEQ, D)

    def visit(totals, item):
        rows_now, grads_now = item
        result, back = jax.vjp(layer, rows_now, *params)
        grads = back(grads_now)
        summed = tuple((held + fresh for held, fresh in zip(totals, grads[1:])))
        return (summed, (result, grads[0]))
    start_totals = tuple((jnp.zeros(p_item.shape, jnp.float32) for p_item in params))
    totals, (results, in_grads) = lax.scan(visit, start_totals, (inputs, cotangents))
    layer_out = results.reshape(TOKENS, D).astype(jnp.bfloat16)
    in_grad = in_grads.reshape(TOKENS, D)
    return (layer_out, in_grad, totals[0], totals[1], totals[2], totals[3], totals[4], totals[5], totals[6], totals[7], totals[8], totals[9], totals[10])
```

```python
import jax
import jax.numpy as jnp
from jax import lax
from jax.sharding import PartitionSpec as P

CONV = 4
GROUP = 64


highest = lax.Precision.HIGHEST
NORM_EPS = 1e-05
UNIT_EPS = 1e-06
bf16 = jnp.bfloat16
f32 = jnp.float32


def scale_norm(matrix, scale_gain):
    return (
        matrix
        * lax.rsqrt(jnp.mean(matrix * matrix, axis=-1, keepdims=True) + NORM_EPS)
        * scale_gain
    )


def unit_rows(matrix):
    return matrix * lax.rsqrt(jnp.sum(matrix * matrix, axis=-1, keepdims=True) + UNIT_EPS)


def group_step(state_now, block):
    queries, key_rows, val_rows, log_decay, strength = block
    width = log_decay.shape[1]
    cumulative = jnp.cumsum(log_decay, axis=1)
    row_ids = lax.broadcasted_iota(jnp.int32, (width, width), 0)
    col_ids = lax.broadcasted_iota(jnp.int32, (width, width), 1)
    lower_mask = row_ids >= col_ids
    strict_mask = row_ids > col_ids
    spread = cumulative[:, :, None] - cumulative[:, None, :]
    decay_map = jnp.where(lower_mask, jnp.exp(jnp.where(lower_mask, spread, 0.0)), 0.0)
    key_dots = jnp.einsum("hid,hjd->hij", key_rows, key_rows, precision=highest)
    system = jnp.where(strict_mask, strength[:, :, None] * key_dots * decay_map, 0.0) + jnp.eye(
        width, dtype=jnp.float32
    )
    start_decay = jnp.exp(cumulative)
    right_side = jnp.concatenate(
        [(strength * start_decay)[:, :, None] * key_rows, strength[:, :, None] * val_rows], axis=2
    )
    solved = jax.scipy.linalg.solve_triangular(system, right_side, lower=True)
    key_width = key_rows.shape[2]
    carried = solved[:, :, key_width:] - jnp.einsum(
        "hcd,hde->hce", solved[:, :, :key_width], state_now, precision=highest
    )
    scores = jnp.einsum("hid,hjd->hij", queries, key_rows, precision=highest) * decay_map
    output = start_decay[:, :, None] * jnp.einsum(
        "hcd,hde->hce", queries, state_now, precision=highest
    )
    output = output + jnp.einsum("hij,hje->hie", scores, carried, precision=highest)
    final_decay = cumulative[:, -1:]
    remaining = jnp.exp(final_decay - cumulative)
    state_next = jnp.exp(final_decay)[:, :, None] * state_now
    state_next = state_next + jnp.einsum(
        "hjd,hje->hde", key_rows * remaining[:, :, None], carried, precision=highest
    )
    return (state_next, output)


def to_blocks(matrix):
    length = matrix.shape[0]
    shaped = matrix.reshape((length // GROUP, GROUP) + matrix.shape[1:])
    return jnp.moveaxis(shaped, 2, 1)


def mixer_core(project, rates, taps, a_log, dt_bias, head_gain, first_head):
    heads_here = project.shape[1]
    channels = taps.shape[2]
    value_width = head_gain.shape[0]
    key_width = (channels - value_width) // 2
    length = project.shape[0]
    padded = jnp.pad(project[:, :, :channels], ((CONV - 1, 0), (0, 0), (0, 0)))
    mixed = taps[0] * padded[0:length]
    for offset in range(1, CONV):
        mixed = mixed + taps[offset] * padded[offset : offset + length]
    mixed = jax.nn.silu(mixed)
    queries = unit_rows(mixed[:, :, :key_width]) * key_width ** (-0.5)
    key_rows = unit_rows(mixed[:, :, key_width : 2 * key_width])
    val_rows = mixed[:, :, 2 * key_width :]
    log_rate = lax.dynamic_slice_in_dim(a_log, first_head, heads_here)
    bias_here = lax.dynamic_slice_in_dim(dt_bias, first_head, heads_here)
    log_decay = -jnp.exp(log_rate) * jax.nn.softplus(rates[:, :, 0] + bias_here)
    strength = jax.nn.sigmoid(rates[:, :, 1])
    initial = jnp.zeros((heads_here, key_width, value_width), jnp.float32)
    blocks = (
        to_blocks(queries),
        to_blocks(key_rows),
        to_blocks(val_rows),
        to_blocks(log_decay),
        to_blocks(strength),
    )
    final_state, outputs = lax.scan(group_step, initial, blocks)
    outputs = jnp.moveaxis(outputs, 1, 2).reshape(length, heads_here, value_width)
    gated = scale_norm(outputs, head_gain) * jax.nn.silu(project[:, :, channels:])
    return gated.reshape(length, heads_here * value_width)


def gate_product(gate_up):
    return jax.nn.silu(gate_up[:, 0]) * gate_up[:, 1]


def rows_dot(left, right, kind=f32):
    return lax.dot_general(
        left, right, (((0,), (0,)), ((), ())), preferred_element_type=f32
    ).astype(kind)


def cols_dot(left, right):
    return lax.dot_general(left, right, (((1,), (1,)), ((), ())), preferred_element_type=f32)


def dot(left, right):
    return jnp.dot(left, right, preferred_element_type=f32)


def swap(array, axis, size, offset):
    return lax.ppermute(array, axis, [(i, i ^ offset) for i in range(size)])


class Dp:
    def __init__(self, size):
        self.size = size
        self.near = size == 8
        self.half = size // 2
        self.offsets = [2 * p for p in range(self.half)] + [2 * p + 1 for p in range(self.half)]
        self.places = [self.offsets.index(k) for k in range(size)]

    def blocks_to_order(self, array):
        if not self.near:
            return array
        parts = array.reshape(array.shape[:-1] + (self.size, -1))
        index = lax.axis_index("dp") ^ jnp.array(self.offsets, jnp.int32)
        return jnp.take(parts, index, axis=-2).reshape(array.shape)

    def blocks_from_order(self, array):
        if not self.near:
            return array
        parts = array.reshape(array.shape[:-1] + (self.size, -1))
        index = jnp.array(self.places, jnp.int32)[lax.axis_index("dp") ^ jnp.arange(self.size, dtype=jnp.int32)]
        return jnp.take(parts, index, axis=-2).reshape(array.shape)

    def gather_start(self, shard):
        return [shard] + [swap(shard, "dp", self.size, 2 * p) for p in range(1, self.half)]

    def gather_end(self, evens):
        return evens + [swap(e, "dp", self.size, 1) for e in evens]

    def gather(self, shard):
        if not self.near:
            whole = lax.all_gather(shard, "dp", axis=0, tiled=False)
            return [whole[k] for k in range(self.size)]
        return self.gather_end(self.gather_start(shard))

    def scatter(self, evens, odds, axis):
        if not self.near:
            return lax.psum_scatter(
                jnp.concatenate([evens, odds.astype(evens.dtype)], axis),
                "dp",
                scatter_dimension=axis,
                tiled=True,
            )
        kind = odds.dtype
        summed = evens + swap(odds, "dp", self.size, 1).astype(f32)
        parts = jnp.split(summed, self.half, axis)
        total = parts[0]
        for p in range(1, self.half):
            total = total + swap(parts[p].astype(kind), "dp", self.size, 2 * p).astype(f32)
        return total


def gather_rows(rows, size):
    blocks = {0: rows}
    step = size // 2
    while step:
        for k in sorted(blocks):
            blocks[k ^ step] = swap(blocks[k], "tensor", size, step)
        step //= 2
    return [blocks[k] for k in range(size)]


def sum_rows(blocks, kind):
    size = len(blocks)
    blocks = dict(enumerate(blocks))
    step = 1
    while step < size:
        keep = {k: blocks[k] for k in blocks if not k & step}
        blocks = {
            k: keep[k] + swap(blocks[k ^ step].astype(kind), "tensor", size, step).astype(f32)
            for k in keep
        }
        step *= 2
    return blocks[0]


def in_time(blocks):
    length = blocks[0].shape[0]
    whole = jnp.zeros((len(blocks) * length,) + blocks[0].shape[1:], blocks[0].dtype)
    me = lax.axis_index("tensor")
    for k, block in enumerate(blocks):
        whole = lax.dynamic_update_slice_in_dim(whole, block, (me ^ k) * length, 0)
    return whole


def from_time(whole, size):
    length = whole.shape[0] // size
    me = lax.axis_index("tensor")
    return [lax.dynamic_slice_in_dim(whole, (me ^ k) * length, length, 0) for k in range(size)]


def after(arrays, others):
    kept, _ = lax.optimization_barrier((arrays, others))
    return kept


def per_device(
    layer_in,
    mixer_gain,
    w_mix,
    w_rates,
    conv_taps,
    a_log,
    dt_bias,
    head_gain,
    w_out,
    ffn_gain,
    w_gate_up,
    w_down,
    out_grad,
):
    dp = Dp(lax.axis_size("dp"))
    ranks = lax.axis_size("tensor")
    depth, heads_here, head_width = w_mix.shape
    hidden_here = w_gate_up.shape[2]
    channels = conv_taps.shape[2] * dp.size
    taps_shape = conv_taps.shape

    mix_shard = w_mix.reshape(depth, heads_here * head_width)
    gate_up_shard = w_gate_up.reshape(depth, 2 * hidden_here)
    small_shard = jnp.concatenate([w_rates.reshape(-1), conv_taps.reshape(-1)])
    small_size = w_rates.size
    small_slots = dp.gather(small_shard.reshape(8, -1))
    mix_slots = dp.gather(mix_shard)
    mix_full = jnp.concatenate(mix_slots, 0)
    small_flat = [s.reshape(-1) for s in small_slots]
    rates_full = jnp.concatenate([s[:small_size].reshape(depth, -1) for s in small_flat], 0)
    taps_order = jnp.concatenate([s[small_size:].reshape(taps_shape) for s in small_flat], 2)
    taps_full = dp.blocks_from_order(taps_order).astype(f32)

    resid_in = dp.blocks_to_order(layer_in).astype(f32)
    mixer_gain = dp.blocks_to_order(mixer_gain)
    ffn_gain = dp.blocks_to_order(ffn_gain)
    out_grad = dp.blocks_to_order(out_grad)

    normed, norm_back = jax.vjp(scale_norm, resid_in, mixer_gain)
    normed_all = in_time(gather_rows(normed.astype(bf16), ranks))
    out_shard, gate_up_shard, down_shard = after((w_out, gate_up_shard, w_down), mix_full)
    out_full = jnp.concatenate(dp.gather(out_shard), 1)
    gate_up_full = jnp.concatenate(dp.gather(gate_up_shard), 0)
    down_full = jnp.concatenate(dp.gather(down_shard), 1)

    project = dot(normed_all, mix_full).reshape(-1, heads_here, head_width)
    rates = dot(normed_all, rates_full).reshape(-1, heads_here, 2)
    first_head = lax.axis_index("tensor") * heads_here

    def core_local(project_in, rates_in, taps_in, log_rates, decay_bias, gain_in):
        return mixer_core(project_in, rates_in, taps_in, log_rates, decay_bias, gain_in, first_head)

    gated, core_back = jax.vjp(core_local, project, rates, taps_full, a_log, dt_bias, head_gain)
    gated_low = gated.astype(bf16)
    mixer_out = sum_rows(from_time(dot(gated_low, out_full), ranks), bf16)
    resid = resid_in + mixer_out
    ffn_in, ffn_back = jax.vjp(scale_norm, resid, ffn_gain)
    ffn_all = jnp.concatenate(gather_rows(ffn_in.astype(bf16), ranks), 0)
    top_grad = jnp.concatenate(gather_rows(out_grad, ranks), 0)
    gate_up = dot(ffn_all, gate_up_full).reshape(-1, 2, hidden_here)
    hidden, act_back = jax.vjp(gate_product, gate_up)
    hidden_low = hidden.astype(bf16)
    ffn_out = sum_rows(jnp.split(dot(hidden_low, down_full), ranks, 0), bf16)
    layer_out = dp.blocks_from_order((resid + ffn_out).astype(bf16))
    half = top_grad.shape[1] // 2
    grad_hidden = cols_dot(top_grad, down_full)
    (grad_gate_up,) = act_back(grad_hidden)
    grad_gate_low = grad_gate_up.astype(bf16).reshape(-1, 2 * hidden_here)
    grad_ffn_in = sum_rows(jnp.split(cols_dot(grad_gate_low, gate_up_full), ranks, 0), bf16)
    grad_resid_norm, grad_ffn_gain = ffn_back(grad_ffn_in)
    grad_resid = out_grad.astype(f32) + grad_resid_norm
    mix_grad = in_time(gather_rows(grad_resid.astype(bf16), ranks))
    grad_w_gate_up = dp.scatter(
        rows_dot(ffn_all[:, :half], grad_gate_low), rows_dot(ffn_all[:, half:], grad_gate_low, bf16), 0
    )
    grad_w_down = dp.scatter(
        rows_dot(hidden_low, top_grad[:, :half]), rows_dot(hidden_low, top_grad[:, half:], bf16), 1
    )
    grad_gated = cols_dot(mix_grad, out_full)
    grad_w_out = dp.scatter(
        rows_dot(gated_low, mix_grad[:, :half]), rows_dot(gated_low, mix_grad[:, half:], bf16), 1
    )
    grad_project, grad_rates, local_taps, grad_log_rates, grad_decay_bias, grad_gain_here = (
        core_back(grad_gated)
    )
    project_low = grad_project.astype(bf16).reshape(-1, heads_here * head_width)
    rates_low = grad_rates.astype(bf16).reshape(-1, heads_here * 2)
    back_terms = cols_dot(project_low, mix_full) + cols_dot(rates_low, rates_full)
    grad_w_mix = dp.scatter(
        rows_dot(normed_all[:, :half], project_low), rows_dot(normed_all[:, half:], project_low, bf16), 0
    )
    grad_normed = sum_rows(from_time(back_terms, ranks), bf16)
    local_rates = rows_dot(normed_all, rates_low).reshape(dp.size, -1)
    local_taps = dp.blocks_to_order(local_taps).reshape(taps_shape[:2] + (dp.size, -1))
    local_taps = jnp.moveaxis(local_taps, 2, 0).reshape(dp.size, -1)
    local_small = jnp.concatenate([local_rates, local_taps], 1)
    summed_small = dp.scatter(local_small[: dp.half], local_small[dp.half :], 0).reshape(-1)
    grad_w_rates = summed_small[:small_size].reshape(w_rates.shape)
    grad_conv_taps = summed_small[small_size:].reshape(taps_shape)
    grad_input_norm, grad_gain_first = norm_back(grad_normed)
    in_grad = dp.blocks_from_order(grad_resid + grad_input_norm)
    grad_mixer_gain, grad_ffn_total, grad_head_gain, grad_a_log, grad_dt_bias = lax.psum(
        (
            dp.blocks_from_order(grad_gain_first),
            dp.blocks_from_order(grad_ffn_gain),
            grad_gain_here,
            grad_log_rates,
            grad_decay_bias,
        ),
        ("dp", "tensor"),
    )
    return (
        layer_out,
        in_grad,
        grad_mixer_gain,
        grad_w_mix.reshape(w_mix.shape),
        grad_w_rates,
        grad_conv_taps,
        grad_a_log,
        grad_dt_bias,
        grad_head_gain,
        grad_w_out,
        grad_ffn_total,
        grad_w_gate_up.reshape(w_gate_up.shape),
        grad_w_down,
    )


def solution(mesh):
    return jax.shard_map(
        per_device,
        mesh=mesh,
        in_specs=(
            P(("dp", "tensor"), None),
            P(),
            P("dp", "tensor", None),
            P("dp", "tensor", None),
            P(None, "tensor", "dp"),
            P(),
            P(),
            P(),
            P("tensor", "dp"),
            P(),
            P("dp", None, "tensor"),
            P("tensor", "dp"),
            P(("dp", "tensor"), None),
        ),
        out_specs=(
            P(("dp", "tensor"), None),
            P(("dp", "tensor"), None),
            P(),
            P("dp", "tensor", None),
            P("dp", "tensor", None),
            P(None, "tensor", "dp"),
            P(),
            P(),
            P(),
            P("tensor", "dp"),
            P(),
            P("dp", None, "tensor"),
            P("tensor", "dp"),
        ),
        check_vma=False,
    )
```

```python
import jax
import jax.numpy as jnp
from jax import lax
from jax.experimental import pallas as pl
from jax.experimental.pallas import tpu as pltpu
from jax.sharding import PartitionSpec as P

CONV = 4


highest = lax.Precision.HIGHEST
NORM_EPS = 1e-05
UNIT_EPS = 1e-06
bf16 = jnp.bfloat16
f32 = jnp.float32


def scale_norm(matrix, scale_gain):
    return (
        matrix
        * lax.rsqrt(jnp.mean(matrix * matrix, axis=-1, keepdims=True) + NORM_EPS)
        * scale_gain
    )


def gate_product(gate_up):
    return jax.nn.silu(gate_up[:, 0]) * gate_up[:, 1]


def rows_dot(left, right, kind=f32):
    return lax.dot_general(
        left, right, (((0,), (0,)), ((), ())), preferred_element_type=f32
    ).astype(kind)


def cols_dot(left, right):
    return lax.dot_general(left, right, (((1,), (1,)), ((), ())), preferred_element_type=f32)


def dot(left, right):
    return jnp.dot(left, right, preferred_element_type=f32)


CHUNK = 128
LANES = 128


def mul(left, right, over=(1, 0), exact=False):
    dims = (((over[0],), (over[1],)), ((), ()))
    if exact:
        return lax.dot_general(left, right, dims, precision=highest, preferred_element_type=f32)
    return lax.dot_general(left.astype(bf16), right.astype(bf16), dims, preferred_element_type=f32)


def square_ids():
    shape = (CHUNK, CHUNK)
    return lax.broadcasted_iota(jnp.int32, shape, 0), lax.broadcasted_iota(jnp.int32, shape, 1)


def sigmoid(v):
    return 1.0 / (1.0 + jnp.exp(-v))


def softplus(v):
    return jnp.maximum(v, 0.0) + jnp.log1p(jnp.exp(-jnp.abs(v)))


def row_sum(v):
    return jnp.sum(v, axis=1, keepdims=True)


def unit_inverse(lower):
    rows, cols = square_ids()
    inverse = jnp.where(rows == cols, 1.0, 0.0)
    block = 1
    while block < CHUNK:
        corner = (
            (rows // (2 * block) == cols // (2 * block))
            & ((rows // block) % 2 == 1)
            & ((cols // block) % 2 == 0)
        )
        part = jnp.where(corner, lower, 0.0)
        if block == 1:
            inverse = inverse - part
        else:
            inverse = inverse - mul(mul(inverse, part), inverse)
        block *= 2
    return inverse


def shifted(ref, start, back, columns):
    if start == 0 and back:
        rows = lax.broadcasted_iota(jnp.int32, (CHUNK, columns.stop - columns.start), 0)
        return jnp.where(rows >= back, pltpu.roll(ref[0:CHUNK, columns], back, 0), 0.0)
    return ref[start - back : start - back + CHUNK, columns]


def short_conv(project_ref, taps_ref, start, columns, tap_columns):
    total = None
    for tap in range(CONV):
        term = taps_ref[tap : tap + 1, tap_columns] * shifted(
            project_ref, start, CONV - 1 - tap, columns
        )
        total = term if total is None else total + term
    return total


def decays(rates, log_rates, bias):
    log_decay = -jnp.exp(log_rates) * softplus(rates + bias)
    place = lax.broadcasted_iota(jnp.int32, rates.shape, 0)
    total = log_decay
    step = 1
    while step < CHUNK:
        total = total + jnp.where(place >= step, pltpu.roll(total, step, 0), 0.0)
        step *= 2
    return log_decay, total


def chunk_terms(head, project_ref, taps_ref, start, total, total_rows, strength, key_width, value_width):
    width = 2 * key_width + 2 * value_width
    base, tap_base = head * width, head * (2 * key_width + value_width)
    terms = {}
    parts = (("q", 0, key_width), ("k", key_width, key_width), ("v", 2 * key_width, value_width))
    for name, at, size in parts:
        pre = short_conv(
            project_ref,
            taps_ref,
            start,
            slice(base + at, base + at + size),
            slice(tap_base + at, tap_base + at + size),
        )
        gate = sigmoid(pre)
        mixed = pre * gate
        if name != "v":
            scale = lax.rsqrt(row_sum(mixed * mixed) + UNIT_EPS)
            mixed = mixed * scale
            terms[name + "_scale"] = scale
        terms[name + "_slope"] = (pre, gate)
        terms[name] = mixed
    terms["unit_q"] = terms["q"]
    terms["q"] = terms["q"] * key_width ** (-0.5)
    lane = 2 * head
    sums = total[:, lane : lane + 1]
    across = total_rows[lane : lane + 1, :]
    rows, cols = square_ids()
    decay = jnp.where(rows >= cols, jnp.exp(jnp.minimum(sums - across, 0.0)), 0.0)
    final = total[CHUNK - 1 : CHUNK, lane : lane + 1]
    terms["b"] = strength[:, lane + 1 : lane + 2]
    terms["since"] = jnp.exp(sums)
    terms["remaining"] = jnp.exp(final - sums)
    terms["through"] = jnp.exp(final)
    terms["decay"] = decay
    terms["dots"] = mul(terms["k"], terms["k"], (1, 1)) * jnp.where(rows > cols, decay, 0.0)
    terms["scores"] = mul(terms["q"], terms["k"], (1, 1)) * decay
    return terms


def mixer_forward(
    normed_ref,
    mix_ref,
    rates_w_ref,
    taps_ref,
    log_rates_ref,
    bias_ref,
    gain_ref,
    gated_ref,
    project_ref,
    rates_ref,
    out_ref,
    states_ref,
    carried_ref,
    inverse_ref,
    q_scr,
    kr_scr,
    p_scr,
    w_scr,
    u_scr,
):
    length = normed_ref.shape[0]
    value_width = gain_ref.shape[1]
    heads = out_ref.shape[1] // value_width
    width = project_ref.shape[1] // heads
    key_width = (width - 2 * value_width) // 2
    chunks = length // CHUNK
    for head in range(heads):
        columns = slice(head * width, (head + 1) * width)
        project_ref[:, columns] = dot(normed_ref[...], mix_ref[:, columns])
    rates_ref[...] = dot(normed_ref[...], rates_w_ref[...])
    through = {}
    for chunk in range(chunks):
        start = chunk * CHUNK
        rows = slice(start, start + CHUNK)
        rates = rates_ref[rows, :]
        _, total = decays(rates, log_rates_ref[...], bias_ref[...])
        strength = sigmoid(rates)
        total_rows = jnp.transpose(total)
        for head in range(heads):
            t = chunk_terms(
                head, project_ref, taps_ref, start, total, total_rows, strength, key_width, value_width
            )
            inverse = unit_inverse(t["b"] * t["dots"])
            inverse_ref[chunk, head] = inverse
            side = jnp.concatenate([(t["b"] * t["since"]) * t["k"], t["b"] * t["v"]], 1)
            solved = mul(inverse, side)
            w_scr[chunk, head] = solved[:, :key_width].astype(bf16)
            u_scr[chunk, head] = solved[:, key_width:]
            q_scr[chunk, head] = (t["q"] * t["since"]).astype(bf16)
            kr_scr[chunk, head] = (t["k"] * t["remaining"]).astype(bf16)
            p_scr[chunk, head] = t["scores"].astype(bf16)
            through[chunk, head] = t["through"]
    state = [jnp.zeros((key_width, value_width), f32) for _ in range(heads)]
    for chunk in range(chunks):
        rows = slice(chunk * CHUNK, (chunk + 1) * CHUNK)
        for head in range(heads):
            columns = slice(head * value_width, (head + 1) * value_width)
            states_ref[chunk, head] = state[head]
            low = state[head].astype(bf16)
            carried = u_scr[chunk, head] - mul(w_scr[chunk, head], low)
            carried_ref[rows, columns] = carried
            carried = carried.astype(bf16)
            out_ref[rows, columns] = mul(q_scr[chunk, head], low) + mul(p_scr[chunk, head], carried)
            state[head] = through[chunk, head] * state[head] + mul(
                kr_scr[chunk, head], carried, (0, 0)
            )
    for chunk in range(chunks):
        rows = slice(chunk * CHUNK, (chunk + 1) * CHUNK)
        for head in range(heads):
            columns = slice(head * value_width, (head + 1) * value_width)
            out = out_ref[rows, columns]
            gate = project_ref[rows, (head + 1) * width - value_width : (head + 1) * width]
            scale = lax.rsqrt(row_sum(out * out) / value_width + NORM_EPS)
            gated_ref[rows, columns] = (
                out * scale * gain_ref[...] * (gate * sigmoid(gate))
            ).astype(bf16)


def mixer_backward(
    grad_ref,
    w_out_ref,
    taps_ref,
    log_rates_ref,
    bias_ref,
    gain_ref,
    project_ref,
    rates_ref,
    out_ref,
    states_ref,
    carried_ref,
    inverse_ref,
    grad_project_ref,
    grad_rates_ref,
    grad_taps_ref,
    grad_gain_ref,
    grad_lanes_ref,
    grad_out_scr,
    back_scr,
    grad_carried_scr,
    q_scr,
    kr_scr,
    p_scr,
    w_scr,
    conv_scr,
    mixed_scr,
):
    length = grad_ref.shape[0]
    value_width = gain_ref.shape[1]
    heads = out_ref.shape[1] // value_width
    width = project_ref.shape[1] // heads
    key_width = (width - 2 * value_width) // 2
    channels = 2 * key_width + value_width
    chunks = length // CHUNK
    grad_out_scr[...] = lax.dot_general(
        grad_ref[...], w_out_ref[...], (((1,), (1,)), ((), ())), preferred_element_type=f32
    )
    gain = gain_ref[...]
    gain_total = jnp.zeros((1, value_width), f32)
    terms = {}

    def gather_terms(chunk):
        start = chunk * CHUNK
        rates = rates_ref[start : start + CHUNK, :]
        _, total = decays(rates, log_rates_ref[...], bias_ref[...])
        strength = sigmoid(rates)
        total_rows = jnp.transpose(total)
        return [
            chunk_terms(
                head, project_ref, taps_ref, start, total, total_rows, strength, key_width, value_width
            )
            for head in range(heads)
        ]

    through = {}
    for chunk in range(chunks):
        rows = slice(chunk * CHUNK, (chunk + 1) * CHUNK)
        terms = gather_terms(chunk)
        for head in range(heads):
            columns = slice(head * value_width, (head + 1) * value_width)
            gate_columns = slice((head + 1) * width - value_width, (head + 1) * width)
            t = terms[head]
            out = out_ref[rows, columns]
            gate = project_ref[rows, gate_columns]
            grad = grad_out_scr[rows, columns]
            scale = lax.rsqrt(row_sum(out * out) / value_width + NORM_EPS)
            unit = out * scale
            sig = sigmoid(gate)
            act = gate * sig
            gain_total = gain_total + jnp.sum(grad * unit * act, axis=0, keepdims=True)
            grad_project_ref[rows, gate_columns] = (
                grad * gain * unit * (sig * (1.0 + gate * (1.0 - sig)))
            ).astype(bf16)
            inner = grad * act * gain
            grad_out_scr[rows, columns] = scale * (
                inner - unit * (row_sum(inner * unit) / value_width)
            )
            w_scr[chunk, head] = mul(
                inverse_ref[chunk, head], (t["b"] * t["since"]) * t["k"]
            ).astype(bf16)
            q_scr[chunk, head] = (t["q"] * t["since"]).astype(bf16)
            kr_scr[chunk, head] = (t["k"] * t["remaining"]).astype(bf16)
            p_scr[chunk, head] = t["scores"].astype(bf16)
            through[chunk, head] = t["through"]
    grad_gain_ref[...] = gain_total

    back = [jnp.zeros((key_width, value_width), f32) for _ in range(heads)]
    for chunk in reversed(range(chunks)):
        rows = slice(chunk * CHUNK, (chunk + 1) * CHUNK)
        for head in range(heads):
            columns = slice(head * value_width, (head + 1) * value_width)
            back_scr[chunk, head] = back[head]
            grad_out = grad_out_scr[rows, columns].astype(bf16)
            grad_carried = mul(p_scr[chunk, head], grad_out, (0, 0)) + mul(
                kr_scr[chunk, head], back[head]
            )
            grad_carried_scr[rows, columns] = grad_carried
            back[head] = (
                through[chunk, head] * back[head]
                + mul(q_scr[chunk, head], grad_out, (0, 0))
                - mul(w_scr[chunk, head], grad_carried, (0, 0))
            )

    rows_at, cols_at = square_ids()
    lane = lax.broadcasted_iota(jnp.int32, (CHUNK, LANES), 1)
    place = lax.broadcasted_iota(jnp.int32, (CHUNK, LANES), 0)
    log_total = jnp.zeros((1, LANES), f32)
    bias_total = jnp.zeros((1, LANES), f32)
    for chunk in range(chunks):
        rows = slice(chunk * CHUNK, (chunk + 1) * CHUNK)
        terms = gather_terms(chunk)
        sums_grad = jnp.zeros((CHUNK, LANES), f32)
        strength_grad = jnp.zeros((CHUNK, LANES), f32)
        for head in range(heads):
            columns = slice(head * value_width, (head + 1) * value_width)
            t = terms[head]
            b, since, remaining, decay = t["b"], t["since"], t["remaining"], t["decay"]
            q, k, v = t["q"], t["k"], t["v"]
            state = states_ref[chunk, head]
            back_now = back_scr[chunk, head]
            carried = carried_ref[rows, columns]
            grad_out = grad_out_scr[rows, columns]
            grad_side = mul(inverse_ref[chunk, head], grad_carried_scr[rows, columns], (0, 0))
            strict = jnp.where(rows_at > cols_at, -mul(grad_side, carried, (1, 1)), 0.0)
            grad_scores = mul(grad_out, carried, (1, 1))
            side_state = mul(grad_side, state, (1, 1))
            out_state = since * mul(grad_out, state, (1, 1))
            carried_back = remaining * mul(carried, back_now, (1, 1))
            key_side = since * row_sum(k * side_state)
            strict_dots = strict * t["dots"]
            grad_strength = row_sum(grad_side * v) - key_side + row_sum(strict_dots)
            pulls = grad_scores * t["scores"] + b * strict_dots
            key_back = row_sum(k * carried_back)
            grad_sums = (
                row_sum(pulls - jnp.transpose(pulls))
                - b * key_side
                + row_sum(q * out_state)
                - key_back
            )
            final = jnp.sum(key_back, axis=0, keepdims=True) + t["through"] * jnp.sum(
                row_sum(back_now * state), axis=0, keepdims=True
            )
            scores_low = (grad_scores * decay).astype(bf16)
            strict_low = (strict * (b * decay)).astype(bf16)
            k_low, q_low = k.astype(bf16), q.astype(bf16)
            grad_q = out_state + mul(scores_low, k_low)
            grad_k = (
                carried_back
                - (b * since) * side_state
                + mul(scores_low, q_low, (0, 0))
                + mul(strict_low, k_low)
                + mul(strict_low, k_low, (0, 0))
            )
            grad_v = b * grad_side
            sums_grad = sums_grad + jnp.where(
                lane == 2 * head, grad_sums + jnp.where(place == CHUNK - 1, final, 0.0), 0.0
            )
            strength_grad = strength_grad + jnp.where(lane == 2 * head + 1, grad_strength, 0.0)
            grad_q = grad_q * key_width ** (-0.5)
            unit = t["unit_q"]
            grad_q = t["q_scale"] * (grad_q - unit * row_sum(grad_q * unit))
            grad_k = t["k_scale"] * (grad_k - k * row_sum(grad_k * k))
            at = head * channels
            for name, grad, size in (
                ("q", grad_q, key_width),
                ("k", grad_k, key_width),
                ("v", grad_v, value_width),
            ):
                pre, sig = t[name + "_slope"]
                mixed_scr[rows, at : at + size] = grad * (sig * (1.0 + pre * (1.0 - sig)))
                at += size
        step = 1
        while step < CHUNK:
            sums_grad = sums_grad + jnp.where(
                place < CHUNK - step, pltpu.roll(sums_grad, CHUNK - step, 0), 0.0
            )
            step *= 2
        rates = rates_ref[rows, :]
        log_decay, _ = decays(rates, log_rates_ref[...], bias_ref[...])
        strength = sigmoid(rates)
        inputs_grad = sums_grad * (-jnp.exp(log_rates_ref[...])) * sigmoid(rates + bias_ref[...])
        log_total = log_total + jnp.sum(sums_grad * log_decay, axis=0, keepdims=True)
        bias_total = bias_total + jnp.sum(inputs_grad, axis=0, keepdims=True)
        grad_rates_ref[rows, :] = (
            inputs_grad + strength_grad * strength * (1.0 - strength)
        ).astype(bf16)
    grad_lanes_ref[0:1, :] = log_total
    grad_lanes_ref[1:2, :] = bias_total

    mixed_scr[length : length + 8, :] = jnp.zeros((8, mixed_scr.shape[1]), f32)
    tap_totals = [jnp.zeros((1, heads * channels), f32) for _ in range(CONV)]
    for head in range(heads):
        columns = slice(head * channels, (head + 1) * channels)
        source = slice(head * width, head * width + channels)
        taps_here = [jnp.zeros((1, channels), f32) for _ in range(CONV)]
        for chunk in range(chunks):
            start = chunk * CHUNK
            total = None
            now = mixed_scr[start : start + CHUNK, columns]
            for tap in range(CONV):
                ahead = CONV - 1 - tap
                term = taps_ref[tap : tap + 1, columns] * (
                    mixed_scr[start + ahead : start + ahead + CHUNK, columns]
                )
                total = term if total is None else total + term
                taps_here[tap] = taps_here[tap] + jnp.sum(
                    now * shifted(project_ref, start, ahead, source), axis=0, keepdims=True
                )
            grad_project_ref[start : start + CHUNK, source] = total.astype(bf16)
        for tap in range(CONV):
            grad_taps_ref[tap : tap + 1, columns] = taps_here[tap]


def whole(count):
    return [pl.BlockSpec(memory_space=pltpu.VMEM)] * count


def run_forward(normed, mix, rates_w, taps, log_rates, bias, gain):
    length, value_width = normed.shape[0], gain.shape[1]
    columns = mix.shape[1]
    channels = taps.shape[1]
    heads = (columns - channels) // value_width
    key_width = (channels // heads - value_width) // 2
    chunks = length // CHUNK
    shape = jax.ShapeDtypeStruct
    values = heads * value_width
    pair = (chunks, heads)
    return pl.pallas_call(
        mixer_forward,
        out_shape=(
            shape((length, values), bf16),
            shape((length, columns), f32),
            shape((length, LANES), f32),
            shape((length, values), f32),
            shape(pair + (key_width, value_width), f32),
            shape((length, values), f32),
            shape(pair + (CHUNK, CHUNK), f32),
        ),
        in_specs=whole(7),
        out_specs=tuple(whole(7)),
        scratch_shapes=[
            pltpu.VMEM(pair + (CHUNK, key_width), bf16),
            pltpu.VMEM(pair + (CHUNK, key_width), bf16),
            pltpu.VMEM(pair + (CHUNK, CHUNK), bf16),
            pltpu.VMEM(pair + (CHUNK, key_width), bf16),
            pltpu.VMEM(pair + (CHUNK, value_width), f32),
        ],
        compiler_params=pltpu.CompilerParams(vmem_limit_bytes=52 * 2**20),
        name="mixer_forward",
    )(normed, mix, rates_w, taps, log_rates, bias, gain)


def run_backward(grad, w_out, taps, log_rates, bias, gain, kept):
    length, value_width = grad.shape[0], gain.shape[1]
    project = kept[0]
    columns = project.shape[1]
    channels = taps.shape[1]
    heads = (columns - channels) // value_width
    key_width = (channels // heads - value_width) // 2
    chunks = length // CHUNK
    shape = jax.ShapeDtypeStruct
    values = heads * value_width
    pair = (chunks, heads)
    return pl.pallas_call(
        mixer_backward,
        out_shape=(
            shape((length, columns), bf16),
            shape((length, LANES), bf16),
            shape((CONV, channels), f32),
            shape((1, value_width), f32),
            shape((2, LANES), f32),
        ),
        in_specs=whole(6 + len(kept)),
        out_specs=tuple(whole(5)),
        scratch_shapes=[
            pltpu.VMEM((length, values), f32),
            pltpu.VMEM(pair + (key_width, value_width), f32),
            pltpu.VMEM((length, values), f32),
            pltpu.VMEM(pair + (CHUNK, key_width), bf16),
            pltpu.VMEM(pair + (CHUNK, key_width), bf16),
            pltpu.VMEM(pair + (CHUNK, CHUNK), bf16),
            pltpu.VMEM(pair + (CHUNK, key_width), bf16),
            pltpu.VMEM((8, LANES), f32),
            pltpu.VMEM((length + 8, channels), f32),
        ],
        compiler_params=pltpu.CompilerParams(vmem_limit_bytes=52 * 2**20),
        name="mixer_backward",
    )(grad, w_out, taps, log_rates, bias, gain, *kept)


def swap(array, axis, size, offset):
    return lax.ppermute(array, axis, [(i, i ^ offset) for i in range(size)])


class Dp:
    def __init__(self, size):
        self.size = size
        self.near = size == 8
        self.half = size // 2
        self.offsets = [2 * p for p in range(self.half)] + [2 * p + 1 for p in range(self.half)]
        self.places = [self.offsets.index(k) for k in range(size)]

    def blocks_to_order(self, array):
        if not self.near:
            return array
        parts = array.reshape(array.shape[:-1] + (self.size, -1))
        index = lax.axis_index("dp") ^ jnp.array(self.offsets, jnp.int32)
        return jnp.take(parts, index, axis=-2).reshape(array.shape)

    def blocks_from_order(self, array):
        if not self.near:
            return array
        parts = array.reshape(array.shape[:-1] + (self.size, -1))
        index = jnp.array(self.places, jnp.int32)[lax.axis_index("dp") ^ jnp.arange(self.size, dtype=jnp.int32)]
        return jnp.take(parts, index, axis=-2).reshape(array.shape)

    def gather_start(self, shard):
        return [shard] + [swap(shard, "dp", self.size, 2 * p) for p in range(1, self.half)]

    def gather_end(self, evens):
        return evens + [swap(e, "dp", self.size, 1) for e in evens]

    def gather(self, shard):
        if not self.near:
            whole = lax.all_gather(shard, "dp", axis=0, tiled=False)
            return [whole[k] for k in range(self.size)]
        return self.gather_end(self.gather_start(shard))

    def scatter(self, evens, odds, axis):
        if not self.near:
            return lax.psum_scatter(
                jnp.concatenate([evens, odds.astype(evens.dtype)], axis),
                "dp",
                scatter_dimension=axis,
                tiled=True,
            )
        kind = odds.dtype
        summed = evens + swap(odds, "dp", self.size, 1).astype(f32)
        parts = jnp.split(summed, self.half, axis)
        total = parts[0]
        for p in range(1, self.half):
            total = total + swap(parts[p].astype(kind), "dp", self.size, 2 * p).astype(f32)
        return total


def gather_rows(rows, size):
    blocks = {0: rows}
    step = size // 2
    while step:
        for k in sorted(blocks):
            blocks[k ^ step] = swap(blocks[k], "tensor", size, step)
        step //= 2
    return [blocks[k] for k in range(size)]


def sum_rows(blocks, kind):
    size = len(blocks)
    blocks = dict(enumerate(blocks))
    step = 1
    while step < size:
        keep = {k: blocks[k] for k in blocks if not k & step}
        blocks = {
            k: keep[k] + swap(blocks[k ^ step].astype(kind), "tensor", size, step).astype(f32)
            for k in keep
        }
        step *= 2
    return blocks[0]


def in_time(blocks):
    length = blocks[0].shape[0]
    whole = jnp.zeros((len(blocks) * length,) + blocks[0].shape[1:], blocks[0].dtype)
    me = lax.axis_index("tensor")
    for k, block in enumerate(blocks):
        whole = lax.dynamic_update_slice_in_dim(whole, block, (me ^ k) * length, 0)
    return whole


def from_time(whole, size):
    length = whole.shape[0] // size
    me = lax.axis_index("tensor")
    return [lax.dynamic_slice_in_dim(whole, (me ^ k) * length, length, 0) for k in range(size)]


def after(arrays, others):
    kept, _ = lax.optimization_barrier((arrays, others))
    return kept


def per_device(
    layer_in,
    mixer_gain,
    w_mix,
    w_rates,
    conv_taps,
    a_log,
    dt_bias,
    head_gain,
    w_out,
    ffn_gain,
    w_gate_up,
    w_down,
    out_grad,
):
    dp = Dp(lax.axis_size("dp"))
    ranks = lax.axis_size("tensor")
    depth, heads_here, head_width = w_mix.shape
    hidden_here = w_gate_up.shape[2]
    channels = conv_taps.shape[2] * dp.size
    taps_shape = conv_taps.shape

    mix_shard = w_mix.reshape(depth, heads_here * head_width)
    gate_up_shard = w_gate_up.reshape(depth, 2 * hidden_here)
    small_shard = jnp.concatenate([w_rates.reshape(-1), conv_taps.reshape(-1)])
    small_size = w_rates.size
    small_slots = dp.gather(small_shard.reshape(8, -1))
    mix_slots = dp.gather(mix_shard)
    mix_full = jnp.concatenate(mix_slots, 0)
    small_flat = [s.reshape(-1) for s in small_slots]
    rates_full = jnp.concatenate([s[:small_size].reshape(depth, -1) for s in small_flat], 0)
    taps_order = jnp.concatenate([s[small_size:].reshape(taps_shape) for s in small_flat], 2)
    taps_full = dp.blocks_from_order(taps_order).astype(f32)

    resid_in = dp.blocks_to_order(layer_in).astype(f32)
    mixer_gain = dp.blocks_to_order(mixer_gain)
    ffn_gain = dp.blocks_to_order(ffn_gain)
    out_grad = dp.blocks_to_order(out_grad)

    normed, norm_back = jax.vjp(scale_norm, resid_in, mixer_gain)
    normed_all = in_time(gather_rows(normed.astype(bf16), ranks))
    out_shard, gate_up_shard, down_shard = after((w_out, gate_up_shard, w_down), mix_full)
    out_full = jnp.concatenate(dp.gather(out_shard), 1)
    gate_up_full = jnp.concatenate(dp.gather(gate_up_shard), 0)
    down_full = jnp.concatenate(dp.gather(down_shard), 1)

    first_head = lax.axis_index("tensor") * heads_here

    def on_lanes(per_head):
        here = lax.dynamic_slice_in_dim(per_head, first_head, heads_here)
        pairs = jnp.stack([here, jnp.zeros_like(here)], 1).reshape(1, -1)
        return jnp.pad(pairs, ((0, 0), (0, LANES - pairs.shape[1])))

    def off_lanes(row):
        here = row[: 2 * heads_here : 2]
        return lax.dynamic_update_slice_in_dim(jnp.zeros_like(a_log), here, first_head, 0)

    rates_wide = jnp.pad(rates_full, ((0, 0), (0, LANES - rates_full.shape[1])))
    small_args = (
        taps_full.reshape(CONV, -1),
        on_lanes(a_log),
        on_lanes(dt_bias),
        head_gain.reshape(1, -1),
    )
    gated_low, *kept = run_forward(normed_all, mix_full, rates_wide, *small_args)
    mixer_out = sum_rows(from_time(dot(gated_low, out_full), ranks), bf16)
    resid = resid_in + mixer_out
    ffn_in, ffn_back = jax.vjp(scale_norm, resid, ffn_gain)
    ffn_all = jnp.concatenate(gather_rows(ffn_in.astype(bf16), ranks), 0)
    top_grad = jnp.concatenate(gather_rows(out_grad, ranks), 0)
    gate_up = dot(ffn_all, gate_up_full).reshape(-1, 2, hidden_here)
    hidden, act_back = jax.vjp(gate_product, gate_up)
    hidden_low = hidden.astype(bf16)
    ffn_out = sum_rows(jnp.split(dot(hidden_low, down_full), ranks, 0), bf16)
    layer_out = dp.blocks_from_order((resid + ffn_out).astype(bf16))
    half = top_grad.shape[1] // 2
    grad_hidden = cols_dot(top_grad, down_full)
    (grad_gate_up,) = act_back(grad_hidden)
    grad_gate_low = grad_gate_up.astype(bf16).reshape(-1, 2 * hidden_here)
    grad_ffn_in = sum_rows(jnp.split(cols_dot(grad_gate_low, gate_up_full), ranks, 0), bf16)
    grad_resid_norm, grad_ffn_gain = ffn_back(grad_ffn_in)
    grad_resid = out_grad.astype(f32) + grad_resid_norm
    mix_grad = in_time(gather_rows(grad_resid.astype(bf16), ranks))
    grad_w_gate_up = dp.scatter(
        rows_dot(ffn_all[:, :half], grad_gate_low), rows_dot(ffn_all[:, half:], grad_gate_low, bf16), 0
    )
    grad_w_down = dp.scatter(
        rows_dot(hidden_low, top_grad[:, :half]), rows_dot(hidden_low, top_grad[:, half:], bf16), 1
    )
    grad_w_out = dp.scatter(
        rows_dot(gated_low, mix_grad[:, :half]), rows_dot(gated_low, mix_grad[:, half:], bf16), 1
    )
    project_low, rates_low, local_taps, grad_gain_here, grad_lanes = run_backward(
        mix_grad, out_full, *small_args, kept
    )
    rates_low = rates_low[:, : rates_full.shape[1]]
    local_taps = local_taps.reshape(CONV, heads_here, -1)
    grad_gain_here = grad_gain_here.reshape(-1)
    grad_log_rates, grad_decay_bias = off_lanes(grad_lanes[0]), off_lanes(grad_lanes[1])
    back_terms = cols_dot(project_low, mix_full) + cols_dot(rates_low, rates_full)
    grad_w_mix = dp.scatter(
        rows_dot(normed_all[:, :half], project_low), rows_dot(normed_all[:, half:], project_low, bf16), 0
    )
    grad_normed = sum_rows(from_time(back_terms, ranks), bf16)
    local_rates = rows_dot(normed_all, rates_low).reshape(dp.size, -1)
    local_taps = dp.blocks_to_order(local_taps).reshape(taps_shape[:2] + (dp.size, -1))
    local_taps = jnp.moveaxis(local_taps, 2, 0).reshape(dp.size, -1)
    local_small = jnp.concatenate([local_rates, local_taps], 1)
    summed_small = dp.scatter(local_small[: dp.half], local_small[dp.half :], 0).reshape(-1)
    grad_w_rates = summed_small[:small_size].reshape(w_rates.shape)
    grad_conv_taps = summed_small[small_size:].reshape(taps_shape)
    grad_input_norm, grad_gain_first = norm_back(grad_normed)
    in_grad = dp.blocks_from_order(grad_resid + grad_input_norm)
    grad_mixer_gain, grad_ffn_total, grad_head_gain, grad_a_log, grad_dt_bias = lax.psum(
        (
            dp.blocks_from_order(grad_gain_first),
            dp.blocks_from_order(grad_ffn_gain),
            grad_gain_here,
            grad_log_rates,
            grad_decay_bias,
        ),
        ("dp", "tensor"),
    )
    return (
        layer_out,
        in_grad,
        grad_mixer_gain,
        grad_w_mix.reshape(w_mix.shape),
        grad_w_rates,
        grad_conv_taps,
        grad_a_log,
        grad_dt_bias,
        grad_head_gain,
        grad_w_out,
        grad_ffn_total,
        grad_w_gate_up.reshape(w_gate_up.shape),
        grad_w_down,
    )


def solution(mesh):
    return jax.shard_map(
        per_device,
        mesh=mesh,
        in_specs=(
            P(("dp", "tensor"), None),
            P(),
            P("dp", "tensor", None),
            P("dp", "tensor", None),
            P(None, "tensor", "dp"),
            P(),
            P(),
            P(),
            P("tensor", "dp"),
            P(),
            P("dp", None, "tensor"),
            P("tensor", "dp"),
            P(("dp", "tensor"), None),
        ),
        out_specs=(
            P(("dp", "tensor"), None),
            P(("dp", "tensor"), None),
            P(),
            P("dp", "tensor", None),
            P("dp", "tensor", None),
            P(None, "tensor", "dp"),
            P(),
            P(),
            P(),
            P("tensor", "dp"),
            P(),
            P("dp", None, "tensor"),
            P("tensor", "dp"),
        ),
        check_vma=False,
    )
```

```python
import jax
import jax.numpy as jnp
from jax import lax
from jax.experimental import pallas as pl
from jax.experimental.pallas import tpu as pltpu
from jax.sharding import PartitionSpec as P

CONV = 4


highest = lax.Precision.HIGHEST
NORM_EPS = 1e-05
UNIT_EPS = 1e-06
bf16 = jnp.bfloat16
f32 = jnp.float32


def rows_dot(left, right, kind=f32):
    return lax.dot_general(
        left, right, (((0,), (0,)), ((), ())), preferred_element_type=f32
    ).astype(kind)


def cols_dot(left, right):
    return lax.dot_general(left, right, (((1,), (1,)), ((), ())), preferred_element_type=f32)


def dot(left, right):
    return jnp.dot(left, right, preferred_element_type=f32)


CHUNK = 128
LANES = 128


def mul(left, right, over=(1, 0), exact=False):
    dims = (((over[0],), (over[1],)), ((), ()))
    if exact:
        return lax.dot_general(left, right, dims, precision=highest, preferred_element_type=f32)
    return lax.dot_general(left.astype(bf16), right.astype(bf16), dims, preferred_element_type=f32)


def square_ids():
    shape = (CHUNK, CHUNK)
    return lax.broadcasted_iota(jnp.int32, shape, 0), lax.broadcasted_iota(jnp.int32, shape, 1)


def sigmoid(v):
    return 1.0 / (1.0 + jnp.exp(-v))


def softplus(v):
    return jnp.maximum(v, 0.0) + jnp.log1p(jnp.exp(-jnp.abs(v)))


def row_sum(v):
    return jnp.sum(v, axis=1, keepdims=True)


def unit_inverse(lower):
    rows, cols = square_ids()
    inverse = jnp.where(rows == cols, 1.0, 0.0)
    block = 1
    while block < CHUNK:
        corner = (
            (rows // (2 * block) == cols // (2 * block))
            & ((rows // block) % 2 == 1)
            & ((cols // block) % 2 == 0)
        )
        part = jnp.where(corner, lower, 0.0)
        if block == 1:
            inverse = inverse - part
        else:
            inverse = inverse - mul(mul(inverse, part), inverse)
        block *= 2
    return inverse


def shifted(ref, start, back, columns):
    if start == 0 and back:
        rows = lax.broadcasted_iota(jnp.int32, (CHUNK, columns.stop - columns.start), 0)
        return jnp.where(rows >= back, pltpu.roll(ref[0:CHUNK, columns], back, 0), 0.0)
    return ref[start - back : start - back + CHUNK, columns]


def short_conv(project_ref, taps_ref, start, head, heads, columns, tap_columns):
    total = None
    for tap in range(CONV):
        row = tap * heads + head
        term = taps_ref[row : row + 1, tap_columns] * shifted(
            project_ref, start, CONV - 1 - tap, columns
        )
        total = term if total is None else total + term
    return total


def decays(rates, log_rates, bias):
    log_decay = -jnp.exp(log_rates) * softplus(rates + bias)
    place = lax.broadcasted_iota(jnp.int32, rates.shape, 0)
    total = log_decay
    step = 1
    while step < CHUNK:
        total = total + jnp.where(place >= step, pltpu.roll(total, step, 0), 0.0)
        step *= 2
    return log_decay, total


def chunk_terms(head, project_ref, taps_ref, start, total, total_rows, strength, key_width, value_width):
    width = 2 * key_width + 2 * value_width
    base = head * width
    heads = project_ref.shape[1] // width
    terms = {}
    parts = (("q", 0, key_width), ("k", key_width, key_width), ("v", 2 * key_width, value_width))
    for name, at, size in parts:
        pre = short_conv(
            project_ref,
            taps_ref,
            start,
            head,
            heads,
            slice(base + at, base + at + size),
            slice(at, at + size),
        )
        gate = sigmoid(pre)
        mixed = pre * gate
        if name != "v":
            scale = lax.rsqrt(row_sum(mixed * mixed) + UNIT_EPS)
            mixed = mixed * scale
            terms[name + "_scale"] = scale
        terms[name + "_slope"] = (pre, gate)
        terms[name] = mixed
    terms["unit_q"] = terms["q"]
    terms["q"] = terms["q"] * key_width ** (-0.5)
    lane = 2 * head
    sums = total[:, lane : lane + 1]
    across = total_rows[lane : lane + 1, :]
    rows, cols = square_ids()
    decay = jnp.where(rows >= cols, jnp.exp(jnp.minimum(sums - across, 0.0)), 0.0)
    final = total[CHUNK - 1 : CHUNK, lane : lane + 1]
    terms["b"] = strength[:, lane + 1 : lane + 2]
    terms["since"] = jnp.exp(sums)
    terms["remaining"] = jnp.exp(final - sums)
    terms["through"] = jnp.exp(final)
    terms["decay"] = decay
    terms["dots"] = mul(terms["k"], terms["k"], (1, 1)) * jnp.where(rows > cols, decay, 0.0)
    terms["scores"] = mul(terms["q"], terms["k"], (1, 1)) * decay
    return terms


def stack_rows(refs, target, column):
    at = 0
    for ref in refs:
        rows = ref.shape[0]
        columns = min(ref.shape[1], target.shape[1] - column)
        target[at : at + rows, column : column + columns] = ref[:, :columns]
        at += rows


def rows_in_time(ids_ref, refs, target):
    size = target.shape[0] // len(refs)
    for k, ref in enumerate(refs):
        at = pl.multiple_of((ids_ref[0] ^ k) * size, size)
        target[pl.ds(at, size), :] = ref[0:size, :]


def order_of(ids_ref, place):
    return ids_ref[1 + place]


def taps_from_blocks(ids_ref, mix_ref, shape):
    rows, channels = shape
    count = mix_ref.shape[0] // LANES
    part = channels // count
    lane = lax.broadcasted_iota(jnp.int32, shape, 1)
    total = jnp.zeros(shape, f32)
    for place in range(count):
        block = mix_ref[place * LANES : place * LANES + 16, mix_ref.shape[1] - LANES :]
        block = block.astype(f32)[0:rows, LANES - part :]
        wide = jnp.concatenate([block] * count, 1)
        total = total + jnp.where(lane // part == order_of(ids_ref, place), wide, 0.0)
    return total


def taps_to_blocks(ids_ref, taps_ref, target, first):
    rows, channels = taps_ref.shape
    count = target.shape[0] // LANES
    part = channels // (2 * count)
    for place in range(count):
        owner = order_of(ids_ref, first + place)
        block = jnp.zeros((rows, part), f32)
        for other in range(2 * count):
            block = block + jnp.where(
                owner == other, taps_ref[:, other * part : (other + 1) * part], 0.0
            )
        block = jnp.concatenate([jnp.zeros((rows, LANES - part), f32), block], 1)
        block = jnp.concatenate([block, jnp.zeros((16 - rows, LANES), f32)], 0)
        at = (slice(place * LANES, place * LANES + 16), slice(target.shape[1] - LANES, target.shape[1]))
        target[at] = (target[at].astype(f32) + block).astype(target.dtype)


def rows_to_blocks(ids_ref, value, send_ref, keep_ref):
    size = value.shape[0] // 4
    for k in range(4):
        target = send_ref if k % 2 else keep_ref
        half = (k // 2) * size
        for block in range(4):

            @pl.when((ids_ref[0] ^ k) == block)
            def _(block=block, half=half, target=target):
                target[half : half + size, :] = value[block * size : (block + 1) * size, :].astype(
                    target.dtype
                )


def mixer_forward(near, refs):
    (ids_ref, taps_in_ref, log_rates_ref, bias_ref, gain_ref), row_refs, mix_refs, outs, scratch = refs
    gated_ref, project_ref, rates_ref, out_ref, states_ref, carried_ref, inverse_ref = outs[:7]
    normed_ref, mix_ref, taps_ref = outs[7:]
    q_scr, kr_scr, p_scr, w_scr, u_scr = scratch
    length = normed_ref.shape[0]
    value_width = gain_ref.shape[1]
    heads = out_ref.shape[1] // value_width
    width = project_ref.shape[1] // heads
    key_width = (width - 2 * value_width) // 2
    chunks = length // CHUNK
    rows_in_time(ids_ref, row_refs, normed_ref)
    stack_rows(mix_refs, mix_ref, 0)
    if near:
        taps_ref[...] = taps_from_blocks(ids_ref, mix_ref, taps_in_ref.shape)
    else:
        taps_ref[...] = taps_in_ref[...]
    for head in range(heads):
        columns = slice(head * width, (head + 1) * width)
        project_ref[:, columns] = dot(normed_ref[...], mix_ref[:, columns])
    rates_ref[...] = dot(normed_ref[...], mix_ref[:, heads * width :])
    through = {}
    for chunk in range(chunks):
        start = chunk * CHUNK
        rows = slice(start, start + CHUNK)
        rates = rates_ref[rows, :]
        _, total = decays(rates, log_rates_ref[...], bias_ref[...])
        strength = sigmoid(rates)
        total_rows = jnp.transpose(total)
        for head in range(heads):
            t = chunk_terms(
                head, project_ref, taps_ref, start, total, total_rows, strength, key_width, value_width
            )
            inverse = unit_inverse(t["b"] * t["dots"])
            inverse_ref[chunk, head] = inverse
            side = jnp.concatenate([(t["b"] * t["since"]) * t["k"], t["b"] * t["v"]], 1)
            solved = mul(inverse, side)
            w_scr[chunk, head] = solved[:, :key_width].astype(bf16)
            u_scr[chunk, head] = solved[:, key_width:]
            q_scr[chunk, head] = (t["q"] * t["since"]).astype(bf16)
            kr_scr[chunk, head] = t["k"] * t["remaining"]
            p_scr[chunk, head] = t["scores"].astype(bf16)
            through[chunk, head] = t["through"]
    state = [jnp.zeros((key_width, value_width), f32) for _ in range(heads)]
    for chunk in range(chunks):
        rows = slice(chunk * CHUNK, (chunk + 1) * CHUNK)
        for head in range(heads):
            columns = slice(head * value_width, (head + 1) * value_width)
            states_ref[chunk, head] = state[head]
            low = state[head].astype(bf16)
            carried = u_scr[chunk, head] - mul(w_scr[chunk, head], low)
            carried_ref[rows, columns] = carried
            out_ref[rows, columns] = mul(q_scr[chunk, head], low) + mul(p_scr[chunk, head], carried)
            state[head] = through[chunk, head] * state[head] + mul(
                kr_scr[chunk, head], carried, (0, 0), exact=True
            )
    for chunk in range(chunks):
        rows = slice(chunk * CHUNK, (chunk + 1) * CHUNK)
        for head in range(heads):
            columns = slice(head * value_width, (head + 1) * value_width)
            out = out_ref[rows, columns]
            gate = project_ref[rows, (head + 1) * width - value_width : (head + 1) * width]
            scale = lax.rsqrt(row_sum(out * out) / value_width + NORM_EPS)
            gated_ref[rows, columns] = (
                out * scale * gain_ref[...] * (gate * sigmoid(gate))
            ).astype(bf16)


def mixer_backward(near, refs):
    fixed, row_refs, w_out_refs, kept, outs, scratch = refs
    ids_ref, log_rates_ref, bias_ref, gain_ref = fixed
    (
        project_ref,
        rates_ref,
        out_ref,
        states_ref,
        carried_ref,
        inverse_ref,
        normed_ref,
        _,
        taps_ref,
    ) = kept
    grads_ref, grad_taps_ref, grad_gain_ref, grad_lanes_ref, send_a_ref, send_b_ref, grad_ref = outs
    (
        grad_out_scr,
        back_scr,
        grad_carried_scr,
        q_scr,
        kr_scr,
        p_scr,
        w_scr,
        w_out_scr,
        mixed_scr,
    ) = scratch
    grad_project_ref = grads_ref
    length = grad_ref.shape[0]
    value_width = gain_ref.shape[1]
    heads = out_ref.shape[1] // value_width
    width = project_ref.shape[1] // heads
    key_width = (width - 2 * value_width) // 2
    channels = 2 * key_width + value_width
    chunks = length // CHUNK
    rows_in_time(ids_ref, row_refs, grad_ref)
    stack_rows(w_out_refs, w_out_scr, 0)
    grad_out_scr[...] = dot(grad_ref[...], w_out_scr[...])
    gain = gain_ref[...]
    gain_total = jnp.zeros((1, value_width), f32)
    terms = {}

    def gather_terms(chunk):
        start = chunk * CHUNK
        rates = rates_ref[start : start + CHUNK, :]
        _, total = decays(rates, log_rates_ref[...], bias_ref[...])
        strength = sigmoid(rates)
        total_rows = jnp.transpose(total)
        return [
            chunk_terms(
                head, project_ref, taps_ref, start, total, total_rows, strength, key_width, value_width
            )
            for head in range(heads)
        ]

    through = {}
    for chunk in range(chunks):
        rows = slice(chunk * CHUNK, (chunk + 1) * CHUNK)
        terms = gather_terms(chunk)
        for head in range(heads):
            columns = slice(head * value_width, (head + 1) * value_width)
            gate_columns = slice((head + 1) * width - value_width, (head + 1) * width)
            t = terms[head]
            out = out_ref[rows, columns]
            gate = project_ref[rows, gate_columns]
            grad = grad_out_scr[rows, columns]
            scale = lax.rsqrt(row_sum(out * out) / value_width + NORM_EPS)
            unit = out * scale
            sig = sigmoid(gate)
            act = gate * sig
            gain_total = gain_total + jnp.sum(grad * unit * act, axis=0, keepdims=True)
            grad_project_ref[rows, gate_columns] = (
                grad * gain * unit * (sig * (1.0 + gate * (1.0 - sig)))
            ).astype(bf16)
            inner = grad * act * gain
            grad_out_scr[rows, columns] = scale * (
                inner - unit * (row_sum(inner * unit) / value_width)
            )
            w_scr[chunk, head] = mul(
                inverse_ref[chunk, head], (t["b"] * t["since"]) * t["k"]
            ).astype(bf16)
            q_scr[chunk, head] = (t["q"] * t["since"]).astype(bf16)
            kr_scr[chunk, head] = (t["k"] * t["remaining"]).astype(bf16)
            p_scr[chunk, head] = t["scores"].astype(bf16)
            through[chunk, head] = t["through"]
    grad_gain_ref[...] = gain_total

    back = [jnp.zeros((key_width, value_width), f32) for _ in range(heads)]
    for chunk in reversed(range(chunks)):
        rows = slice(chunk * CHUNK, (chunk + 1) * CHUNK)
        for head in range(heads):
            columns = slice(head * value_width, (head + 1) * value_width)
            back_scr[chunk, head] = back[head]
            grad_out = grad_out_scr[rows, columns].astype(bf16)
            grad_carried = mul(p_scr[chunk, head], grad_out, (0, 0)) + mul(
                kr_scr[chunk, head], back[head]
            )
            grad_carried_scr[rows, columns] = grad_carried
            back[head] = (
                through[chunk, head] * back[head]
                + mul(q_scr[chunk, head], grad_out, (0, 0))
                - mul(w_scr[chunk, head], grad_carried, (0, 0))
            )

    rows_at, cols_at = square_ids()
    lane = lax.broadcasted_iota(jnp.int32, (CHUNK, LANES), 1)
    place = lax.broadcasted_iota(jnp.int32, (CHUNK, LANES), 0)
    log_total = jnp.zeros((1, LANES), f32)
    bias_total = jnp.zeros((1, LANES), f32)
    for chunk in range(chunks):
        rows = slice(chunk * CHUNK, (chunk + 1) * CHUNK)
        terms = gather_terms(chunk)
        sums_grad = jnp.zeros((CHUNK, LANES), f32)
        strength_grad = jnp.zeros((CHUNK, LANES), f32)
        for head in range(heads):
            columns = slice(head * value_width, (head + 1) * value_width)
            t = terms[head]
            b, since, remaining, decay = t["b"], t["since"], t["remaining"], t["decay"]
            q, k, v = t["q"], t["k"], t["v"]
            state = states_ref[chunk, head]
            back_now = back_scr[chunk, head]
            carried = carried_ref[rows, columns]
            grad_out = grad_out_scr[rows, columns]
            grad_side = mul(inverse_ref[chunk, head], grad_carried_scr[rows, columns], (0, 0))
            strict = jnp.where(rows_at > cols_at, -mul(grad_side, carried, (1, 1)), 0.0)
            grad_scores = mul(grad_out, carried, (1, 1))
            side_state = mul(grad_side, state, (1, 1))
            out_state = since * mul(grad_out, state, (1, 1))
            carried_back = remaining * mul(carried, back_now, (1, 1))
            key_side = since * row_sum(k * side_state)
            strict_dots = strict * t["dots"]
            grad_strength = row_sum(grad_side * v) - key_side + row_sum(strict_dots)
            pulls = grad_scores * t["scores"] + b * strict_dots
            key_back = row_sum(k * carried_back)
            grad_sums = (
                row_sum(pulls - jnp.transpose(pulls))
                - b * key_side
                + row_sum(q * out_state)
                - key_back
            )
            final = jnp.sum(key_back, axis=0, keepdims=True) + t["through"] * jnp.sum(
                row_sum(back_now * state), axis=0, keepdims=True
            )
            scores_low = (grad_scores * decay).astype(bf16)
            strict_low = (strict * (b * decay)).astype(bf16)
            k_low, q_low = k.astype(bf16), q.astype(bf16)
            grad_q = out_state + mul(scores_low, k_low)
            grad_k = (
                carried_back
                - (b * since) * side_state
                + mul(scores_low, q_low, (0, 0))
                + mul(strict_low, k_low)
                + mul(strict_low, k_low, (0, 0))
            )
            grad_v = b * grad_side
            sums_grad = sums_grad + jnp.where(
                lane == 2 * head, grad_sums + jnp.where(place == CHUNK - 1, final, 0.0), 0.0
            )
            strength_grad = strength_grad + jnp.where(lane == 2 * head + 1, grad_strength, 0.0)
            grad_q = grad_q * key_width ** (-0.5)
            unit = t["unit_q"]
            grad_q = t["q_scale"] * (grad_q - unit * row_sum(grad_q * unit))
            grad_k = t["k_scale"] * (grad_k - k * row_sum(grad_k * k))
            at = head * channels
            for name, grad, size in (
                ("q", grad_q, key_width),
                ("k", grad_k, key_width),
                ("v", grad_v, value_width),
            ):
                pre, sig = t[name + "_slope"]
                mixed_scr[rows, at : at + size] = grad * (sig * (1.0 + pre * (1.0 - sig)))
                at += size
        step = 1
        while step < CHUNK:
            sums_grad = sums_grad + jnp.where(
                place < CHUNK - step, pltpu.roll(sums_grad, CHUNK - step, 0), 0.0
            )
            step *= 2
        rates = rates_ref[rows, :]
        log_decay, _ = decays(rates, log_rates_ref[...], bias_ref[...])
        strength = sigmoid(rates)
        inputs_grad = sums_grad * (-jnp.exp(log_rates_ref[...])) * sigmoid(rates + bias_ref[...])
        log_total = log_total + jnp.sum(sums_grad * log_decay, axis=0, keepdims=True)
        bias_total = bias_total + jnp.sum(inputs_grad, axis=0, keepdims=True)
        grads_ref[rows, heads * width :] = (
            inputs_grad + strength_grad * strength * (1.0 - strength)
        ).astype(bf16)
    grad_lanes_ref[0:1, :] = log_total
    grad_lanes_ref[1:2, :] = bias_total

    mixed_scr[length : length + 8, :] = jnp.zeros((8, mixed_scr.shape[1]), f32)
    for head in range(heads):
        columns = slice(head * channels, (head + 1) * channels)
        source = slice(head * width, head * width + channels)
        taps_here = [jnp.zeros((1, channels), f32) for _ in range(CONV)]
        for chunk in range(chunks):
            start = chunk * CHUNK
            total = None
            now = mixed_scr[start : start + CHUNK, columns]
            for tap in range(CONV):
                ahead = CONV - 1 - tap
                row = tap * heads + head
                term = taps_ref[row : row + 1, :] * (
                    mixed_scr[start + ahead : start + ahead + CHUNK, columns]
                )
                total = term if total is None else total + term
                taps_here[tap] = taps_here[tap] + jnp.sum(
                    now * shifted(project_ref, start, ahead, source), axis=0, keepdims=True
                )
            grads_ref[start : start + CHUNK, source] = total.astype(bf16)
        for tap in range(CONV):
            row = tap * heads + head
            grad_taps_ref[row : row + 1, :] = taps_here[tap]
    half = normed_ref.shape[1] // 2
    cut = send_a_ref.shape[1]
    send_a_ref[...] = rows_dot(normed_ref[:, half:], grads_ref[:, :cut], bf16)
    send_b_ref[...] = rows_dot(normed_ref[:, half:], grads_ref[:, cut:], bf16)
    if near:
        taps_to_blocks(ids_ref, grad_taps_ref, send_b_ref, half // LANES)


def mixer_products(near, refs):
    ids_ref, normed_ref, grads_ref, mix_ref, grad_taps_ref, keep_a_ref, keep_b_ref, back_send_ref, back_keep_ref = refs
    back = cols_dot(grads_ref[...], mix_ref[...])
    rows_to_blocks(ids_ref, back, back_send_ref, back_keep_ref)
    half = normed_ref.shape[1] // 2
    cut = keep_a_ref.shape[1]
    keep_a_ref[...] = rows_dot(normed_ref[:, :half], grads_ref[:, :cut])
    keep_b_ref[...] = rows_dot(normed_ref[:, :half], grads_ref[:, cut:])
    if near:
        taps_to_blocks(ids_ref, grad_taps_ref, keep_b_ref, 0)


def norm_scale(rows):
    return lax.rsqrt(jnp.mean(rows * rows, axis=1, keepdims=True) + NORM_EPS)


def prepare(ids_ref, rows_ref, grad_ref, mixer_gain_ref, ffn_gain_ref, resid_ref, both_ref, gains_ref):
    size = rows_ref.shape[0]
    count = rows_ref.shape[1] // LANES
    for place in range(count):
        at = pl.multiple_of(order_of(ids_ref, place) * LANES, LANES)
        here = slice(place * LANES, (place + 1) * LANES)
        resid_ref[:, here] = rows_ref[:, pl.ds(at, LANES)].astype(f32)
        both_ref[size:, here] = grad_ref[:, pl.ds(at, LANES)]
        gains_ref[0:1, here] = mixer_gain_ref[:, pl.ds(at, LANES)]
        gains_ref[1:2, here] = ffn_gain_ref[:, pl.ds(at, LANES)]
    resid = resid_ref[...]
    both_ref[0:size, :] = (resid * norm_scale(resid) * gains_ref[0:1, :]).astype(bf16)


def out_product(ids_ref, gated_ref, *refs):
    w_out_refs, (send_ref, keep_ref, w_out_scr) = refs[:-3], refs[-3:]
    stack_rows(w_out_refs, w_out_scr, 0)
    rows_to_blocks(ids_ref, cols_dot(gated_ref[...], w_out_scr[...]), send_ref, keep_ref)


def fold(keep_ref, got_ref, keep_out_ref, send_ref):
    size = send_ref.shape[0]
    keep_out_ref[...] = keep_ref[0:size, :] + got_ref[0:size, :].astype(f32)
    send_ref[...] = (keep_ref[size:, :] + got_ref[size:, :].astype(f32)).astype(bf16)


def middle_norm(keep_ref, got_ref, resid_in_ref, gains_ref, resid_ref, ffn_in_ref):
    resid = resid_in_ref[...] + keep_ref[...] + got_ref[...].astype(f32)
    resid_ref[...] = resid
    ffn_in_ref[...] = (resid * norm_scale(resid) * gains_ref[1:2, :]).astype(bf16)


def feed_forward(groups, refs):
    ffn_refs, grad_refs, weight_refs, outs, weights_scr = refs
    ffn_ref, top_ref, hidden_ref, grad_gate_ref, out_send, out_keep, back_send, back_keep = outs
    size = ffn_refs[0].shape[0]
    column = 0
    for group in weight_refs:
        stack_rows(group, weights_scr, column)
        column += group[0].shape[1]
    for k in range(4):
        ffn_ref[k * size : (k + 1) * size, :] = ffn_refs[k][...]
        top_ref[k * size : (k + 1) * size, :] = grad_refs[k][size:, :]
    hidden_size = hidden_ref.shape[1]
    first, second = groups
    gate_up_w = weights_scr[:, first:second]
    down_w = weights_scr[:, second : second + hidden_size]
    gate_up = dot(ffn_ref[...], gate_up_w)
    grad_hidden = dot(top_ref[...], down_w)
    gate, up = gate_up[:, :hidden_size], gate_up[:, hidden_size:]
    sig = sigmoid(gate)
    act = gate * sig
    hidden_ref[...] = (act * up).astype(bf16)
    grad_gate_ref[:, :hidden_size] = (grad_hidden * up * (sig * (1.0 + gate * (1.0 - sig)))).astype(bf16)
    grad_gate_ref[:, hidden_size:] = (grad_hidden * act).astype(bf16)
    back = cols_dot(grad_gate_ref[...], gate_up_w)
    out = cols_dot(hidden_ref[...], down_w)
    for value, send, keep in ((back, back_send, back_keep), (out, out_send, out_keep)):
        for k in range(4):
            target = send if k % 2 else keep
            half = (k // 2) * size
            target[half : half + size, :] = value[k * size : (k + 1) * size, :].astype(target.dtype)


def norm_reverse(grad, rows, gain):
    scale = norm_scale(rows)
    unit = rows * scale
    inner = grad * gain
    gain_grad = jnp.sum(grad * unit, axis=0, keepdims=True)
    return scale * (inner - unit * jnp.mean(inner * unit, axis=1, keepdims=True)), gain_grad


def middle_back(
    back_keep_ref, back_got_ref, resid_ref, both_ref, gains_ref, grad_ref, low_ref, gain_grad_ref
):
    grad_ffn_in = back_keep_ref[...] + back_got_ref[...].astype(f32)
    grad, gain_grad = norm_reverse(grad_ffn_in, resid_ref[...], gains_ref[1:2, :])
    grad = grad + both_ref[both_ref.shape[0] // 2 :, :].astype(f32)
    grad_ref[...] = grad
    low_ref[...] = grad.astype(bf16)
    gain_grad_ref[...] = gain_grad


def place_of(ids_ref, block, count):
    return ids_ref[1 + count + block]


def last_out(ids_ref, keep_ref, got_ref, resid_ref, out_ref, scr):
    scr[...] = resid_ref[...] + keep_ref[...] + got_ref[...].astype(f32)
    count = out_ref.shape[1] // LANES
    for block in range(count):
        at = pl.multiple_of(place_of(ids_ref, block, count) * LANES, LANES)
        out_ref[:, block * LANES : (block + 1) * LANES] = scr[:, pl.ds(at, LANES)].astype(bf16)


def last_grad(
    ids_ref, keep_ref, got_ref, resid_in_ref, gains_ref, grad_ref, gain_grad_ref, out_ref, gains_out_ref, scr, gain_scr
):
    grad_normed = keep_ref[...] + got_ref[...].astype(f32)
    grad, gain_grad = norm_reverse(grad_normed, resid_in_ref[...], gains_ref[0:1, :])
    scr[...] = grad + grad_ref[...]
    gain_scr[0:1, :] = gain_grad
    gain_scr[1:2, :] = gain_grad_ref[...]
    count = out_ref.shape[1] // LANES
    for block in range(count):
        at = pl.multiple_of(place_of(ids_ref, block, count) * LANES, LANES)
        here = slice(block * LANES, (block + 1) * LANES)
        out_ref[:, here] = scr[:, pl.ds(at, LANES)]
        gains_out_ref[:, here] = gain_scr[:, pl.ds(at, LANES)]


def call(kernel, outs, operands, scratch=(), name=None, scalar=True):
    specs = [pl.BlockSpec(memory_space=pltpu.VMEM)] * len(operands)
    if scalar:
        specs[0] = pl.BlockSpec(memory_space=pltpu.SMEM)
    return pl.pallas_call(
        kernel,
        out_shape=tuple(jax.ShapeDtypeStruct(shape, kind) for shape, kind in outs),
        in_specs=specs,
        out_specs=tuple([pl.BlockSpec(memory_space=pltpu.VMEM)] * len(outs)),
        scratch_shapes=[pltpu.VMEM(shape, kind) for shape, kind in scratch],
        compiler_params=pltpu.CompilerParams(vmem_limit_bytes=56 * 2**20),
        name=name,
    )(*operands)


def cut_list(items, sizes):
    parts, at = [], 0
    for size in sizes:
        parts.append(items[at : at + size])
        at += size
    return parts


def run_forward(near, ids, rows, mix, taps, log_rates, bias, gain):
    length = rows[0].shape[0] // 2 * len(rows)
    model, value_width = rows[0].shape[1], gain.shape[1]
    wide = mix[0].shape[1]
    columns = wide - LANES
    channels = taps.shape[1]
    heads = taps.shape[0] // CONV
    key_width = (channels - value_width) // 2
    pair = (length // CHUNK, heads)
    values = heads * value_width

    def kernel(*refs):
        mixer_forward(near, cut_list(refs, (5, len(rows), len(mix), 10, 5)))

    return call(
        kernel,
        (
            ((length, values), bf16),
            ((length, columns), f32),
            ((length, LANES), f32),
            ((length, values), f32),
            (pair + (key_width, value_width), f32),
            ((length, values), f32),
            (pair + (CHUNK, CHUNK), f32),
            ((length, model), bf16),
            ((model, wide), bf16),
            (taps.shape, f32),
        ),
        (ids, taps, log_rates, bias, gain, *rows, *mix),
        (
            (pair + (CHUNK, key_width), bf16),
            (pair + (CHUNK, key_width), f32),
            (pair + (CHUNK, CHUNK), bf16),
            (pair + (CHUNK, key_width), bf16),
            (pair + (CHUNK, value_width), f32),
        ),
        "mixer_forward",
    )


def run_backward(near, ids, rows, w_out, log_rates, bias, gain, kept):
    project, _, out, states, _, _, normed, mix, taps = kept
    length, model = normed.shape
    values, value_width = out.shape[1], gain.shape[1]
    wide = mix.shape[1]
    key_width, heads = states.shape[2], states.shape[1]
    pair = (length // CHUNK, heads)
    cut = wide // 2 // LANES * LANES + LANES

    def kernel(*refs):
        mixer_backward(near, cut_list(refs, (4, len(rows), len(w_out), len(kept), 7, 9)))

    return call(
        kernel,
        (
            ((length, wide), bf16),
            (taps.shape, f32),
            ((1, value_width), f32),
            ((2, LANES), f32),
            ((model // 2, cut), bf16),
            ((model // 2, wide - cut), bf16),
            ((length, model), bf16),
        ),
        (ids, log_rates, bias, gain, *rows, *w_out, *kept),
        (
            ((length, values), f32),
            (pair + (key_width, value_width), f32),
            ((length, values), f32),
            (pair + (CHUNK, key_width), bf16),
            (pair + (CHUNK, key_width), bf16),
            (pair + (CHUNK, CHUNK), bf16),
            (pair + (CHUNK, key_width), bf16),
            ((model, values), bf16),
            ((length + 8, heads * taps.shape[1]), f32),
        ),
        "mixer_backward",
    )


def swap(array, axis, size, offset):
    return lax.ppermute(array, axis, [(i, i ^ offset) for i in range(size)])


def after(arrays, others):
    kept, _ = lax.optimization_barrier((arrays, others))
    return kept


def per_device(
    layer_in,
    mixer_gain,
    w_mix,
    w_rates,
    conv_taps,
    a_log,
    dt_bias,
    head_gain,
    w_out,
    ffn_gain,
    w_gate_up,
    w_down,
    out_grad,
):
    size = lax.axis_size("dp")
    ranks = lax.axis_size("tensor")
    depth, heads, width = w_mix.shape
    model = layer_in.shape[1]
    hidden = w_gate_up.shape[2]
    value_size = w_out.shape[0]
    rows = layer_in.shape[0]
    taps_shape = conv_taps.shape
    part = taps_shape[2]
    near = size == 8 and depth == LANES and 2 * part == LANES
    half = size // 2
    rank, own = lax.axis_index("tensor"), lax.axis_index("dp")
    blocks = model // LANES
    if near:
        offsets = [2 * p for p in range(half)] + [2 * p + 1 for p in range(half)]
        order = own ^ jnp.array(offsets, jnp.int32)
        places = [offsets.index(k) for k in range(size)]
        index = own ^ jnp.arange(size, dtype=jnp.int32)
        place = jnp.where(index % 2 == 0, index // 2, half + index // 2)
        assert places == [k // 2 if k % 2 == 0 else half + k // 2 for k in range(size)]
    else:
        order = place = jnp.arange(blocks, dtype=jnp.int32)
    ids = jnp.concatenate([jnp.full((1,), rank, jnp.int32), order, place])

    def near_z(shard):
        return [shard] + [swap(shard, "dp", size, 2 * p) for p in range(1, half)]

    def near_x(shards):
        return [swap(shard, "dp", size, 1) for shard in shards]

    def far(shard):
        return lax.all_gather(shard, "dp", axis=0, tiled=True)

    def rows_y(block):
        return swap(block, "tensor", ranks, 2)

    def rows_core(block):
        return swap(block, "tensor", ranks, 1)

    def gather_rows(block):
        across = rows_y(block)
        return [block, rows_core(block), across, rows_core(across)]

    def sum_rows(send, keep, name):
        got = rows_core(send)
        shape = (rows, model)
        keep, send = call(fold, ((shape, f32), (shape, bf16)), (keep, got), name=name, scalar=False)
        return keep, rows_y(send)

    rates_tile = jnp.pad(w_rates.reshape(depth, 2 * heads), ((0, 0), (0, LANES - 2 * heads)))
    if near:
        taps_tile = conv_taps.reshape(CONV * heads, part)
        taps_tile = jnp.pad(taps_tile, ((0, depth - CONV * heads), (LANES - part, 0)))
        rates_tile = rates_tile + taps_tile
    mix_shard = jnp.concatenate([w_mix.reshape(depth, heads * width), rates_tile], 1)
    gate_up_shard = w_gate_up.reshape(depth, 2 * hidden)
    total = value_size + 3 * hidden
    filler = -total % (3 * LANES)
    rest_shard = jnp.concatenate(
        [w_out.T, gate_up_shard, w_down.T, jnp.zeros((depth, filler), bf16)], 1
    )
    step = (total + filler) // 3

    if near:
        mix_a, mix_b = mix_shard[: depth // 2], mix_shard[depth // 2 :]
        mix_az = near_z(mix_a)
    square = (rows, model)
    resid_in, both, gains = call(
        prepare,
        ((square, f32), ((2 * rows, model), bf16), ((2, model), f32)),
        (ids, layer_in, out_grad, mixer_gain.reshape(1, -1), ffn_gain.reshape(1, -1)),
        name="prepare",
    )
    if near:
        mix_b = after(mix_b, mix_az)
        mix_bz = near_z(mix_b)
        mix_ax = near_x(mix_az)
    both_all = gather_rows(both)
    if near:
        rest_0, rest_1, rest_2 = (rest_shard[:, g * step : (g + 1) * step] for g in range(3))
        rest_0 = after(rest_0, (mix_bz, mix_ax))
        rest_0z = near_z(rest_0)
        mix_bx = near_x(mix_bz)
        rest_1 = after(rest_1, (rest_0z, mix_bx))
        rest_1z = near_z(rest_1)
        rest_0x = near_x(rest_0z)
        mix_slots = [half_slot for pair in zip(mix_az + mix_ax, mix_bz + mix_bx) for half_slot in pair]
        taps = jnp.zeros((CONV * heads, part * size), f32)
    else:
        mix_slots = [far(mix_shard)]
        taps = lax.all_gather(conv_taps, "dp", axis=2, tiled=True).astype(f32)
        taps = taps.reshape(CONV * heads, part * size)
        rest_full = far(rest_shard)
        rest_slots = [[rest_full[:, g * step : (g + 1) * step]] for g in range(3)]

    first_head = rank * heads

    def on_lanes(per_head):
        here = lax.dynamic_slice_in_dim(per_head, first_head, heads)
        pairs = jnp.stack([here, jnp.zeros_like(here)], 1).reshape(1, -1)
        return jnp.pad(pairs, ((0, 0), (0, LANES - pairs.shape[1])))

    def off_lanes(row):
        here = row[: 2 * heads : 2]
        return lax.dynamic_update_slice_in_dim(jnp.zeros_like(a_log), here, first_head, 0)

    lanes = (on_lanes(a_log), on_lanes(dt_bias), head_gain.reshape(1, -1))
    gated, *kept = run_forward(near, ids, both_all, mix_slots, taps, *lanes)
    if near:
        gated, rest_2, rest_1z, rest_0x = lax.optimization_barrier((gated, rest_2, rest_1z, rest_0x))
        rest_2z = near_z(rest_2)
        rest_1x = near_x(rest_1z)
        rest_slots = [rest_0z + rest_0x]
    block_pair = (2 * rows, model)
    out_send, out_keep = call(
        out_product,
        ((block_pair, bf16), (block_pair, f32)),
        (ids, gated, *rest_slots[0]),
        (((model, value_size), bf16),),
        "out_product",
    )
    out_keep, out_got = sum_rows(out_send, out_keep, "out_fold")
    resid, ffn_in = call(
        middle_norm, ((square, f32), (square, bf16)), (out_keep, out_got, resid_in, gains), name="middle_norm", scalar=False
    )
    if near:
        ffn_in, rest_2z, rest_1x = lax.optimization_barrier((ffn_in, rest_2z, rest_1x))
        rest_2x = near_x(rest_2z)
        rest_slots += [rest_1z + rest_1x, rest_2z + rest_2x]
    ffn_all = gather_rows(ffn_in)
    tokens = rows * ranks
    counts = [len(group) for group in rest_slots]

    def ffn_kernel(*refs):
        ffn_refs, grad_refs, weights, outs, scratch = cut_list(refs, (4, 4, sum(counts), 8, 1))
        feed_forward(
            (value_size, value_size + 2 * hidden),
            (ffn_refs, grad_refs, cut_list(weights, counts), outs, scratch[0]),
        )

    ffn_rows, top_rows, hidden_low, grad_gate, ffn_send, ffn_keep, back_send, back_keep = call(
        ffn_kernel,
        (
            ((tokens, model), bf16),
            ((tokens, model), bf16),
            ((tokens, hidden), bf16),
            ((tokens, 2 * hidden), bf16),
            (block_pair, bf16),
            (block_pair, f32),
            (block_pair, bf16),
            (block_pair, f32),
        ),
        (*ffn_all, *both_all, *[slot for group in rest_slots for slot in group]),
        (((model, total + filler), bf16),),
        "feed_forward",
        scalar=False,
    )
    split = model // 2

    def scatter_x(send):
        return swap(send, "dp", size, 1) if near else send

    def scatter_z(keep, got):
        if not near:
            return keep, got
        summed = keep + got.astype(f32)
        low = summed.astype(bf16)
        return summed[:depth], [
            swap(low[p * depth : (p + 1) * depth], "dp", size, 2 * p) for p in range(1, half)
        ]

    def scatter_end(keep, got):
        if not near:
            return lax.psum_scatter(
                jnp.concatenate([keep, got.astype(f32)], 0), "dp", scatter_dimension=0, tiled=True
            )
        for block in got:
            keep = keep + block.astype(f32)
        return keep

    gate_x = scatter_x(rows_dot(ffn_rows[:, split:], grad_gate, bf16))
    back_keep, back_got = sum_rows(back_send, back_keep, "back_fold")
    down_x = scatter_x(rows_dot(top_rows[:, split:], hidden_low, bf16))
    grad_resid, mix_low, ffn_gain_grad = call(
        middle_back,
        ((square, f32), (square, bf16), ((1, model), f32)),
        (back_keep, back_got, resid, both, gains),
        name="middle_back",
        scalar=False,
    )
    mix_all = gather_rows(mix_low)
    gate_keep = rows_dot(ffn_rows[:, :split], grad_gate)
    down_keep = rows_dot(top_rows[:, :split], hidden_low)
    ffn_keep, ffn_got = sum_rows(ffn_send, ffn_keep, "ffn_fold")
    (layer_out,) = call(
        last_out, ((square, bf16),), (ids, ffn_keep, ffn_got, resid), ((square, f32),), "last_out"
    )
    gate_own, gate_z = scatter_z(gate_keep, gate_x)
    down_own, down_z = scatter_z(down_keep, down_x)
    grads, taps_grad, head_gain_grad, lanes_grad, mix_send_a, mix_send_b, grad_rows = run_backward(
        near, ids, mix_all, rest_slots[0], *lanes, kept
    )
    mix_xa, mix_xb = scatter_x(mix_send_a), scatter_x(mix_send_b)
    out_x = scatter_x(rows_dot(grad_rows[:, split:], gated, bf16))
    normed_rows, mix_full = kept[6], kept[7]
    cuts = (mix_send_a.shape[1], mix_send_b.shape[1])

    def products_kernel(*refs):
        mixer_products(near, refs)

    mix_keep_a, mix_keep_b, norm_send, norm_keep = call(
        products_kernel,
        (
            ((split, cuts[0]), f32),
            ((split, cuts[1]), f32),
            (block_pair, bf16),
            (block_pair, f32),
        ),
        (ids, normed_rows, grads, mix_full, taps_grad),
        name="mixer_products",
    )
    norm_keep, norm_got = sum_rows(norm_send, norm_keep, "norm_fold")
    out_keep = rows_dot(grad_rows[:, :split], gated)
    in_grad, gains_grad = call(
        last_grad,
        ((square, f32), ((2, model), f32)),
        (ids, norm_keep, norm_got, resid_in, gains, grad_resid, ffn_gain_grad),
        ((square, f32), ((2, model), f32)),
        "last_grad",
    )
    mix_own_a, mix_za = scatter_z(mix_keep_a, mix_xa)
    mix_own_b, mix_zb = scatter_z(mix_keep_b, mix_xb)
    out_own, out_z = scatter_z(out_keep, out_x)

    small = jnp.concatenate(
        [
            gains_grad.reshape(-1),
            head_gain_grad.reshape(-1),
            off_lanes(lanes_grad[0]),
            off_lanes(lanes_grad[1]),
        ]
    )
    length = small.size
    small = jnp.pad(small, (0, -length % (8 * LANES))).reshape(8, -1)
    for offset in (1, 2):
        small = small + swap(small, "tensor", ranks, offset)
    if near:
        for offset in (1, 2, 4):
            small = small + swap(small, "dp", size, offset)
    else:
        small = lax.psum(small, "dp")
    small = small.reshape(-1)[:length]
    grad_mixer_gain, grad_ffn_gain = small[:model], small[model : 2 * model]
    small = small[2 * model :]
    grad_head_gain, small = small[: head_gain.size], small[head_gain.size :]
    grad_a_log, grad_dt_bias = small[: a_log.size], small[a_log.size :]

    gate_total = scatter_end(gate_own, gate_z)
    down_total = scatter_end(down_own, down_z)
    out_total = scatter_end(out_own, out_z)
    mix_total = jnp.concatenate([scatter_end(mix_own_a, mix_za), scatter_end(mix_own_b, mix_zb)], 1)
    grad_w_rates = mix_total[:, heads * width : heads * width + 2 * heads].reshape(w_rates.shape)
    if near:
        grad_taps = mix_total[: CONV * heads, mix_total.shape[1] - part :].reshape(taps_shape)
    else:
        grad_taps = lax.psum_scatter(
            taps_grad.reshape(CONV, heads, -1), "dp", scatter_dimension=2, tiled=True
        )
    return (
        layer_out,
        in_grad,
        grad_mixer_gain,
        mix_total[:, : heads * width].reshape(w_mix.shape),
        grad_w_rates,
        grad_taps,
        grad_a_log,
        grad_dt_bias,
        grad_head_gain,
        out_total.T,
        grad_ffn_gain,
        gate_total.reshape(w_gate_up.shape),
        down_total.T,
    )


def solution(mesh):
    return jax.shard_map(
        per_device,
        mesh=mesh,
        in_specs=(
            P(("dp", "tensor"), None),
            P(),
            P("dp", "tensor", None),
            P("dp", "tensor", None),
            P(None, "tensor", "dp"),
            P(),
            P(),
            P(),
            P("tensor", "dp"),
            P(),
            P("dp", None, "tensor"),
            P("tensor", "dp"),
            P(("dp", "tensor"), None),
        ),
        out_specs=(
            P(("dp", "tensor"), None),
            P(("dp", "tensor"), None),
            P(),
            P("dp", "tensor", None),
            P("dp", "tensor", None),
            P(None, "tensor", "dp"),
            P(),
            P(),
            P(),
            P("tensor", "dp"),
            P(),
            P("dp", None, "tensor"),
            P("tensor", "dp"),
        ),
        check_vma=False,
    )
```

```python
import jax
import jax.numpy as jnp
from jax import lax
from jax.experimental import pallas as pl
from jax.experimental.pallas import tpu as pltpu
from jax.sharding import PartitionSpec as P

CONV = 4


highest = lax.Precision.HIGHEST
NORM_EPS = 1e-05
UNIT_EPS = 1e-06
bf16 = jnp.bfloat16
f32 = jnp.float32


def rows_dot(left, right, kind=f32):
    return lax.dot_general(
        left, right, (((0,), (0,)), ((), ())), preferred_element_type=f32
    ).astype(kind)


def cols_dot(left, right):
    return lax.dot_general(left, right, (((1,), (1,)), ((), ())), preferred_element_type=f32)


def dot(left, right):
    return jnp.dot(left, right, preferred_element_type=f32)


CHUNK = 128
LANES = 128


def mul(left, right, over=(1, 0), exact=False):
    dims = (((over[0],), (over[1],)), ((), ()))
    if exact:
        return lax.dot_general(left, right, dims, precision=highest, preferred_element_type=f32)
    return lax.dot_general(left.astype(bf16), right.astype(bf16), dims, preferred_element_type=f32)


def square_ids():
    shape = (CHUNK, CHUNK)
    return lax.broadcasted_iota(jnp.int32, shape, 0), lax.broadcasted_iota(jnp.int32, shape, 1)


def sigmoid(v):
    return 1.0 / (1.0 + jnp.exp(-v))


def softplus(v):
    return jnp.maximum(v, 0.0) + jnp.log1p(jnp.exp(-jnp.abs(v)))


def row_sum(v):
    return jnp.sum(v, axis=1, keepdims=True)


def unit_inverse(lower):
    rows, cols = square_ids()
    inverse = jnp.where(rows == cols, 1.0, 0.0)
    block = 1
    while block < CHUNK:
        corner = (
            (rows // (2 * block) == cols // (2 * block))
            & ((rows // block) % 2 == 1)
            & ((cols // block) % 2 == 0)
        )
        part = jnp.where(corner, lower, 0.0)
        if block == 1:
            inverse = inverse - part
        else:
            inverse = inverse - mul(mul(inverse, part), inverse)
        block *= 2
    return inverse


def shifted(ref, start, back, columns):
    if start == 0 and back:
        rows = lax.broadcasted_iota(jnp.int32, (CHUNK, columns.stop - columns.start), 0)
        return jnp.where(rows >= back, pltpu.roll(ref[0:CHUNK, columns], back, 0), 0.0)
    return ref[start - back : start - back + CHUNK, columns]


def short_conv(project_ref, taps_ref, start, head, heads, columns, tap_columns):
    total = None
    for tap in range(CONV):
        row = tap * heads + head
        term = taps_ref[row : row + 1, tap_columns] * shifted(
            project_ref, start, CONV - 1 - tap, columns
        )
        total = term if total is None else total + term
    return total


def decays(rates, log_rates, bias):
    log_decay = -jnp.exp(log_rates) * softplus(rates + bias)
    place = lax.broadcasted_iota(jnp.int32, rates.shape, 0)
    total = log_decay
    step = 1
    while step < CHUNK:
        total = total + jnp.where(place >= step, pltpu.roll(total, step, 0), 0.0)
        step *= 2
    return log_decay, total


def chunk_terms(head, project_ref, taps_ref, start, total, total_rows, strength, key_width, value_width):
    width = 2 * key_width + value_width
    base = head * width
    heads = project_ref.shape[1] // width
    terms = {}
    parts = (("q", 0, key_width), ("k", key_width, key_width), ("v", 2 * key_width, value_width))
    for name, at, size in parts:
        pre = short_conv(
            project_ref,
            taps_ref,
            start,
            head,
            heads,
            slice(base + at, base + at + size),
            slice(at, at + size),
        )
        gate = sigmoid(pre)
        mixed = pre * gate
        if name != "v":
            scale = lax.rsqrt(row_sum(mixed * mixed) + UNIT_EPS)
            mixed = mixed * scale
            terms[name + "_scale"] = scale
        terms[name + "_slope"] = (pre, gate)
        terms[name] = mixed
    terms["unit_q"] = terms["q"]
    terms["q"] = terms["q"] * key_width ** (-0.5)
    lane = 2 * head
    sums = total[:, lane : lane + 1]
    across = total_rows[lane : lane + 1, :]
    rows, cols = square_ids()
    decay = jnp.where(rows >= cols, jnp.exp(jnp.minimum(sums - across, 0.0)), 0.0)
    final = total[CHUNK - 1 : CHUNK, lane : lane + 1]
    terms["b"] = strength[:, lane + 1 : lane + 2]
    terms["since"] = jnp.exp(sums)
    terms["remaining"] = jnp.exp(final - sums)
    terms["through"] = jnp.exp(final)
    terms["decay"] = decay
    terms["dots"] = mul(terms["k"], terms["k"], (1, 1)) * jnp.where(rows > cols, decay, 0.0)
    terms["scores"] = mul(terms["q"], terms["k"], (1, 1)) * decay
    return terms


def stack_rows(refs, target, column):
    at = 0
    for ref in refs:
        rows = ref.shape[0]
        columns = min(ref.shape[1], target.shape[1] - column)
        target[at : at + rows, column : column + columns] = ref[:, :columns]
        at += rows


def rows_in_time(ids_ref, refs, target):
    size = target.shape[0] // len(refs)
    for k, ref in enumerate(refs):
        at = pl.multiple_of((ids_ref[0] ^ k) * size, size)
        target[pl.ds(at, size), :] = ref[0:size, :]


def order_of(ids_ref, place):
    return ids_ref[1 + place]


def taps_from_blocks(ids_ref, mix_ref, shape):
    rows, channels = shape
    count = mix_ref.shape[0] // LANES
    part = channels // count
    lane = lax.broadcasted_iota(jnp.int32, shape, 1)
    total = jnp.zeros(shape, f32)
    for place in range(count):
        block = mix_ref[place * LANES : place * LANES + 16, mix_ref.shape[1] - LANES :]
        block = block.astype(f32)[0:rows, LANES - part :]
        wide = jnp.concatenate([block] * count, 1)
        total = total + jnp.where(lane // part == order_of(ids_ref, place), wide, 0.0)
    return total


def taps_to_blocks(ids_ref, taps_ref, target, first):
    rows, channels = taps_ref.shape
    count = target.shape[0] // LANES
    part = channels // (2 * count)
    for place in range(count):
        owner = order_of(ids_ref, first + place)
        block = jnp.zeros((rows, part), f32)
        for other in range(2 * count):
            block = block + jnp.where(
                owner == other, taps_ref[:, other * part : (other + 1) * part], 0.0
            )
        block = jnp.concatenate([jnp.zeros((rows, LANES - part), f32), block], 1)
        block = jnp.concatenate([block, jnp.zeros((16 - rows, LANES), f32)], 0)
        at = (slice(place * LANES, place * LANES + 16), slice(target.shape[1] - LANES, target.shape[1]))
        target[at] = (target[at].astype(f32) + block).astype(target.dtype)


def rows_to_blocks(ids_ref, value, send_ref, keep_ref):
    size = value.shape[0] // 4
    for k in range(4):
        target = send_ref if k % 2 else keep_ref
        half = (k // 2) * size
        for block in range(4):

            @pl.when((ids_ref[0] ^ k) == block)
            def _(block=block, half=half, target=target):
                target[half : half + size, :] = value[block * size : (block + 1) * size, :].astype(
                    target.dtype
                )


def mixer_forward(near, refs):
    (ids_ref, taps_in_ref, log_rates_ref, bias_ref), row_refs, mix_refs, outs, scratch = refs
    project_ref, rates_ref, out_ref, states_ref, carried_ref, inverse_ref = outs[:6]
    normed_ref, mix_ref, taps_ref = outs[6:]
    q_scr, kr_scr, p_scr, w_scr, u_scr = scratch
    length = normed_ref.shape[0]
    heads = states_ref.shape[1]
    key_width, value_width = states_ref.shape[2:]
    width = project_ref.shape[1] // heads
    chunks = length // CHUNK
    rows_in_time(ids_ref, row_refs, normed_ref)
    stack_rows(mix_refs, mix_ref, 0)
    if near:
        taps_ref[...] = taps_from_blocks(ids_ref, mix_ref, taps_in_ref.shape)
    else:
        taps_ref[...] = taps_in_ref[...]
    for head in range(heads):
        columns = slice(head * width, (head + 1) * width)
        project_ref[:, columns] = dot(normed_ref[...], mix_ref[:, columns])
    rates_ref[...] = dot(normed_ref[...], mix_ref[:, heads * width :])
    through = {}
    for chunk in range(chunks):
        start = chunk * CHUNK
        rows = slice(start, start + CHUNK)
        rates = rates_ref[rows, :]
        _, total = decays(rates, log_rates_ref[...], bias_ref[...])
        strength = sigmoid(rates)
        total_rows = jnp.transpose(total)
        for head in range(heads):
            t = chunk_terms(
                head, project_ref, taps_ref, start, total, total_rows, strength, key_width, value_width
            )
            inverse = unit_inverse(t["b"] * t["dots"])
            inverse_ref[chunk, head] = inverse
            side = jnp.concatenate([(t["b"] * t["since"]) * t["k"], t["b"] * t["v"]], 1)
            solved = mul(inverse, side)
            w_scr[chunk, head] = solved[:, :key_width].astype(bf16)
            u_scr[chunk, head] = solved[:, key_width:]
            q_scr[chunk, head] = (t["q"] * t["since"]).astype(bf16)
            kr_scr[chunk, head] = t["k"] * t["remaining"]
            p_scr[chunk, head] = t["scores"].astype(bf16)
            through[chunk, head] = t["through"]
    state = [jnp.zeros((key_width, value_width), f32) for _ in range(heads)]
    for chunk in range(chunks):
        rows = slice(chunk * CHUNK, (chunk + 1) * CHUNK)
        for head in range(heads):
            columns = slice(head * value_width, (head + 1) * value_width)
            states_ref[chunk, head] = state[head]
            low = state[head].astype(bf16)
            carried = u_scr[chunk, head] - mul(w_scr[chunk, head], low)
            carried_ref[rows, columns] = carried
            out_ref[rows, columns] = mul(q_scr[chunk, head], low) + mul(p_scr[chunk, head], carried)
            state[head] = through[chunk, head] * state[head] + mul(
                kr_scr[chunk, head], carried, (0, 0), exact=True
            )


def out_product(ids_ref, gain_ref, normed_ref, out_ref, *refs):
    weight_refs, (gated_ref, gate_ref, weights_ref, send_ref, keep_ref) = refs[:-5], refs[-5:]
    value_width = gain_ref.shape[1]
    values = out_ref.shape[1]
    stack_rows(weight_refs, weights_ref, 0)
    for head in range(values // value_width):
        columns = slice(head * value_width, (head + 1) * value_width)
        gate = dot(normed_ref[...], weights_ref[:, columns])
        gate_ref[:, columns] = gate
        out = out_ref[:, columns]
        scale = lax.rsqrt(row_sum(out * out) / value_width + NORM_EPS)
        gated_ref[:, columns] = (out * scale * gain_ref[...] * (gate * sigmoid(gate))).astype(bf16)
    rows_to_blocks(ids_ref, cols_dot(gated_ref[...], weights_ref[:, values:]), send_ref, keep_ref)


def gate_back(ids_ref, gain_ref, normed_ref, out_ref, gated_ref, gate_ref, weights_ref, *refs):
    row_refs, (rows_ref, grad_out_ref, grad_gate_ref, gain_grad_ref, send_ref) = refs[:-5], refs[-5:]
    value_width = gain_ref.shape[1]
    values = out_ref.shape[1]
    rows_in_time(ids_ref, row_refs, rows_ref)
    gain = gain_ref[...]
    gain_total = jnp.zeros((1, value_width), f32)
    for head in range(values // value_width):
        columns = slice(head * value_width, (head + 1) * value_width)
        grad = dot(rows_ref[...], weights_ref[:, values + head * value_width : values + (head + 1) * value_width])
        out, gate = out_ref[:, columns], gate_ref[:, columns]
        scale = lax.rsqrt(row_sum(out * out) / value_width + NORM_EPS)
        unit = out * scale
        sig = sigmoid(gate)
        act = gate * sig
        gain_total = gain_total + jnp.sum(grad * unit * act, axis=0, keepdims=True)
        grad_gate_ref[:, columns] = (
            grad * gain * unit * (sig * (1.0 + gate * (1.0 - sig)))
        ).astype(bf16)
        inner = grad * act * gain
        grad_out_ref[:, columns] = scale * (inner - unit * (row_sum(inner * unit) / value_width))
    gain_grad_ref[...] = gain_total
    half = normed_ref.shape[1] // 2
    send_ref[:, :values] = rows_dot(normed_ref[:, half:], grad_gate_ref[...], bf16)
    send_ref[:, values:] = rows_dot(rows_ref[:, half:], gated_ref[...], bf16)


def mixer_backward(near, refs):
    (ids_ref, log_rates_ref, bias_ref, grad_out_scr), kept, outs, scratch = refs
    (
        project_ref,
        rates_ref,
        out_ref,
        states_ref,
        carried_ref,
        inverse_ref,
        normed_ref,
        _,
        taps_ref,
    ) = kept
    grads_ref, grad_taps_ref, grad_lanes_ref, send_ref = outs
    back_scr, grad_carried_scr, q_scr, kr_scr, p_scr, w_scr, mixed_scr = scratch
    length = normed_ref.shape[0]
    heads = states_ref.shape[1]
    key_width, value_width = states_ref.shape[2:]
    width = channels = project_ref.shape[1] // heads
    chunks = length // CHUNK

    def gather_terms(chunk):
        start = chunk * CHUNK
        rates = rates_ref[start : start + CHUNK, :]
        _, total = decays(rates, log_rates_ref[...], bias_ref[...])
        strength = sigmoid(rates)
        total_rows = jnp.transpose(total)
        return [
            chunk_terms(
                head, project_ref, taps_ref, start, total, total_rows, strength, key_width, value_width
            )
            for head in range(heads)
        ]

    through = {}
    for chunk in range(chunks):
        rows = slice(chunk * CHUNK, (chunk + 1) * CHUNK)
        terms = gather_terms(chunk)
        for head in range(heads):
            columns = slice(head * value_width, (head + 1) * value_width)
            t = terms[head]
            w_scr[chunk, head] = mul(
                inverse_ref[chunk, head], (t["b"] * t["since"]) * t["k"]
            ).astype(bf16)
            q_scr[chunk, head] = (t["q"] * t["since"]).astype(bf16)
            kr_scr[chunk, head] = (t["k"] * t["remaining"]).astype(bf16)
            p_scr[chunk, head] = t["scores"].astype(bf16)
            through[chunk, head] = t["through"]

    back = [jnp.zeros((key_width, value_width), f32) for _ in range(heads)]
    for chunk in reversed(range(chunks)):
        rows = slice(chunk * CHUNK, (chunk + 1) * CHUNK)
        for head in range(heads):
            columns = slice(head * value_width, (head + 1) * value_width)
            back_scr[chunk, head] = back[head]
            grad_out = grad_out_scr[rows, columns].astype(bf16)
            grad_carried = mul(p_scr[chunk, head], grad_out, (0, 0)) + mul(
                kr_scr[chunk, head], back[head]
            )
            grad_carried_scr[rows, columns] = grad_carried
            back[head] = (
                through[chunk, head] * back[head]
                + mul(q_scr[chunk, head], grad_out, (0, 0))
                - mul(w_scr[chunk, head], grad_carried, (0, 0))
            )

    rows_at, cols_at = square_ids()
    lane = lax.broadcasted_iota(jnp.int32, (CHUNK, LANES), 1)
    place = lax.broadcasted_iota(jnp.int32, (CHUNK, LANES), 0)
    log_total = jnp.zeros((1, LANES), f32)
    bias_total = jnp.zeros((1, LANES), f32)
    for chunk in range(chunks):
        rows = slice(chunk * CHUNK, (chunk + 1) * CHUNK)
        terms = gather_terms(chunk)
        sums_grad = jnp.zeros((CHUNK, LANES), f32)
        strength_grad = jnp.zeros((CHUNK, LANES), f32)
        for head in range(heads):
            columns = slice(head * value_width, (head + 1) * value_width)
            t = terms[head]
            b, since, remaining, decay = t["b"], t["since"], t["remaining"], t["decay"]
            q, k, v = t["q"], t["k"], t["v"]
            state = states_ref[chunk, head]
            back_now = back_scr[chunk, head]
            carried = carried_ref[rows, columns]
            grad_out = grad_out_scr[rows, columns]
            grad_side = mul(inverse_ref[chunk, head], grad_carried_scr[rows, columns], (0, 0))
            strict = jnp.where(rows_at > cols_at, -mul(grad_side, carried, (1, 1)), 0.0)
            grad_scores = mul(grad_out, carried, (1, 1))
            side_state = mul(grad_side, state, (1, 1))
            out_state = since * mul(grad_out, state, (1, 1))
            carried_back = remaining * mul(carried, back_now, (1, 1))
            key_side = since * row_sum(k * side_state)
            strict_dots = strict * t["dots"]
            grad_strength = row_sum(grad_side * v) - key_side + row_sum(strict_dots)
            pulls = grad_scores * t["scores"] + b * strict_dots
            key_back = row_sum(k * carried_back)
            grad_sums = (
                row_sum(pulls - jnp.transpose(pulls))
                - b * key_side
                + row_sum(q * out_state)
                - key_back
            )
            final = jnp.sum(key_back, axis=0, keepdims=True) + t["through"] * jnp.sum(
                row_sum(back_now * state), axis=0, keepdims=True
            )
            scores_low = (grad_scores * decay).astype(bf16)
            strict_low = (strict * (b * decay)).astype(bf16)
            k_low, q_low = k.astype(bf16), q.astype(bf16)
            grad_q = out_state + mul(scores_low, k_low)
            grad_k = (
                carried_back
                - (b * since) * side_state
                + mul(scores_low, q_low, (0, 0))
                + mul(strict_low, k_low)
                + mul(strict_low, k_low, (0, 0))
            )
            grad_v = b * grad_side
            sums_grad = sums_grad + jnp.where(
                lane == 2 * head, grad_sums + jnp.where(place == CHUNK - 1, final, 0.0), 0.0
            )
            strength_grad = strength_grad + jnp.where(lane == 2 * head + 1, grad_strength, 0.0)
            grad_q = grad_q * key_width ** (-0.5)
            unit = t["unit_q"]
            grad_q = t["q_scale"] * (grad_q - unit * row_sum(grad_q * unit))
            grad_k = t["k_scale"] * (grad_k - k * row_sum(grad_k * k))
            at = head * channels
            for name, grad, size in (
                ("q", grad_q, key_width),
                ("k", grad_k, key_width),
                ("v", grad_v, value_width),
            ):
                pre, sig = t[name + "_slope"]
                mixed_scr[rows, at : at + size] = grad * (sig * (1.0 + pre * (1.0 - sig)))
                at += size
        step = 1
        while step < CHUNK:
            sums_grad = sums_grad + jnp.where(
                place < CHUNK - step, pltpu.roll(sums_grad, CHUNK - step, 0), 0.0
            )
            step *= 2
        rates = rates_ref[rows, :]
        log_decay, _ = decays(rates, log_rates_ref[...], bias_ref[...])
        strength = sigmoid(rates)
        inputs_grad = sums_grad * (-jnp.exp(log_rates_ref[...])) * sigmoid(rates + bias_ref[...])
        log_total = log_total + jnp.sum(sums_grad * log_decay, axis=0, keepdims=True)
        bias_total = bias_total + jnp.sum(inputs_grad, axis=0, keepdims=True)
        grads_ref[rows, heads * width :] = (
            inputs_grad + strength_grad * strength * (1.0 - strength)
        ).astype(bf16)
    grad_lanes_ref[0:1, :] = log_total
    grad_lanes_ref[1:2, :] = bias_total

    mixed_scr[length : length + 8, :] = jnp.zeros((8, mixed_scr.shape[1]), f32)
    for head in range(heads):
        columns = slice(head * channels, (head + 1) * channels)
        source = slice(head * width, head * width + channels)
        taps_here = [jnp.zeros((1, channels), f32) for _ in range(CONV)]
        for chunk in range(chunks):
            start = chunk * CHUNK
            total = None
            now = mixed_scr[start : start + CHUNK, columns]
            for tap in range(CONV):
                ahead = CONV - 1 - tap
                row = tap * heads + head
                term = taps_ref[row : row + 1, :] * (
                    mixed_scr[start + ahead : start + ahead + CHUNK, columns]
                )
                total = term if total is None else total + term
                taps_here[tap] = taps_here[tap] + jnp.sum(
                    now * shifted(project_ref, start, ahead, source), axis=0, keepdims=True
                )
            grads_ref[start : start + CHUNK, source] = total.astype(bf16)
        for tap in range(CONV):
            row = tap * heads + head
            grad_taps_ref[row : row + 1, :] = taps_here[tap]
    half = normed_ref.shape[1] // 2
    send_ref[...] = rows_dot(normed_ref[:, half:], grads_ref[...], bf16)
    if near:
        taps_to_blocks(ids_ref, grad_taps_ref, send_ref, half // LANES)


def mixer_products(near, refs):
    ids_ref, normed_ref, rows_ref, gated_ref, grads_ref, grad_gate_ref, mix_ref, weights_ref, grad_taps_ref = refs[:9]
    back_send_ref, back_keep_ref, gate_keep_ref, mix_keep_ref = refs[9:]
    values = grad_gate_ref.shape[1]
    back = cols_dot(grads_ref[...], mix_ref[...])
    back = back + cols_dot(grad_gate_ref[...], weights_ref[:, :values])
    rows_to_blocks(ids_ref, back, back_send_ref, back_keep_ref)
    half = normed_ref.shape[1] // 2
    gate_keep_ref[:, :values] = rows_dot(normed_ref[:, :half], grad_gate_ref[...])
    gate_keep_ref[:, values:] = rows_dot(rows_ref[:, :half], gated_ref[...])
    mix_keep_ref[...] = rows_dot(normed_ref[:, :half], grads_ref[...])
    if near:
        taps_to_blocks(ids_ref, grad_taps_ref, mix_keep_ref, 0)


def norm_scale(rows):
    return lax.rsqrt(jnp.mean(rows * rows, axis=1, keepdims=True) + NORM_EPS)


def prepare(ids_ref, rows_ref, grad_ref, mixer_gain_ref, ffn_gain_ref, resid_ref, both_ref, gains_ref):
    size = rows_ref.shape[0]
    count = rows_ref.shape[1] // LANES
    for place in range(count):
        at = pl.multiple_of(order_of(ids_ref, place) * LANES, LANES)
        here = slice(place * LANES, (place + 1) * LANES)
        resid_ref[:, here] = rows_ref[:, pl.ds(at, LANES)].astype(f32)
        both_ref[size:, here] = grad_ref[:, pl.ds(at, LANES)]
        gains_ref[0:1, here] = mixer_gain_ref[:, pl.ds(at, LANES)]
        gains_ref[1:2, here] = ffn_gain_ref[:, pl.ds(at, LANES)]
    resid = resid_ref[...]
    both_ref[0:size, :] = (resid * norm_scale(resid) * gains_ref[0:1, :]).astype(bf16)


def fold(keep_ref, got_ref, keep_out_ref, send_ref):
    size = send_ref.shape[0]
    keep_out_ref[...] = keep_ref[0:size, :] + got_ref[0:size, :].astype(f32)
    send_ref[...] = (keep_ref[size:, :] + got_ref[size:, :].astype(f32)).astype(bf16)


def middle_norm(keep_ref, got_ref, resid_in_ref, gains_ref, resid_ref, ffn_in_ref):
    resid = resid_in_ref[...] + keep_ref[...] + got_ref[...].astype(f32)
    resid_ref[...] = resid
    ffn_in_ref[...] = (resid * norm_scale(resid) * gains_ref[1:2, :]).astype(bf16)


def place_of(ids_ref, block, count):
    return ids_ref[1 + count + block]


def feed_forward(ids_ref, refs):
    ffn_refs, grad_refs, (weights_ref,), outs, (ffn_ref, top_ref, weights_scr) = refs
    ffn_out_ref, top_out_ref, hidden_ref, grad_gate_ref, out_send, out_keep, back_send, back_keep = outs
    size = ffn_refs[0].shape[0]
    count = ffn_ref.shape[1] // LANES
    for block in range(count):
        at = pl.multiple_of(order_of(ids_ref, block) * LANES, LANES)
        weights_scr[block * LANES : (block + 1) * LANES, :] = weights_ref[pl.ds(at, LANES), :]
    for k in range(4):
        ffn_ref[k * size : (k + 1) * size, :] = ffn_refs[k][...]
        top_ref[k * size : (k + 1) * size, :] = grad_refs[k][size:, :]
    hidden_size = hidden_ref.shape[1]
    gate_up_w = weights_scr[:, : 2 * hidden_size]
    down_w = weights_scr[:, 2 * hidden_size : 3 * hidden_size]
    gate_up = dot(ffn_ref[...], gate_up_w)
    grad_hidden = dot(top_ref[...], down_w)
    gate, up = gate_up[:, :hidden_size], gate_up[:, hidden_size:]
    sig = sigmoid(gate)
    act = gate * sig
    hidden_ref[...] = (act * up).astype(bf16)
    grad_gate_ref[:, :hidden_size] = (grad_hidden * up * (sig * (1.0 + gate * (1.0 - sig)))).astype(bf16)
    grad_gate_ref[:, hidden_size:] = (grad_hidden * act).astype(bf16)
    back = cols_dot(grad_gate_ref[...], gate_up_w)
    out = cols_dot(hidden_ref[...], down_w)
    for value, send, keep in ((back, back_send, back_keep), (out, out_send, out_keep)):
        for k in range(4):
            target = send if k % 2 else keep
            half = (k // 2) * size
            target[half : half + size, :] = value[k * size : (k + 1) * size, :].astype(target.dtype)
    for block in range(count):
        at = pl.multiple_of(place_of(ids_ref, block, count) * LANES, LANES)
        here = slice(block * LANES, (block + 1) * LANES)
        ffn_out_ref[:, here] = ffn_ref[:, pl.ds(at, LANES)]
        top_out_ref[:, here] = top_ref[:, pl.ds(at, LANES)]


def feed_products(ffn_ref, top_ref, hidden_ref, grad_gate_ref, out_ref):
    hidden_size = hidden_ref.shape[1]
    out_ref[:, : 2 * hidden_size] = rows_dot(ffn_ref[...], grad_gate_ref[...], out_ref.dtype)
    out_ref[:, 2 * hidden_size : 3 * hidden_size] = rows_dot(
        top_ref[...], hidden_ref[...], out_ref.dtype
    )
    rest = out_ref.shape[1] - 3 * hidden_size
    if rest:
        out_ref[:, 3 * hidden_size :] = jnp.zeros((out_ref.shape[0], rest), out_ref.dtype)


def norm_reverse(grad, rows, gain):
    scale = norm_scale(rows)
    unit = rows * scale
    inner = grad * gain
    gain_grad = jnp.sum(grad * unit, axis=0, keepdims=True)
    return scale * (inner - unit * jnp.mean(inner * unit, axis=1, keepdims=True)), gain_grad


def middle_back(
    back_keep_ref, back_got_ref, resid_ref, both_ref, gains_ref, grad_ref, low_ref, gain_grad_ref
):
    grad_ffn_in = back_keep_ref[...] + back_got_ref[...].astype(f32)
    grad, gain_grad = norm_reverse(grad_ffn_in, resid_ref[...], gains_ref[1:2, :])
    grad = grad + both_ref[both_ref.shape[0] // 2 :, :].astype(f32)
    grad_ref[...] = grad
    low_ref[...] = grad.astype(bf16)
    gain_grad_ref[...] = gain_grad


def last_out(ids_ref, keep_ref, got_ref, resid_ref, out_ref, scr):
    scr[...] = resid_ref[...] + keep_ref[...] + got_ref[...].astype(f32)
    count = out_ref.shape[1] // LANES
    for block in range(count):
        at = pl.multiple_of(place_of(ids_ref, block, count) * LANES, LANES)
        out_ref[:, block * LANES : (block + 1) * LANES] = scr[:, pl.ds(at, LANES)].astype(bf16)


def last_grad(
    ids_ref, keep_ref, got_ref, resid_in_ref, gains_ref, grad_ref, gain_grad_ref, out_ref, gains_out_ref, scr, gain_scr
):
    grad_normed = keep_ref[...] + got_ref[...].astype(f32)
    grad, gain_grad = norm_reverse(grad_normed, resid_in_ref[...], gains_ref[0:1, :])
    scr[...] = grad + grad_ref[...]
    gain_scr[0:1, :] = gain_grad
    gain_scr[1:2, :] = gain_grad_ref[...]
    count = out_ref.shape[1] // LANES
    for block in range(count):
        at = pl.multiple_of(place_of(ids_ref, block, count) * LANES, LANES)
        here = slice(block * LANES, (block + 1) * LANES)
        out_ref[:, here] = scr[:, pl.ds(at, LANES)]
        gains_out_ref[:, here] = gain_scr[:, pl.ds(at, LANES)]


def call(kernel, outs, operands, scratch=(), name=None, scalar=True):
    specs = [pl.BlockSpec(memory_space=pltpu.VMEM)] * len(operands)
    if scalar:
        specs[0] = pl.BlockSpec(memory_space=pltpu.SMEM)
    return pl.pallas_call(
        kernel,
        out_shape=tuple(jax.ShapeDtypeStruct(shape, kind) for shape, kind in outs),
        in_specs=specs,
        out_specs=tuple([pl.BlockSpec(memory_space=pltpu.VMEM)] * len(outs)),
        scratch_shapes=[pltpu.VMEM(shape, kind) for shape, kind in scratch],
        compiler_params=pltpu.CompilerParams(vmem_limit_bytes=56 * 2**20),
        name=name,
    )(*operands)


def cut_list(items, sizes):
    parts, at = [], 0
    for size in sizes:
        parts.append(items[at : at + size])
        at += size
    return parts


def run_forward(near, ids, rows, mix, taps, log_rates, bias, value_width):
    length = rows[0].shape[0] // 2 * len(rows)
    model = rows[0].shape[1]
    wide = mix[0].shape[1]
    columns = wide - LANES
    channels = taps.shape[1]
    heads = taps.shape[0] // CONV
    key_width = (channels - value_width) // 2
    pair = (length // CHUNK, heads)
    values = heads * value_width

    def kernel(*refs):
        mixer_forward(near, cut_list(refs, (4, len(rows), len(mix), 9, 5)))

    return call(
        kernel,
        (
            ((length, columns), f32),
            ((length, LANES), f32),
            ((length, values), f32),
            (pair + (key_width, value_width), f32),
            ((length, values), f32),
            (pair + (CHUNK, CHUNK), f32),
            ((length, model), bf16),
            ((model, wide), bf16),
            (taps.shape, f32),
        ),
        (ids, taps, log_rates, bias, *rows, *mix),
        (
            (pair + (CHUNK, key_width), bf16),
            (pair + (CHUNK, key_width), f32),
            (pair + (CHUNK, CHUNK), bf16),
            (pair + (CHUNK, key_width), bf16),
            (pair + (CHUNK, value_width), f32),
        ),
        "mixer_forward",
    )


def run_backward(near, ids, grad_out, log_rates, bias, kept):
    project, _, out, states, _, _, normed, mix, taps = kept
    length, model = normed.shape
    values = out.shape[1]
    wide = mix.shape[1]
    heads, key_width, value_width = states.shape[1:]
    pair = (length // CHUNK, heads)

    def kernel(*refs):
        mixer_backward(near, cut_list(refs, (4, len(kept), 4, 7)))

    return call(
        kernel,
        (
            ((length, wide), bf16),
            (taps.shape, f32),
            ((2, LANES), f32),
            ((model // 2, wide), bf16),
        ),
        (ids, log_rates, bias, grad_out, *kept),
        (
            (pair + (key_width, value_width), f32),
            ((length, values), f32),
            (pair + (CHUNK, key_width), bf16),
            (pair + (CHUNK, key_width), bf16),
            (pair + (CHUNK, CHUNK), bf16),
            (pair + (CHUNK, key_width), bf16),
            ((length + 8, heads * taps.shape[1]), f32),
        ),
        "mixer_backward",
    )


def swap(array, axis, size, offset):
    return lax.ppermute(array, axis, [(i, i ^ offset) for i in range(size)])


def after(arrays, others):
    kept, _ = lax.optimization_barrier((arrays, others))
    return kept


def per_device(
    layer_in,
    mixer_gain,
    w_mix,
    w_rates,
    conv_taps,
    a_log,
    dt_bias,
    head_gain,
    w_out,
    ffn_gain,
    w_gate_up,
    w_down,
    out_grad,
):
    size = lax.axis_size("dp")
    ranks = lax.axis_size("tensor")
    depth, heads, width = w_mix.shape
    model = layer_in.shape[1]
    hidden = w_gate_up.shape[2]
    value_size = w_out.shape[0]
    rows = layer_in.shape[0]
    taps_shape = conv_taps.shape
    part = taps_shape[2]
    near = size == 8 and depth == LANES and 2 * part == LANES
    half = size // 2
    rank, own = lax.axis_index("tensor"), lax.axis_index("dp")
    blocks = model // LANES
    if near:
        offsets = [2 * p for p in range(half)] + [2 * p + 1 for p in range(half)]
        order = own ^ jnp.array(offsets, jnp.int32)
        places = [offsets.index(k) for k in range(size)]
        index = own ^ jnp.arange(size, dtype=jnp.int32)
        place = jnp.where(index % 2 == 0, index // 2, half + index // 2)
        assert places == [k // 2 if k % 2 == 0 else half + k // 2 for k in range(size)]
    else:
        order = place = jnp.arange(blocks, dtype=jnp.int32)
    ids = jnp.concatenate([jnp.full((1,), rank, jnp.int32), order, place])

    def near_z(shard):
        return [shard] + [swap(shard, "dp", size, 2 * p) for p in range(1, half)]

    def near_x(shards):
        return [swap(shard, "dp", size, 1) for shard in shards]

    def far(shard):
        return lax.all_gather(shard, "dp", axis=0, tiled=True)

    def rows_y(block):
        return swap(block, "tensor", ranks, 2)

    def rows_core(block):
        return swap(block, "tensor", ranks, 1)

    def gather_rows(block):
        across = rows_y(block)
        return [block, rows_core(block), across, rows_core(across)]

    def sum_rows(send, keep, name):
        got = rows_core(send)
        shape = (rows, model)
        keep, send = call(fold, ((shape, f32), (shape, bf16)), (keep, got), name=name, scalar=False)
        return keep, rows_y(send)

    channels = width - head_gain.shape[0]
    values = value_size
    rates_tile = jnp.pad(w_rates.reshape(depth, 2 * heads), ((0, 0), (0, LANES - 2 * heads)))
    if near:
        taps_tile = conv_taps.reshape(CONV * heads, part)
        taps_tile = jnp.pad(taps_tile, ((0, depth - CONV * heads), (LANES - part, 0)))
        rates_tile = rates_tile + taps_tile
    mix_shard = jnp.concatenate(
        [w_mix[:, :, :channels].reshape(depth, heads * channels), rates_tile], 1
    )
    gate_shard = jnp.concatenate([w_mix[:, :, channels:].reshape(depth, values), w_out.T], 1)
    filler = -3 * hidden % LANES
    ffn_shard = jnp.concatenate(
        [w_gate_up.reshape(depth, 2 * hidden), w_down.T, jnp.zeros((depth, filler), bf16)], 1
    )

    if near:
        mix_z = near_z(mix_shard)
    square = (rows, model)
    resid_in, both, gains = call(
        prepare,
        ((square, f32), ((2 * rows, model), bf16), ((2, model), f32)),
        (ids, layer_in, out_grad, mixer_gain.reshape(1, -1), ffn_gain.reshape(1, -1)),
        name="prepare",
    )
    ffn_full = far(ffn_shard)
    both_all = gather_rows(both)
    if near:
        gate_shard = after(gate_shard, mix_z)
        gate_z = near_z(gate_shard)
        mix_slots = mix_z + near_x(mix_z)
        taps = jnp.zeros((CONV * heads, part * size), f32)
    else:
        mix_slots = [far(mix_shard)]
        gate_slots = [far(gate_shard)]
        taps = lax.all_gather(conv_taps, "dp", axis=2, tiled=True).astype(f32)
        taps = taps.reshape(CONV * heads, part * size)

    first_head = rank * heads

    def on_lanes(per_head):
        here = lax.dynamic_slice_in_dim(per_head, first_head, heads)
        pairs = jnp.stack([here, jnp.zeros_like(here)], 1).reshape(1, -1)
        return jnp.pad(pairs, ((0, 0), (0, LANES - pairs.shape[1])))

    def off_lanes(row):
        here = row[: 2 * heads : 2]
        return lax.dynamic_update_slice_in_dim(jnp.zeros_like(a_log), here, first_head, 0)

    lanes = (on_lanes(a_log), on_lanes(dt_bias))
    gain_row = head_gain.reshape(1, -1)
    kept = run_forward(near, ids, both_all, mix_slots, taps, *lanes, head_gain.shape[0])
    heads_out, normed_rows, mix_full = kept[2], kept[6], kept[7]
    if near:
        gate_slots = gate_z + near_x(gate_z)
    tokens = rows * ranks
    block_pair = (2 * rows, model)
    gated, gate, gate_full, out_send, out_keep = call(
        out_product,
        (
            ((tokens, values), bf16),
            ((tokens, values), f32),
            ((model, 2 * values), bf16),
            (block_pair, bf16),
            (block_pair, f32),
        ),
        (ids, gain_row, normed_rows, heads_out, *gate_slots),
        (),
        "out_product",
    )
    out_keep, out_got = sum_rows(out_send, out_keep, "out_fold")
    resid, ffn_in = call(
        middle_norm, ((square, f32), (square, bf16)), (out_keep, out_got, resid_in, gains), name="middle_norm", scalar=False
    )
    ffn_all = gather_rows(ffn_in)

    def ffn_kernel(ids_ref, *refs):
        feed_forward(ids_ref, cut_list(refs, (4, 4, 1, 8, 3)))

    ffn_rows, top_rows, hidden_low, grad_gate, ffn_send, ffn_keep, back_send, back_keep = call(
        ffn_kernel,
        (
            ((tokens, model), bf16),
            ((tokens, model), bf16),
            ((tokens, hidden), bf16),
            ((tokens, 2 * hidden), bf16),
            (block_pair, bf16),
            (block_pair, f32),
            (block_pair, bf16),
            (block_pair, f32),
        ),
        (ids, *ffn_all, *both_all, ffn_full),
        (((tokens, model), bf16), ((tokens, model), bf16), (ffn_full.shape, bf16)),
        "feed_forward",
    )
    split = model // 2

    def scatter_x(send):
        return swap(send, "dp", size, 1) if near else send

    def scatter_z(keep, got):
        if not near:
            return keep, got
        summed = keep + got.astype(f32)
        low = summed.astype(bf16)
        return summed[:depth], [
            swap(low[p * depth : (p + 1) * depth], "dp", size, 2 * p) for p in range(1, half)
        ]

    def scatter_end(keep, got):
        if not near:
            return lax.psum_scatter(
                jnp.concatenate([keep, got.astype(f32)], 0), "dp", scatter_dimension=0, tiled=True
            )
        for block in got:
            keep = keep + block.astype(f32)
        return keep

    back_keep, back_got = sum_rows(back_send, back_keep, "back_fold")
    (ffn_grads,) = call(
        feed_products,
        (((model, 3 * hidden + filler), bf16 if near else f32),),
        (ffn_rows, top_rows, hidden_low, grad_gate),
        name="feed_products",
        scalar=False,
    )
    ffn_total = lax.psum_scatter(ffn_grads, "dp", scatter_dimension=0, tiled=True).astype(f32)
    grad_resid, mix_low, ffn_gain_grad = call(
        middle_back,
        ((square, f32), (square, bf16), ((1, model), f32)),
        (back_keep, back_got, resid, both, gains),
        name="middle_back",
        scalar=False,
    )
    mix_all = gather_rows(mix_low)
    ffn_keep, ffn_got = sum_rows(ffn_send, ffn_keep, "ffn_fold")
    (layer_out,) = call(
        last_out, ((square, bf16),), (ids, ffn_keep, ffn_got, resid), ((square, f32),), "last_out"
    )
    grad_rows, grad_out, gate_grad, head_gain_grad, gate_send = call(
        gate_back,
        (
            ((tokens, model), bf16),
            ((tokens, values), f32),
            ((tokens, values), bf16),
            (gain_row.shape, f32),
            ((split, 2 * values), bf16),
        ),
        (ids, gain_row, normed_rows, heads_out, gated, gate, gate_full, *mix_all),
        (),
        "gate_back",
    )
    gate_got = scatter_x(gate_send)
    grads, taps_grad, lanes_grad, mix_send = run_backward(near, ids, grad_out, *lanes, kept)
    mix_got = scatter_x(mix_send)

    def products_kernel(*refs):
        mixer_products(near, refs)

    norm_send, norm_keep, gate_keep, mix_keep = call(
        products_kernel,
        (
            (block_pair, bf16),
            (block_pair, f32),
            ((split, 2 * values), f32),
            (mix_send.shape, f32),
        ),
        (ids, normed_rows, grad_rows, gated, grads, gate_grad, mix_full, gate_full, taps_grad),
        name="mixer_products",
    )
    gate_own, gate_far = scatter_z(gate_keep, gate_got)
    norm_keep, norm_got = sum_rows(norm_send, norm_keep, "norm_fold")
    in_grad, gains_grad = call(
        last_grad,
        ((square, f32), ((2, model), f32)),
        (ids, norm_keep, norm_got, resid_in, gains, grad_resid, ffn_gain_grad),
        ((square, f32), ((2, model), f32)),
        "last_grad",
    )
    mix_own, mix_far = scatter_z(mix_keep, mix_got)

    small = jnp.concatenate(
        [
            gains_grad.reshape(-1),
            head_gain_grad.reshape(-1),
            off_lanes(lanes_grad[0]),
            off_lanes(lanes_grad[1]),
        ]
    )
    length = small.size
    small = jnp.pad(small, (0, -length % (8 * LANES))).reshape(8, -1)
    for offset in (1, 2):
        small = small + swap(small, "tensor", ranks, offset)
    if near:
        for offset in (1, 2, 4):
            small = small + swap(small, "dp", size, offset)
    else:
        small = lax.psum(small, "dp")
    small = small.reshape(-1)[:length]
    grad_mixer_gain, grad_ffn_gain = small[:model], small[model : 2 * model]
    small = small[2 * model :]
    grad_head_gain, small = small[: head_gain.size], small[head_gain.size :]
    grad_a_log, grad_dt_bias = small[: a_log.size], small[a_log.size :]

    gate_total = scatter_end(gate_own, gate_far)
    mix_total = scatter_end(mix_own, mix_far)
    grad_w_mix = jnp.concatenate(
        [
            mix_total[:, : heads * channels].reshape(depth, heads, channels),
            gate_total[:, :values].reshape(depth, heads, -1),
        ],
        2,
    )
    grad_w_rates = mix_total[:, heads * channels : heads * channels + 2 * heads].reshape(w_rates.shape)
    if near:
        grad_taps = mix_total[: CONV * heads, mix_total.shape[1] - part :].reshape(taps_shape)
    else:
        grad_taps = lax.psum_scatter(
            taps_grad.reshape(CONV, heads, -1), "dp", scatter_dimension=2, tiled=True
        )
    return (
        layer_out,
        in_grad,
        grad_mixer_gain,
        grad_w_mix,
        grad_w_rates,
        grad_taps,
        grad_a_log,
        grad_dt_bias,
        grad_head_gain,
        gate_total[:, values:].T,
        grad_ffn_gain,
        ffn_total[:, : 2 * hidden].reshape(w_gate_up.shape),
        ffn_total[:, 2 * hidden : 3 * hidden].T,
    )


def solution(mesh):
    return jax.shard_map(
        per_device,
        mesh=mesh,
        in_specs=(
            P(("dp", "tensor"), None),
            P(),
            P("dp", "tensor", None),
            P("dp", "tensor", None),
            P(None, "tensor", "dp"),
            P(),
            P(),
            P(),
            P("tensor", "dp"),
            P(),
            P("dp", None, "tensor"),
            P("tensor", "dp"),
            P(("dp", "tensor"), None),
        ),
        out_specs=(
            P(("dp", "tensor"), None),
            P(("dp", "tensor"), None),
            P(),
            P("dp", "tensor", None),
            P("dp", "tensor", None),
            P(None, "tensor", "dp"),
            P(),
            P(),
            P(),
            P("tensor", "dp"),
            P(),
            P("dp", None, "tensor"),
            P("tensor", "dp"),
        ),
        check_vma=False,
    )
```

```python
import jax
import jax.numpy as jnp
from jax import lax
from jax.experimental import pallas as pl
from jax.experimental.pallas import tpu as pltpu
from jax.sharding import PartitionSpec as P

CONV = 4


highest = lax.Precision.HIGHEST
NORM_EPS = 1e-05
UNIT_EPS = 1e-06
bf16 = jnp.bfloat16
f32 = jnp.float32


def rows_dot(left, right, kind=f32):
    return lax.dot_general(
        left, right, (((0,), (0,)), ((), ())), preferred_element_type=f32
    ).astype(kind)


def cols_dot(left, right):
    return lax.dot_general(left, right, (((1,), (1,)), ((), ())), preferred_element_type=f32)


def dot(left, right):
    return jnp.dot(left, right, preferred_element_type=f32)


CHUNK = 128
LANES = 128


def mul(left, right, over=(1, 0), exact=False):
    dims = (((over[0],), (over[1],)), ((), ()))
    if exact:
        return lax.dot_general(left, right, dims, precision=highest, preferred_element_type=f32)
    return lax.dot_general(left.astype(bf16), right.astype(bf16), dims, preferred_element_type=f32)


def square_ids():
    shape = (CHUNK, CHUNK)
    return lax.broadcasted_iota(jnp.int32, shape, 0), lax.broadcasted_iota(jnp.int32, shape, 1)


def sigmoid(v):
    return 1.0 / (1.0 + jnp.exp(-v))


def softplus(v):
    return jnp.maximum(v, 0.0) + jnp.log1p(jnp.exp(-jnp.abs(v)))


def row_sum(v):
    return jnp.sum(v, axis=1, keepdims=True)


def unit_inverse(lower):
    rows, cols = square_ids()
    inverse = jnp.where(rows == cols, 1.0, 0.0)
    block = 1
    while block < CHUNK:
        corner = (
            (rows // (2 * block) == cols // (2 * block))
            & ((rows // block) % 2 == 1)
            & ((cols // block) % 2 == 0)
        )
        part = jnp.where(corner, lower, 0.0)
        if block == 1:
            inverse = inverse - part
        else:
            inverse = inverse - mul(mul(inverse, part), inverse)
        block *= 2
    return inverse


def shifted(ref, start, back, columns):
    if start == 0 and back:
        rows = lax.broadcasted_iota(jnp.int32, (CHUNK, columns.stop - columns.start), 0)
        return jnp.where(rows >= back, pltpu.roll(ref[0:CHUNK, columns], back, 0), 0.0)
    return ref[start - back : start - back + CHUNK, columns]


def short_conv(project_ref, taps_ref, start, head, heads, columns, tap_columns):
    total = None
    for tap in range(CONV):
        row = tap * heads + head
        term = taps_ref[row : row + 1, tap_columns] * shifted(
            project_ref, start, CONV - 1 - tap, columns
        )
        total = term if total is None else total + term
    return total


def decays(rates, log_rates, bias):
    log_decay = -jnp.exp(log_rates) * softplus(rates + bias)
    place = lax.broadcasted_iota(jnp.int32, rates.shape, 0)
    total = log_decay
    step = 1
    while step < CHUNK:
        total = total + jnp.where(place >= step, pltpu.roll(total, step, 0), 0.0)
        step *= 2
    return log_decay, total


def chunk_terms(head, project_ref, taps_ref, start, total, total_rows, strength, key_width, value_width):
    width = 2 * key_width + value_width
    base = head * width
    heads = project_ref.shape[1] // width
    terms = {}
    parts = (("q", 0, key_width), ("k", key_width, key_width), ("v", 2 * key_width, value_width))
    for name, at, size in parts:
        pre = short_conv(
            project_ref,
            taps_ref,
            start,
            head,
            heads,
            slice(base + at, base + at + size),
            slice(at, at + size),
        )
        gate = sigmoid(pre)
        mixed = pre * gate
        if name != "v":
            scale = lax.rsqrt(row_sum(mixed * mixed) + UNIT_EPS)
            mixed = mixed * scale
            terms[name + "_scale"] = scale
        terms[name + "_slope"] = (pre, gate)
        terms[name] = mixed
    terms["unit_q"] = terms["q"]
    terms["q"] = terms["q"] * key_width ** (-0.5)
    lane = 2 * head
    sums = total[:, lane : lane + 1]
    across = total_rows[lane : lane + 1, :]
    rows, cols = square_ids()
    decay = jnp.where(rows >= cols, jnp.exp(jnp.minimum(sums - across, 0.0)), 0.0)
    final = total[CHUNK - 1 : CHUNK, lane : lane + 1]
    terms["b"] = strength[:, lane + 1 : lane + 2]
    terms["since"] = jnp.exp(sums)
    terms["remaining"] = jnp.exp(final - sums)
    terms["through"] = jnp.exp(final)
    terms["decay"] = decay
    terms["dots"] = mul(terms["k"], terms["k"], (1, 1)) * jnp.where(rows > cols, decay, 0.0)
    terms["scores"] = mul(terms["q"], terms["k"], (1, 1)) * decay
    return terms


def stack_rows(refs, target, column):
    at = 0
    for ref in refs:
        rows = ref.shape[0]
        columns = min(ref.shape[1], target.shape[1] - column)
        target[at : at + rows, column : column + columns] = ref[:, :columns]
        at += rows


def rows_in_time(ids_ref, refs, target):
    size = target.shape[0] // len(refs)
    for k, ref in enumerate(refs):
        at = pl.multiple_of((ids_ref[0] ^ k) * size, size)
        target[pl.ds(at, size), :] = ref[0:size, :]


def order_of(ids_ref, place):
    return ids_ref[1 + place]


def taps_from_blocks(ids_ref, mix_ref, shape):
    rows, channels = shape
    count = mix_ref.shape[0] // LANES
    part = channels // count
    lane = lax.broadcasted_iota(jnp.int32, shape, 1)
    total = jnp.zeros(shape, f32)
    for place in range(count):
        block = mix_ref[place * LANES : place * LANES + 16, mix_ref.shape[1] - LANES :]
        block = block.astype(f32)[0:rows, LANES - part :]
        wide = jnp.concatenate([block] * count, 1)
        total = total + jnp.where(lane // part == order_of(ids_ref, place), wide, 0.0)
    return total


def taps_to_blocks(ids_ref, taps_ref, target, first):
    rows, channels = taps_ref.shape
    count = target.shape[0] // LANES
    part = channels // (2 * count)
    for place in range(count):
        owner = order_of(ids_ref, first + place)
        block = jnp.zeros((rows, part), f32)
        for other in range(2 * count):
            block = block + jnp.where(
                owner == other, taps_ref[:, other * part : (other + 1) * part], 0.0
            )
        block = jnp.concatenate([jnp.zeros((rows, LANES - part), f32), block], 1)
        block = jnp.concatenate([block, jnp.zeros((16 - rows, LANES), f32)], 0)
        at = (slice(place * LANES, place * LANES + 16), slice(target.shape[1] - LANES, target.shape[1]))
        target[at] = (target[at].astype(f32) + block).astype(target.dtype)


def rows_to_blocks(ids_ref, value, send_ref, keep_ref):
    size = value.shape[0] // 4
    for k in range(4):
        target = send_ref if k % 2 else keep_ref
        half = (k // 2) * size
        for block in range(4):

            @pl.when((ids_ref[0] ^ k) == block)
            def _(block=block, half=half, target=target):
                target[half : half + size, :] = value[block * size : (block + 1) * size, :].astype(
                    target.dtype
                )


def mixer_forward(near, refs):
    (ids_ref, taps_in_ref, log_rates_ref, bias_ref), row_refs, mix_refs, outs, scratch = refs
    project_ref, rates_ref, out_ref, states_ref, carried_ref, inverse_ref = outs[:6]
    normed_ref, mix_ref, taps_ref = outs[6:]
    q_scr, kr_scr, p_scr, w_scr, u_scr = scratch
    length = normed_ref.shape[0]
    heads = states_ref.shape[1]
    key_width, value_width = states_ref.shape[2:]
    width = project_ref.shape[1] // heads
    chunks = length // CHUNK
    rows_in_time(ids_ref, row_refs, normed_ref)
    stack_rows(mix_refs, mix_ref, 0)
    if near:
        taps_ref[...] = taps_from_blocks(ids_ref, mix_ref, taps_in_ref.shape)
    else:
        taps_ref[...] = taps_in_ref[...]
    for head in range(heads):
        columns = slice(head * width, (head + 1) * width)
        project_ref[:, columns] = dot(normed_ref[...], mix_ref[:, columns])
    rates_ref[...] = dot(normed_ref[...], mix_ref[:, heads * width :])
    through = {}
    for chunk in range(chunks):
        start = chunk * CHUNK
        rows = slice(start, start + CHUNK)
        rates = rates_ref[rows, :]
        _, total = decays(rates, log_rates_ref[...], bias_ref[...])
        strength = sigmoid(rates)
        total_rows = jnp.transpose(total)
        for head in range(heads):
            t = chunk_terms(
                head, project_ref, taps_ref, start, total, total_rows, strength, key_width, value_width
            )
            inverse = unit_inverse(t["b"] * t["dots"])
            inverse_ref[chunk, head] = inverse
            side = jnp.concatenate([(t["b"] * t["since"]) * t["k"], t["b"] * t["v"]], 1)
            solved = mul(inverse, side)
            w_scr[chunk, head] = solved[:, :key_width].astype(bf16)
            u_scr[chunk, head] = solved[:, key_width:]
            q_scr[chunk, head] = (t["q"] * t["since"]).astype(bf16)
            kr_scr[chunk, head] = t["k"] * t["remaining"]
            p_scr[chunk, head] = t["scores"].astype(bf16)
            through[chunk, head] = t["through"]
    state = [jnp.zeros((key_width, value_width), f32) for _ in range(heads)]
    for chunk in range(chunks):
        rows = slice(chunk * CHUNK, (chunk + 1) * CHUNK)
        for head in range(heads):
            columns = slice(head * value_width, (head + 1) * value_width)
            states_ref[chunk, head] = state[head]
            low = state[head].astype(bf16)
            carried = u_scr[chunk, head] - mul(w_scr[chunk, head], low)
            carried_ref[rows, columns] = carried
            out_ref[rows, columns] = mul(q_scr[chunk, head], low) + mul(p_scr[chunk, head], carried)
            state[head] = through[chunk, head] * state[head] + mul(
                kr_scr[chunk, head], carried, (0, 0), exact=True
            )


def out_product(ids_ref, gain_ref, normed_ref, out_ref, *refs):
    weight_refs, (gated_ref, gate_ref, weights_ref, send_ref, keep_ref) = refs[:-5], refs[-5:]
    value_width = gain_ref.shape[1]
    values = out_ref.shape[1]
    stack_rows(weight_refs, weights_ref, 0)
    for head in range(values // value_width):
        columns = slice(head * value_width, (head + 1) * value_width)
        gate = dot(normed_ref[...], weights_ref[:, columns])
        gate_ref[:, columns] = gate
        out = out_ref[:, columns]
        scale = lax.rsqrt(row_sum(out * out) / value_width + NORM_EPS)
        gated_ref[:, columns] = (out * scale * gain_ref[...] * (gate * sigmoid(gate))).astype(bf16)
    rows_to_blocks(ids_ref, cols_dot(gated_ref[...], weights_ref[:, values:]), send_ref, keep_ref)


def gate_back(ids_ref, gain_ref, normed_ref, out_ref, gated_ref, gate_ref, weights_ref, *refs):
    row_refs, (rows_ref, grad_out_ref, grad_gate_ref, gain_grad_ref, send_ref) = refs[:-5], refs[-5:]
    value_width = gain_ref.shape[1]
    values = out_ref.shape[1]
    rows_in_time(ids_ref, row_refs, rows_ref)
    gain = gain_ref[...]
    gain_total = jnp.zeros((1, value_width), f32)
    for head in range(values // value_width):
        columns = slice(head * value_width, (head + 1) * value_width)
        grad = dot(rows_ref[...], weights_ref[:, values + head * value_width : values + (head + 1) * value_width])
        out, gate = out_ref[:, columns], gate_ref[:, columns]
        scale = lax.rsqrt(row_sum(out * out) / value_width + NORM_EPS)
        unit = out * scale
        sig = sigmoid(gate)
        act = gate * sig
        gain_total = gain_total + jnp.sum(grad * unit * act, axis=0, keepdims=True)
        grad_gate_ref[:, columns] = (
            grad * gain * unit * (sig * (1.0 + gate * (1.0 - sig)))
        ).astype(bf16)
        inner = grad * act * gain
        grad_out_ref[:, columns] = scale * (inner - unit * (row_sum(inner * unit) / value_width))
    gain_grad_ref[...] = gain_total
    half = normed_ref.shape[1] // 2
    send_ref[:, :values] = rows_dot(normed_ref[:, half:], grad_gate_ref[...], bf16)
    send_ref[:, values:] = rows_dot(rows_ref[:, half:], gated_ref[...], bf16)


def mixer_backward(near, refs):
    (ids_ref, log_rates_ref, bias_ref, grad_out_scr), kept, outs, scratch = refs
    (
        project_ref,
        rates_ref,
        out_ref,
        states_ref,
        carried_ref,
        inverse_ref,
        normed_ref,
        _,
        taps_ref,
    ) = kept
    grads_ref, grad_taps_ref, grad_lanes_ref, send_ref = outs
    back_scr, grad_carried_scr, q_scr, kr_scr, p_scr, w_scr, mixed_scr = scratch
    length = normed_ref.shape[0]
    heads = states_ref.shape[1]
    key_width, value_width = states_ref.shape[2:]
    width = channels = project_ref.shape[1] // heads
    chunks = length // CHUNK

    def gather_terms(chunk):
        start = chunk * CHUNK
        rates = rates_ref[start : start + CHUNK, :]
        _, total = decays(rates, log_rates_ref[...], bias_ref[...])
        strength = sigmoid(rates)
        total_rows = jnp.transpose(total)
        return [
            chunk_terms(
                head, project_ref, taps_ref, start, total, total_rows, strength, key_width, value_width
            )
            for head in range(heads)
        ]

    through = {}
    for chunk in range(chunks):
        rows = slice(chunk * CHUNK, (chunk + 1) * CHUNK)
        terms = gather_terms(chunk)
        for head in range(heads):
            columns = slice(head * value_width, (head + 1) * value_width)
            t = terms[head]
            w_scr[chunk, head] = mul(
                inverse_ref[chunk, head], (t["b"] * t["since"]) * t["k"]
            ).astype(bf16)
            q_scr[chunk, head] = (t["q"] * t["since"]).astype(bf16)
            kr_scr[chunk, head] = (t["k"] * t["remaining"]).astype(bf16)
            p_scr[chunk, head] = t["scores"].astype(bf16)
            through[chunk, head] = t["through"]

    back = [jnp.zeros((key_width, value_width), f32) for _ in range(heads)]
    for chunk in reversed(range(chunks)):
        rows = slice(chunk * CHUNK, (chunk + 1) * CHUNK)
        for head in range(heads):
            columns = slice(head * value_width, (head + 1) * value_width)
            back_scr[chunk, head] = back[head]
            grad_out = grad_out_scr[rows, columns].astype(bf16)
            grad_carried = mul(p_scr[chunk, head], grad_out, (0, 0)) + mul(
                kr_scr[chunk, head], back[head]
            )
            grad_carried_scr[rows, columns] = grad_carried
            back[head] = (
                through[chunk, head] * back[head]
                + mul(q_scr[chunk, head], grad_out, (0, 0))
                - mul(w_scr[chunk, head], grad_carried, (0, 0))
            )

    rows_at, cols_at = square_ids()
    lane = lax.broadcasted_iota(jnp.int32, (CHUNK, LANES), 1)
    place = lax.broadcasted_iota(jnp.int32, (CHUNK, LANES), 0)
    log_total = jnp.zeros((1, LANES), f32)
    bias_total = jnp.zeros((1, LANES), f32)
    for chunk in range(chunks):
        rows = slice(chunk * CHUNK, (chunk + 1) * CHUNK)
        terms = gather_terms(chunk)
        sums_grad = jnp.zeros((CHUNK, LANES), f32)
        strength_grad = jnp.zeros((CHUNK, LANES), f32)
        for head in range(heads):
            columns = slice(head * value_width, (head + 1) * value_width)
            t = terms[head]
            b, since, remaining, decay = t["b"], t["since"], t["remaining"], t["decay"]
            q, k, v = t["q"], t["k"], t["v"]
            state = states_ref[chunk, head]
            back_now = back_scr[chunk, head]
            carried = carried_ref[rows, columns]
            grad_out = grad_out_scr[rows, columns]
            grad_side = mul(inverse_ref[chunk, head], grad_carried_scr[rows, columns], (0, 0))
            strict = jnp.where(rows_at > cols_at, -mul(grad_side, carried, (1, 1)), 0.0)
            grad_scores = mul(grad_out, carried, (1, 1))
            side_state = mul(grad_side, state, (1, 1))
            out_state = since * mul(grad_out, state, (1, 1))
            carried_back = remaining * mul(carried, back_now, (1, 1))
            key_side = since * row_sum(k * side_state)
            strict_dots = strict * t["dots"]
            grad_strength = row_sum(grad_side * v) - key_side + row_sum(strict_dots)
            pulls = grad_scores * t["scores"] + b * strict_dots
            key_back = row_sum(k * carried_back)
            grad_sums = (
                row_sum(pulls - jnp.transpose(pulls))
                - b * key_side
                + row_sum(q * out_state)
                - key_back
            )
            final = jnp.sum(key_back, axis=0, keepdims=True) + t["through"] * jnp.sum(
                row_sum(back_now * state), axis=0, keepdims=True
            )
            scores_low = (grad_scores * decay).astype(bf16)
            strict_low = (strict * (b * decay)).astype(bf16)
            k_low, q_low = k.astype(bf16), q.astype(bf16)
            grad_q = out_state + mul(scores_low, k_low)
            grad_k = (
                carried_back
                - (b * since) * side_state
                + mul(scores_low, q_low, (0, 0))
                + mul(strict_low, k_low)
                + mul(strict_low, k_low, (0, 0))
            )
            grad_v = b * grad_side
            sums_grad = sums_grad + jnp.where(
                lane == 2 * head, grad_sums + jnp.where(place == CHUNK - 1, final, 0.0), 0.0
            )
            strength_grad = strength_grad + jnp.where(lane == 2 * head + 1, grad_strength, 0.0)
            grad_q = grad_q * key_width ** (-0.5)
            unit = t["unit_q"]
            grad_q = t["q_scale"] * (grad_q - unit * row_sum(grad_q * unit))
            grad_k = t["k_scale"] * (grad_k - k * row_sum(grad_k * k))
            at = head * channels
            for name, grad, size in (
                ("q", grad_q, key_width),
                ("k", grad_k, key_width),
                ("v", grad_v, value_width),
            ):
                pre, sig = t[name + "_slope"]
                mixed_scr[rows, at : at + size] = grad * (sig * (1.0 + pre * (1.0 - sig)))
                at += size
        step = 1
        while step < CHUNK:
            sums_grad = sums_grad + jnp.where(
                place < CHUNK - step, pltpu.roll(sums_grad, CHUNK - step, 0), 0.0
            )
            step *= 2
        rates = rates_ref[rows, :]
        log_decay, _ = decays(rates, log_rates_ref[...], bias_ref[...])
        strength = sigmoid(rates)
        inputs_grad = sums_grad * (-jnp.exp(log_rates_ref[...])) * sigmoid(rates + bias_ref[...])
        log_total = log_total + jnp.sum(sums_grad * log_decay, axis=0, keepdims=True)
        bias_total = bias_total + jnp.sum(inputs_grad, axis=0, keepdims=True)
        grads_ref[rows, heads * width :] = (
            inputs_grad + strength_grad * strength * (1.0 - strength)
        ).astype(bf16)
    grad_lanes_ref[0:1, :] = log_total
    grad_lanes_ref[1:2, :] = bias_total

    mixed_scr[length : length + 8, :] = jnp.zeros((8, mixed_scr.shape[1]), f32)
    for head in range(heads):
        columns = slice(head * channels, (head + 1) * channels)
        source = slice(head * width, head * width + channels)
        taps_here = [jnp.zeros((1, channels), f32) for _ in range(CONV)]
        for chunk in range(chunks):
            start = chunk * CHUNK
            total = None
            now = mixed_scr[start : start + CHUNK, columns]
            for tap in range(CONV):
                ahead = CONV - 1 - tap
                row = tap * heads + head
                term = taps_ref[row : row + 1, :] * (
                    mixed_scr[start + ahead : start + ahead + CHUNK, columns]
                )
                total = term if total is None else total + term
                taps_here[tap] = taps_here[tap] + jnp.sum(
                    now * shifted(project_ref, start, ahead, source), axis=0, keepdims=True
                )
            grads_ref[start : start + CHUNK, source] = total.astype(bf16)
        for tap in range(CONV):
            row = tap * heads + head
            grad_taps_ref[row : row + 1, :] = taps_here[tap]
    half = normed_ref.shape[1] // 2
    send_ref[...] = rows_dot(normed_ref[:, half:], grads_ref[...], bf16)
    if near:
        taps_to_blocks(ids_ref, grad_taps_ref, send_ref, half // LANES)


def fold_blocks(keep, got_ref, own_ref, low_refs):
    size = own_ref.shape[0]
    own_ref[...] = keep[0:size, :] + got_ref[0:size, :].astype(f32)
    for k, ref in enumerate(low_refs):
        here = slice((k + 1) * size, (k + 2) * size)
        ref[...] = (keep[here, :] + got_ref[here, :].astype(f32)).astype(bf16)


def mixer_products(near, refs):
    ids_ref, normed_ref, rows_ref, gated_ref, grads_ref, grad_gate_ref, mix_ref, weights_ref, grad_taps_ref = refs[:9]
    back_send_ref, back_keep_ref, mix_keep_ref = refs[10:13]
    values = grad_gate_ref.shape[1]
    half = normed_ref.shape[1] // 2
    gate_keep_ref = refs[-1]
    gate_keep_ref[:, :values] = rows_dot(normed_ref[:, :half], grad_gate_ref[...])
    gate_keep_ref[:, values:] = rows_dot(rows_ref[:, :half], gated_ref[...])
    if near:
        fold_blocks(gate_keep_ref, refs[9], refs[13], refs[14:-1])
    back = cols_dot(grads_ref[...], mix_ref[...])
    back = back + cols_dot(grad_gate_ref[...], weights_ref[:, :values])
    rows_to_blocks(ids_ref, back, back_send_ref, back_keep_ref)
    mix_keep_ref[...] = rows_dot(normed_ref[:, :half], grads_ref[...])
    if near:
        taps_to_blocks(ids_ref, grad_taps_ref, mix_keep_ref, 0)


def last_fold(keep_ref, got_ref, mix_keep_ref, mix_got_ref, keep_out_ref, send_ref, own_ref, *low_refs):
    fold(keep_ref, got_ref, keep_out_ref, send_ref)
    fold_blocks(mix_keep_ref, mix_got_ref, own_ref, low_refs)


def norm_scale(rows):
    return lax.rsqrt(jnp.mean(rows * rows, axis=1, keepdims=True) + NORM_EPS)


def prepare(ids_ref, rows_ref, grad_ref, mixer_gain_ref, ffn_gain_ref, resid_ref, both_ref, gains_ref):
    size = rows_ref.shape[0]
    count = rows_ref.shape[1] // LANES
    for place in range(count):
        at = pl.multiple_of(order_of(ids_ref, place) * LANES, LANES)
        here = slice(place * LANES, (place + 1) * LANES)
        resid_ref[:, here] = rows_ref[:, pl.ds(at, LANES)].astype(f32)
        both_ref[size:, here] = grad_ref[:, pl.ds(at, LANES)]
        gains_ref[0:1, here] = mixer_gain_ref[:, pl.ds(at, LANES)]
        gains_ref[1:2, here] = ffn_gain_ref[:, pl.ds(at, LANES)]
    resid = resid_ref[...]
    both_ref[0:size, :] = (resid * norm_scale(resid) * gains_ref[0:1, :]).astype(bf16)


def fold(keep_ref, got_ref, keep_out_ref, send_ref):
    size = send_ref.shape[0]
    keep_out_ref[...] = keep_ref[0:size, :] + got_ref[0:size, :].astype(f32)
    send_ref[...] = (keep_ref[size:, :] + got_ref[size:, :].astype(f32)).astype(bf16)


def middle_norm(keep_ref, got_ref, resid_in_ref, gains_ref, resid_ref, ffn_in_ref):
    resid = resid_in_ref[...] + keep_ref[...] + got_ref[...].astype(f32)
    resid_ref[...] = resid
    ffn_in_ref[...] = (resid * norm_scale(resid) * gains_ref[1:2, :]).astype(bf16)


def place_of(ids_ref, block, count):
    return ids_ref[1 + count + block]


def feed_forward(ids_ref, refs):
    ffn_refs, grad_refs, (weights_ref,), outs, (ffn_ref, top_ref, weights_scr) = refs
    ffn_out_ref, top_out_ref, hidden_ref, grad_gate_ref, out_send, out_keep, back_send, back_keep = outs
    size = ffn_refs[0].shape[0]
    count = ffn_ref.shape[1] // LANES
    for block in range(count):
        at = pl.multiple_of(order_of(ids_ref, block) * LANES, LANES)
        weights_scr[block * LANES : (block + 1) * LANES, :] = weights_ref[pl.ds(at, LANES), :]
    for k in range(4):
        ffn_ref[k * size : (k + 1) * size, :] = ffn_refs[k][...]
        top_ref[k * size : (k + 1) * size, :] = grad_refs[k][size:, :]
    hidden_size = hidden_ref.shape[1]
    gate_up_w = weights_scr[:, : 2 * hidden_size]
    down_w = weights_scr[:, 2 * hidden_size : 3 * hidden_size]
    gate_up = dot(ffn_ref[...], gate_up_w)
    grad_hidden = dot(top_ref[...], down_w)
    gate, up = gate_up[:, :hidden_size], gate_up[:, hidden_size:]
    sig = sigmoid(gate)
    act = gate * sig
    hidden_ref[...] = (act * up).astype(bf16)
    grad_gate_ref[:, :hidden_size] = (grad_hidden * up * (sig * (1.0 + gate * (1.0 - sig)))).astype(bf16)
    grad_gate_ref[:, hidden_size:] = (grad_hidden * act).astype(bf16)
    back = cols_dot(grad_gate_ref[...], gate_up_w)
    out = cols_dot(hidden_ref[...], down_w)
    for value, send, keep in ((back, back_send, back_keep), (out, out_send, out_keep)):
        for k in range(4):
            target = send if k % 2 else keep
            half = (k // 2) * size
            target[half : half + size, :] = value[k * size : (k + 1) * size, :].astype(target.dtype)
    for block in range(count):
        at = pl.multiple_of(place_of(ids_ref, block, count) * LANES, LANES)
        here = slice(block * LANES, (block + 1) * LANES)
        ffn_out_ref[:, here] = ffn_ref[:, pl.ds(at, LANES)]
        top_out_ref[:, here] = top_ref[:, pl.ds(at, LANES)]


def feed_products(ffn_ref, top_ref, hidden_ref, grad_gate_ref, out_ref):
    hidden_size = hidden_ref.shape[1]
    out_ref[:, : 2 * hidden_size] = rows_dot(ffn_ref[...], grad_gate_ref[...], out_ref.dtype)
    out_ref[:, 2 * hidden_size : 3 * hidden_size] = rows_dot(
        top_ref[...], hidden_ref[...], out_ref.dtype
    )
    rest = out_ref.shape[1] - 3 * hidden_size
    if rest:
        out_ref[:, 3 * hidden_size :] = jnp.zeros((out_ref.shape[0], rest), out_ref.dtype)


def norm_reverse(grad, rows, gain):
    scale = norm_scale(rows)
    unit = rows * scale
    inner = grad * gain
    gain_grad = jnp.sum(grad * unit, axis=0, keepdims=True)
    return scale * (inner - unit * jnp.mean(inner * unit, axis=1, keepdims=True)), gain_grad


def middle_back(
    back_keep_ref, back_got_ref, resid_ref, both_ref, gains_ref, grad_ref, low_ref, gain_grad_ref
):
    grad_ffn_in = back_keep_ref[...] + back_got_ref[...].astype(f32)
    grad, gain_grad = norm_reverse(grad_ffn_in, resid_ref[...], gains_ref[1:2, :])
    grad = grad + both_ref[both_ref.shape[0] // 2 :, :].astype(f32)
    grad_ref[...] = grad
    low_ref[...] = grad.astype(bf16)
    gain_grad_ref[...] = gain_grad


def last_out(ids_ref, keep_ref, got_ref, resid_ref, out_ref, scr):
    scr[...] = resid_ref[...] + keep_ref[...] + got_ref[...].astype(f32)
    count = out_ref.shape[1] // LANES
    for block in range(count):
        at = pl.multiple_of(place_of(ids_ref, block, count) * LANES, LANES)
        out_ref[:, block * LANES : (block + 1) * LANES] = scr[:, pl.ds(at, LANES)].astype(bf16)


def last_grad(
    ids_ref, keep_ref, got_ref, resid_in_ref, gains_ref, grad_ref, gain_grad_ref, out_ref, gains_out_ref, scr, gain_scr
):
    grad_normed = keep_ref[...] + got_ref[...].astype(f32)
    grad, gain_grad = norm_reverse(grad_normed, resid_in_ref[...], gains_ref[0:1, :])
    scr[...] = grad + grad_ref[...]
    gain_scr[0:1, :] = gain_grad
    gain_scr[1:2, :] = gain_grad_ref[...]
    count = out_ref.shape[1] // LANES
    for block in range(count):
        at = pl.multiple_of(place_of(ids_ref, block, count) * LANES, LANES)
        here = slice(block * LANES, (block + 1) * LANES)
        out_ref[:, here] = scr[:, pl.ds(at, LANES)]
        gains_out_ref[:, here] = gain_scr[:, pl.ds(at, LANES)]


def call(kernel, outs, operands, scratch=(), name=None, scalar=True):
    specs = [pl.BlockSpec(memory_space=pltpu.VMEM)] * len(operands)
    if scalar:
        specs[0] = pl.BlockSpec(memory_space=pltpu.SMEM)
    return pl.pallas_call(
        kernel,
        out_shape=tuple(jax.ShapeDtypeStruct(shape, kind) for shape, kind in outs),
        in_specs=specs,
        out_specs=tuple([pl.BlockSpec(memory_space=pltpu.VMEM)] * len(outs)),
        scratch_shapes=[pltpu.VMEM(shape, kind) for shape, kind in scratch],
        compiler_params=pltpu.CompilerParams(vmem_limit_bytes=56 * 2**20),
        name=name,
    )(*operands)


def cut_list(items, sizes):
    parts, at = [], 0
    for size in sizes:
        parts.append(items[at : at + size])
        at += size
    return parts


def run_forward(near, ids, rows, mix, taps, log_rates, bias, value_width):
    length = rows[0].shape[0] // 2 * len(rows)
    model = rows[0].shape[1]
    wide = mix[0].shape[1]
    columns = wide - LANES
    channels = taps.shape[1]
    heads = taps.shape[0] // CONV
    key_width = (channels - value_width) // 2
    pair = (length // CHUNK, heads)
    values = heads * value_width

    def kernel(*refs):
        mixer_forward(near, cut_list(refs, (4, len(rows), len(mix), 9, 5)))

    return call(
        kernel,
        (
            ((length, columns), f32),
            ((length, LANES), f32),
            ((length, values), f32),
            (pair + (key_width, value_width), f32),
            ((length, values), f32),
            (pair + (CHUNK, CHUNK), f32),
            ((length, model), bf16),
            ((model, wide), bf16),
            (taps.shape, f32),
        ),
        (ids, taps, log_rates, bias, *rows, *mix),
        (
            (pair + (CHUNK, key_width), bf16),
            (pair + (CHUNK, key_width), f32),
            (pair + (CHUNK, CHUNK), bf16),
            (pair + (CHUNK, key_width), bf16),
            (pair + (CHUNK, value_width), f32),
        ),
        "mixer_forward",
    )


def run_backward(near, ids, grad_out, log_rates, bias, kept):
    project, _, out, states, _, _, normed, mix, taps = kept
    length, model = normed.shape
    values = out.shape[1]
    wide = mix.shape[1]
    heads, key_width, value_width = states.shape[1:]
    pair = (length // CHUNK, heads)

    def kernel(*refs):
        mixer_backward(near, cut_list(refs, (4, len(kept), 4, 7)))

    return call(
        kernel,
        (
            ((length, wide), bf16),
            (taps.shape, f32),
            ((2, LANES), f32),
            ((model // 2, wide), bf16),
        ),
        (ids, log_rates, bias, grad_out, *kept),
        (
            (pair + (key_width, value_width), f32),
            ((length, values), f32),
            (pair + (CHUNK, key_width), bf16),
            (pair + (CHUNK, key_width), bf16),
            (pair + (CHUNK, CHUNK), bf16),
            (pair + (CHUNK, key_width), bf16),
            ((length + 8, heads * taps.shape[1]), f32),
        ),
        "mixer_backward",
    )


def swap(array, axis, size, offset):
    return lax.ppermute(array, axis, [(i, i ^ offset) for i in range(size)])


def after(arrays, others):
    kept, _ = lax.optimization_barrier((arrays, others))
    return kept


def per_device(
    layer_in,
    mixer_gain,
    w_mix,
    w_rates,
    conv_taps,
    a_log,
    dt_bias,
    head_gain,
    w_out,
    ffn_gain,
    w_gate_up,
    w_down,
    out_grad,
):
    size = lax.axis_size("dp")
    ranks = lax.axis_size("tensor")
    depth, heads, width = w_mix.shape
    model = layer_in.shape[1]
    hidden = w_gate_up.shape[2]
    value_size = w_out.shape[0]
    rows = layer_in.shape[0]
    taps_shape = conv_taps.shape
    part = taps_shape[2]
    near = size == 8 and depth == LANES and 2 * part == LANES
    half = size // 2
    rank, own = lax.axis_index("tensor"), lax.axis_index("dp")
    blocks = model // LANES
    if near:
        offsets = [2 * p for p in range(half)] + [2 * p + 1 for p in range(half)]
        order = own ^ jnp.array(offsets, jnp.int32)
        places = [offsets.index(k) for k in range(size)]
        index = own ^ jnp.arange(size, dtype=jnp.int32)
        place = jnp.where(index % 2 == 0, index // 2, half + index // 2)
        assert places == [k // 2 if k % 2 == 0 else half + k // 2 for k in range(size)]
    else:
        order = place = jnp.arange(blocks, dtype=jnp.int32)
    ids = jnp.concatenate([jnp.full((1,), rank, jnp.int32), order, place])

    def near_z(shard):
        return [shard] + [swap(shard, "dp", size, 2 * p) for p in range(1, half)]

    def near_x(shards, own_side):
        return [own_side, swap(jnp.concatenate(shards[1:], 0), "dp", size, 1)]

    def far(shard):
        return lax.all_gather(shard, "dp", axis=0, tiled=True)

    def rows_y(block):
        return swap(block, "tensor", ranks, 2)

    def rows_core(block):
        return swap(block, "tensor", ranks, 1)

    def gather_rows(block):
        across = rows_y(block)
        return [block, rows_core(block), across, rows_core(across)]

    def sum_rows(send, keep, name):
        got = rows_core(send)
        shape = (rows, model)
        keep, send = call(fold, ((shape, f32), (shape, bf16)), (keep, got), name=name, scalar=False)
        return keep, rows_y(send)

    channels = width - head_gain.shape[0]
    values = value_size
    rates_tile = jnp.pad(w_rates.reshape(depth, 2 * heads), ((0, 0), (0, LANES - 2 * heads)))
    if near:
        taps_tile = conv_taps.reshape(CONV * heads, part)
        taps_tile = jnp.pad(taps_tile, ((0, depth - CONV * heads), (LANES - part, 0)))
        rates_tile = rates_tile + taps_tile
    mix_shard = jnp.concatenate(
        [w_mix[:, :, :channels].reshape(depth, heads * channels), rates_tile], 1
    )
    gate_shard = jnp.concatenate([w_mix[:, :, channels:].reshape(depth, values), w_out.T], 1)
    filler = -3 * hidden % LANES
    ffn_shard = jnp.concatenate(
        [w_gate_up.reshape(depth, 2 * hidden), w_down.T, jnp.zeros((depth, filler), bf16)], 1
    )

    if near:
        mix_z = near_z(mix_shard)
        mix_side = swap(mix_shard, "dp", size, 1)
    square = (rows, model)
    resid_in, both, gains = call(
        prepare,
        ((square, f32), ((2 * rows, model), bf16), ((2, model), f32)),
        (ids, layer_in, out_grad, mixer_gain.reshape(1, -1), ffn_gain.reshape(1, -1)),
        name="prepare",
    )
    ffn_full = far(after(ffn_shard, (mix_z, mix_side)) if near else ffn_shard)
    both_all = gather_rows(both)
    if near:
        gate_shard = after(gate_shard, (mix_z, mix_side))
        gate_z = near_z(gate_shard)
        gate_side = swap(gate_shard, "dp", size, 1)
        mix_slots = mix_z + near_x(mix_z, mix_side)
        taps = jnp.zeros((CONV * heads, part * size), f32)
    else:
        mix_slots = [far(mix_shard)]
        gate_slots = [far(gate_shard)]
        taps = lax.all_gather(conv_taps, "dp", axis=2, tiled=True).astype(f32)
        taps = taps.reshape(CONV * heads, part * size)

    first_head = rank * heads

    def on_lanes(per_head):
        here = lax.dynamic_slice_in_dim(per_head, first_head, heads)
        pairs = jnp.stack([here, jnp.zeros_like(here)], 1).reshape(1, -1)
        return jnp.pad(pairs, ((0, 0), (0, LANES - pairs.shape[1])))

    def off_lanes(row):
        here = row[: 2 * heads : 2]
        return lax.dynamic_update_slice_in_dim(jnp.zeros_like(a_log), here, first_head, 0)

    lanes = (on_lanes(a_log), on_lanes(dt_bias))
    gain_row = head_gain.reshape(1, -1)
    kept = run_forward(near, ids, both_all, mix_slots, taps, *lanes, head_gain.shape[0])
    heads_out, normed_rows, mix_full = kept[2], kept[6], kept[7]
    if near:
        gate_slots = gate_z + near_x(gate_z, gate_side)
    tokens = rows * ranks
    block_pair = (2 * rows, model)
    gated, gate, gate_full, out_send, out_keep = call(
        out_product,
        (
            ((tokens, values), bf16),
            ((tokens, values), f32),
            ((model, 2 * values), bf16),
            (block_pair, bf16),
            (block_pair, f32),
        ),
        (ids, gain_row, normed_rows, heads_out, *gate_slots),
        (),
        "out_product",
    )
    out_keep, out_got = sum_rows(out_send, out_keep, "out_fold")
    resid, ffn_in = call(
        middle_norm, ((square, f32), (square, bf16)), (out_keep, out_got, resid_in, gains), name="middle_norm", scalar=False
    )
    ffn_all = gather_rows(ffn_in)

    def ffn_kernel(ids_ref, *refs):
        feed_forward(ids_ref, cut_list(refs, (4, 4, 1, 8, 3)))

    ffn_rows, top_rows, hidden_low, grad_gate, ffn_send, ffn_keep, back_send, back_keep = call(
        ffn_kernel,
        (
            ((tokens, model), bf16),
            ((tokens, model), bf16),
            ((tokens, hidden), bf16),
            ((tokens, 2 * hidden), bf16),
            (block_pair, bf16),
            (block_pair, f32),
            (block_pair, bf16),
            (block_pair, f32),
        ),
        (ids, *ffn_all, *both_all, ffn_full),
        (((tokens, model), bf16), ((tokens, model), bf16), (ffn_full.shape, bf16)),
        "feed_forward",
    )
    split = model // 2

    def scatter_x(send):
        return swap(send, "dp", size, 1) if near else send

    back_keep, back_got = sum_rows(back_send, back_keep, "back_fold")
    (ffn_grads,) = call(
        feed_products,
        (((model, 3 * hidden + filler), bf16 if near else f32),),
        (ffn_rows, top_rows, hidden_low, grad_gate),
        name="feed_products",
        scalar=False,
    )
    ffn_total = lax.psum_scatter(ffn_grads, "dp", scatter_dimension=0, tiled=True).astype(f32)
    grad_resid, mix_low, ffn_gain_grad = call(
        middle_back,
        ((square, f32), (square, bf16), ((1, model), f32)),
        (back_keep, back_got, resid, both, gains),
        name="middle_back",
        scalar=False,
    )
    mix_all = gather_rows(mix_low)
    ffn_keep, ffn_got = sum_rows(ffn_send, ffn_keep, "ffn_fold")
    (layer_out,) = call(
        last_out, ((square, bf16),), (ids, ffn_keep, ffn_got, resid), ((square, f32),), "last_out"
    )
    grad_rows, grad_out, gate_grad, head_gain_grad, gate_send = call(
        gate_back,
        (
            ((tokens, model), bf16),
            ((tokens, values), f32),
            ((tokens, values), bf16),
            (gain_row.shape, f32),
            ((split, 2 * values), bf16),
        ),
        (ids, gain_row, normed_rows, heads_out, gated, gate, gate_full, *mix_all),
        (),
        "gate_back",
    )
    gate_got = scatter_x(gate_send)
    grads, taps_grad, lanes_grad, mix_send = run_backward(near, ids, grad_out, *lanes, kept)
    mix_got = scatter_x(mix_send)

    def products_kernel(*refs):
        mixer_products(near, refs)

    def blocks_of(send):
        return (((depth, send.shape[1]), f32),) + (((depth, send.shape[1]), bf16),) * (half - 1)

    keep_shape = ((split, 2 * values), f32)
    norm_send, norm_keep, mix_keep, *gate_parts = call(
        products_kernel,
        ((block_pair, bf16), (block_pair, f32), (mix_send.shape, f32))
        + (blocks_of(gate_send) if near else (keep_shape,)),
        (ids, normed_rows, grad_rows, gated, grads, gate_grad, mix_full, gate_full, taps_grad, gate_got),
        (keep_shape,) if near else (),
        "mixer_products",
    )

    def far_sum(parts, got):
        if near:
            own, lows = parts[0], parts[1:]
            return [own] + [swap(low, "dp", size, 2 * (p + 1)) for p, low in enumerate(lows)]
        return [
            lax.psum_scatter(
                jnp.concatenate([parts[0], got.astype(f32)], 0), "dp", scatter_dimension=0, tiled=True
            )
        ]

    def add_up(blocks):
        total = blocks[0]
        for block in blocks[1:]:
            total = total + block.astype(f32)
        return total

    gate_blocks = far_sum(gate_parts, gate_got)
    norm_got = rows_core(norm_send)
    norm_keep, norm_send, *mix_parts = call(
        last_fold if near else fold,
        ((square, f32), (square, bf16)) + (blocks_of(mix_send) if near else ()),
        (norm_keep, norm_got) + ((mix_keep, mix_got) if near else ()),
        name="last_fold",
        scalar=False,
    )
    mix_blocks = far_sum(mix_parts if near else [mix_keep], mix_got)
    norm_got = rows_y(norm_send)
    in_grad, gains_grad = call(
        last_grad,
        ((square, f32), ((2, model), f32)),
        (ids, norm_keep, norm_got, resid_in, gains, grad_resid, ffn_gain_grad),
        ((square, f32), ((2, model), f32)),
        "last_grad",
    )

    small = jnp.concatenate(
        [
            gains_grad.reshape(-1),
            head_gain_grad.reshape(-1),
            off_lanes(lanes_grad[0]),
            off_lanes(lanes_grad[1]),
        ]
    )
    length = small.size
    small = jnp.pad(small, (0, -length % (8 * LANES))).reshape(8, -1)
    for offset in (1, 2):
        small = small + swap(small, "tensor", ranks, offset)
    if near:
        for offset in (1, 2, 4):
            small = small + swap(small, "dp", size, offset)
    else:
        small = lax.psum(small, "dp")
    small = small.reshape(-1)[:length]
    grad_mixer_gain, grad_ffn_gain = small[:model], small[model : 2 * model]
    small = small[2 * model :]
    grad_head_gain, small = small[: head_gain.size], small[head_gain.size :]
    grad_a_log, grad_dt_bias = small[: a_log.size], small[a_log.size :]

    gate_total = add_up(gate_blocks)
    mix_total = add_up(mix_blocks)
    grad_w_mix = jnp.concatenate(
        [
            mix_total[:, : heads * channels].reshape(depth, heads, channels),
            gate_total[:, :values].reshape(depth, heads, -1),
        ],
        2,
    )
    grad_w_rates = mix_total[:, heads * channels : heads * channels + 2 * heads].reshape(w_rates.shape)
    if near:
        grad_taps = mix_total[: CONV * heads, mix_total.shape[1] - part :].reshape(taps_shape)
    else:
        grad_taps = lax.psum_scatter(
            taps_grad.reshape(CONV, heads, -1), "dp", scatter_dimension=2, tiled=True
        )
    return (
        layer_out,
        in_grad,
        grad_mixer_gain,
        grad_w_mix,
        grad_w_rates,
        grad_taps,
        grad_a_log,
        grad_dt_bias,
        grad_head_gain,
        gate_total[:, values:].T,
        grad_ffn_gain,
        ffn_total[:, : 2 * hidden].reshape(w_gate_up.shape),
        ffn_total[:, 2 * hidden : 3 * hidden].T,
    )


def solution(mesh):
    return jax.shard_map(
        per_device,
        mesh=mesh,
        in_specs=(
            P(("dp", "tensor"), None),
            P(),
            P("dp", "tensor", None),
            P("dp", "tensor", None),
            P(None, "tensor", "dp"),
            P(),
            P(),
            P(),
            P("tensor", "dp"),
            P(),
            P("dp", None, "tensor"),
            P("tensor", "dp"),
            P(("dp", "tensor"), None),
        ),
        out_specs=(
            P(("dp", "tensor"), None),
            P(("dp", "tensor"), None),
            P(),
            P("dp", "tensor", None),
            P("dp", "tensor", None),
            P(None, "tensor", "dp"),
            P(),
            P(),
            P(),
            P("tensor", "dp"),
            P(),
            P("dp", None, "tensor"),
            P("tensor", "dp"),
        ),
        check_vma=False,
    )
```

```python
import jax
import jax.numpy as jnp
from jax import lax
from jax.experimental import pallas as pl
from jax.experimental.pallas import tpu as pltpu
from jax.sharding import PartitionSpec as P

CONV = 4


highest = lax.Precision.HIGHEST
NORM_EPS = 1e-05
UNIT_EPS = 1e-06
bf16 = jnp.bfloat16
f32 = jnp.float32


def rows_dot(left, right, kind=f32):
    return lax.dot_general(
        left, right, (((0,), (0,)), ((), ())), preferred_element_type=f32
    ).astype(kind)


def cols_dot(left, right):
    return lax.dot_general(left, right, (((1,), (1,)), ((), ())), preferred_element_type=f32)


def dot(left, right):
    return jnp.dot(left, right, preferred_element_type=f32)


CHUNK = 128
LANES = 128


def mul(left, right, over=(1, 0), exact=False):
    dims = (((over[0],), (over[1],)), ((), ()))
    if exact:
        return lax.dot_general(left, right, dims, precision=highest, preferred_element_type=f32)
    return lax.dot_general(left.astype(bf16), right.astype(bf16), dims, preferred_element_type=f32)


def square_ids():
    shape = (CHUNK, CHUNK)
    return lax.broadcasted_iota(jnp.int32, shape, 0), lax.broadcasted_iota(jnp.int32, shape, 1)


def sigmoid(v):
    return 1.0 / (1.0 + jnp.exp(-v))


def softplus(v):
    return jnp.maximum(v, 0.0) + jnp.log1p(jnp.exp(-jnp.abs(v)))


def row_sum(v):
    return jnp.sum(v, axis=1, keepdims=True)


def unit_inverse(lower):
    rows, cols = square_ids()
    inverse = jnp.where(rows == cols, 1.0, 0.0)
    block = 1
    while block < CHUNK:
        corner = (
            (rows // (2 * block) == cols // (2 * block))
            & ((rows // block) % 2 == 1)
            & ((cols // block) % 2 == 0)
        )
        part = jnp.where(corner, lower, 0.0)
        if block == 1:
            inverse = inverse - part
        else:
            inverse = inverse - mul(mul(inverse, part), inverse)
        block *= 2
    return inverse


def shifted(ref, start, back, columns):
    if start == 0 and back:
        rows = lax.broadcasted_iota(jnp.int32, (CHUNK, columns.stop - columns.start), 0)
        return jnp.where(rows >= back, pltpu.roll(ref[0:CHUNK, columns], back, 0), 0.0)
    return ref[start - back : start - back + CHUNK, columns]


def short_conv(project_ref, taps_ref, start, head, heads, columns, tap_columns):
    total = None
    for tap in range(CONV):
        row = tap * heads + head
        term = taps_ref[row : row + 1, tap_columns] * shifted(
            project_ref, start, CONV - 1 - tap, columns
        )
        total = term if total is None else total + term
    return total


def decays(rates, log_rates, bias):
    log_decay = -jnp.exp(log_rates) * softplus(rates + bias)
    place = lax.broadcasted_iota(jnp.int32, rates.shape, 0)
    total = log_decay
    step = 1
    while step < CHUNK:
        total = total + jnp.where(place >= step, pltpu.roll(total, step, 0), 0.0)
        step *= 2
    return log_decay, total


def chunk_terms(head, project_ref, taps_ref, start, total, total_rows, strength, key_width, value_width):
    width = 2 * key_width + value_width
    base = head * width
    heads = project_ref.shape[1] // width
    terms = {}
    parts = (("q", 0, key_width), ("k", key_width, key_width), ("v", 2 * key_width, value_width))
    for name, at, size in parts:
        pre = short_conv(
            project_ref,
            taps_ref,
            start,
            head,
            heads,
            slice(base + at, base + at + size),
            slice(at, at + size),
        )
        gate = sigmoid(pre)
        mixed = pre * gate
        if name != "v":
            scale = lax.rsqrt(row_sum(mixed * mixed) + UNIT_EPS)
            mixed = mixed * scale
            terms[name + "_scale"] = scale
        terms[name + "_slope"] = (pre, gate)
        terms[name] = mixed
    terms["unit_q"] = terms["q"]
    terms["q"] = terms["q"] * key_width ** (-0.5)
    lane = 2 * head
    sums = total[:, lane : lane + 1]
    across = total_rows[lane : lane + 1, :]
    rows, cols = square_ids()
    decay = jnp.where(rows >= cols, jnp.exp(jnp.minimum(sums - across, 0.0)), 0.0)
    final = total[CHUNK - 1 : CHUNK, lane : lane + 1]
    terms["b"] = strength[:, lane + 1 : lane + 2]
    terms["since"] = jnp.exp(sums)
    terms["remaining"] = jnp.exp(final - sums)
    terms["through"] = jnp.exp(final)
    terms["decay"] = decay
    terms["dots"] = mul(terms["k"], terms["k"], (1, 1)) * jnp.where(rows > cols, decay, 0.0)
    terms["scores"] = mul(terms["q"], terms["k"], (1, 1)) * decay
    return terms


def stack_rows(refs, target, column):
    at = 0
    for ref in refs:
        rows = ref.shape[0]
        columns = min(ref.shape[1], target.shape[1] - column)
        target[at : at + rows, column : column + columns] = ref[:, :columns]
        at += rows


def rows_in_time(ids_ref, refs, target):
    size = target.shape[0] // len(refs)
    for k, ref in enumerate(refs):
        at = pl.multiple_of((ids_ref[0] ^ k) * size, size)
        target[pl.ds(at, size), :] = ref[0:size, :]


def order_of(ids_ref, place):
    return ids_ref[1 + place]


def taps_from_blocks(ids_ref, mix_ref, shape):
    rows, channels = shape
    count = mix_ref.shape[0] // LANES
    part = channels // count
    lane = lax.broadcasted_iota(jnp.int32, shape, 1)
    total = jnp.zeros(shape, f32)
    for place in range(count):
        block = mix_ref[place * LANES : place * LANES + 16, mix_ref.shape[1] - LANES :]
        block = block.astype(f32)[0:rows, LANES - part :]
        wide = jnp.concatenate([block] * count, 1)
        total = total + jnp.where(lane // part == order_of(ids_ref, place), wide, 0.0)
    return total


def taps_to_blocks(ids_ref, taps_ref, target, first):
    rows, channels = taps_ref.shape
    count = target.shape[0] // LANES
    part = channels // (2 * count)
    for place in range(count):
        owner = order_of(ids_ref, first + place)
        block = jnp.zeros((rows, part), f32)
        for other in range(2 * count):
            block = block + jnp.where(
                owner == other, taps_ref[:, other * part : (other + 1) * part], 0.0
            )
        block = jnp.concatenate([jnp.zeros((rows, LANES - part), f32), block], 1)
        block = jnp.concatenate([block, jnp.zeros((16 - rows, LANES), f32)], 0)
        at = (slice(place * LANES, place * LANES + 16), slice(target.shape[1] - LANES, target.shape[1]))
        target[at] = (target[at].astype(f32) + block).astype(target.dtype)


def rows_to_blocks(ids_ref, value, send_ref, keep_ref):
    size = value.shape[0] // 4
    for k in range(4):
        target = send_ref if k % 2 else keep_ref
        half = (k // 2) * size
        for block in range(4):

            @pl.when((ids_ref[0] ^ k) == block)
            def _(block=block, half=half, target=target):
                target[half : half + size, :] = value[block * size : (block + 1) * size, :].astype(
                    target.dtype
                )


def mixer_forward(near, refs):
    (ids_ref, taps_in_ref, log_rates_ref, bias_ref), row_refs, mix_refs, outs, scratch = refs
    project_ref, rates_ref, out_ref, states_ref, carried_ref, inverse_ref = outs[:6]
    normed_ref, mix_ref, taps_ref = outs[6:]
    q_scr, kr_scr, p_scr, w_scr, u_scr = scratch
    length = normed_ref.shape[0]
    heads = states_ref.shape[1]
    key_width, value_width = states_ref.shape[2:]
    width = project_ref.shape[1] // heads
    chunks = length // CHUNK
    rows_in_time(ids_ref, row_refs, normed_ref)
    stack_rows(mix_refs, mix_ref, 0)
    if near:
        taps_ref[...] = taps_from_blocks(ids_ref, mix_ref, taps_in_ref.shape)
    else:
        taps_ref[...] = taps_in_ref[...]
    for head in range(heads):
        columns = slice(head * width, (head + 1) * width)
        project_ref[:, columns] = dot(normed_ref[...], mix_ref[:, columns])
    rates_ref[...] = dot(normed_ref[...], mix_ref[:, heads * width :])
    through = {}
    for chunk in range(chunks):
        start = chunk * CHUNK
        rows = slice(start, start + CHUNK)
        rates = rates_ref[rows, :]
        _, total = decays(rates, log_rates_ref[...], bias_ref[...])
        strength = sigmoid(rates)
        total_rows = jnp.transpose(total)
        for head in range(heads):
            t = chunk_terms(
                head, project_ref, taps_ref, start, total, total_rows, strength, key_width, value_width
            )
            inverse = unit_inverse(t["b"] * t["dots"])
            inverse_ref[chunk, head] = inverse
            side = jnp.concatenate([(t["b"] * t["since"]) * t["k"], t["b"] * t["v"]], 1)
            solved = mul(inverse, side)
            w_scr[chunk, head] = solved[:, :key_width].astype(bf16)
            u_scr[chunk, head] = solved[:, key_width:]
            q_scr[chunk, head] = (t["q"] * t["since"]).astype(bf16)
            kr_scr[chunk, head] = t["k"] * t["remaining"]
            p_scr[chunk, head] = t["scores"].astype(bf16)
            through[chunk, head] = t["through"]
    state = [jnp.zeros((key_width, value_width), f32) for _ in range(heads)]
    for chunk in range(chunks):
        rows = slice(chunk * CHUNK, (chunk + 1) * CHUNK)
        for head in range(heads):
            columns = slice(head * value_width, (head + 1) * value_width)
            states_ref[chunk, head] = state[head]
            low = state[head].astype(bf16)
            carried = u_scr[chunk, head] - mul(w_scr[chunk, head], low)
            carried_ref[rows, columns] = carried
            out_ref[rows, columns] = mul(q_scr[chunk, head], low) + mul(p_scr[chunk, head], carried)
            state[head] = through[chunk, head] * state[head] + mul(
                kr_scr[chunk, head], carried, (0, 0), exact=True
            )


def out_product(ids_ref, gain_ref, normed_ref, out_ref, *refs):
    weight_refs, (gated_ref, gate_ref, weights_ref, send_ref, keep_ref) = refs[:-5], refs[-5:]
    value_width = gain_ref.shape[1]
    values = out_ref.shape[1]
    stack_rows(weight_refs, weights_ref, 0)
    for head in range(values // value_width):
        columns = slice(head * value_width, (head + 1) * value_width)
        gate = dot(normed_ref[...], weights_ref[:, columns])
        gate_ref[:, columns] = gate
        out = out_ref[:, columns]
        scale = lax.rsqrt(row_sum(out * out) / value_width + NORM_EPS)
        gated_ref[:, columns] = (out * scale * gain_ref[...] * (gate * sigmoid(gate))).astype(bf16)
    rows_to_blocks(ids_ref, cols_dot(gated_ref[...], weights_ref[:, values:]), send_ref, keep_ref)


def gate_back(ids_ref, gain_ref, normed_ref, out_ref, gated_ref, gate_ref, weights_ref, *refs):
    row_refs, (rows_ref, grad_out_ref, grad_gate_ref, gain_grad_ref, send_ref) = refs[:-5], refs[-5:]
    value_width = gain_ref.shape[1]
    values = out_ref.shape[1]
    rows_in_time(ids_ref, row_refs, rows_ref)
    gain = gain_ref[...]
    gain_total = jnp.zeros((1, value_width), f32)
    for head in range(values // value_width):
        columns = slice(head * value_width, (head + 1) * value_width)
        grad = dot(rows_ref[...], weights_ref[:, values + head * value_width : values + (head + 1) * value_width])
        out, gate = out_ref[:, columns], gate_ref[:, columns]
        scale = lax.rsqrt(row_sum(out * out) / value_width + NORM_EPS)
        unit = out * scale
        sig = sigmoid(gate)
        act = gate * sig
        gain_total = gain_total + jnp.sum(grad * unit * act, axis=0, keepdims=True)
        grad_gate_ref[:, columns] = (
            grad * gain * unit * (sig * (1.0 + gate * (1.0 - sig)))
        ).astype(bf16)
        inner = grad * act * gain
        grad_out_ref[:, columns] = scale * (inner - unit * (row_sum(inner * unit) / value_width))
    gain_grad_ref[...] = gain_total
    half = normed_ref.shape[1] // 2
    send_ref[:, :values] = rows_dot(normed_ref[:, half:], grad_gate_ref[...], bf16)
    send_ref[:, values:] = rows_dot(rows_ref[:, half:], gated_ref[...], bf16)


def mixer_backward(near, refs):
    (ids_ref, log_rates_ref, bias_ref, grad_out_scr), kept, outs, scratch = refs
    (
        project_ref,
        rates_ref,
        out_ref,
        states_ref,
        carried_ref,
        inverse_ref,
        normed_ref,
        _,
        taps_ref,
    ) = kept
    grads_ref, grad_taps_ref, grad_lanes_ref, send_ref = outs
    back_scr, grad_carried_scr, q_scr, kr_scr, p_scr, w_scr, mixed_scr = scratch
    length = normed_ref.shape[0]
    heads = states_ref.shape[1]
    key_width, value_width = states_ref.shape[2:]
    width = channels = project_ref.shape[1] // heads
    chunks = length // CHUNK

    def gather_terms(chunk):
        start = chunk * CHUNK
        rates = rates_ref[start : start + CHUNK, :]
        _, total = decays(rates, log_rates_ref[...], bias_ref[...])
        strength = sigmoid(rates)
        total_rows = jnp.transpose(total)
        return [
            chunk_terms(
                head, project_ref, taps_ref, start, total, total_rows, strength, key_width, value_width
            )
            for head in range(heads)
        ]

    through = {}
    for chunk in range(chunks):
        rows = slice(chunk * CHUNK, (chunk + 1) * CHUNK)
        terms = gather_terms(chunk)
        for head in range(heads):
            columns = slice(head * value_width, (head + 1) * value_width)
            t = terms[head]
            w_scr[chunk, head] = mul(
                inverse_ref[chunk, head], (t["b"] * t["since"]) * t["k"]
            ).astype(bf16)
            q_scr[chunk, head] = (t["q"] * t["since"]).astype(bf16)
            kr_scr[chunk, head] = (t["k"] * t["remaining"]).astype(bf16)
            p_scr[chunk, head] = t["scores"].astype(bf16)
            through[chunk, head] = t["through"]

    back = [jnp.zeros((key_width, value_width), f32) for _ in range(heads)]
    for chunk in reversed(range(chunks)):
        rows = slice(chunk * CHUNK, (chunk + 1) * CHUNK)
        for head in range(heads):
            columns = slice(head * value_width, (head + 1) * value_width)
            back_scr[chunk, head] = back[head]
            grad_out = grad_out_scr[rows, columns].astype(bf16)
            grad_carried = mul(p_scr[chunk, head], grad_out, (0, 0)) + mul(
                kr_scr[chunk, head], back[head]
            )
            grad_carried_scr[rows, columns] = grad_carried
            back[head] = (
                through[chunk, head] * back[head]
                + mul(q_scr[chunk, head], grad_out, (0, 0))
                - mul(w_scr[chunk, head], grad_carried, (0, 0))
            )

    rows_at, cols_at = square_ids()
    lane = lax.broadcasted_iota(jnp.int32, (CHUNK, LANES), 1)
    place = lax.broadcasted_iota(jnp.int32, (CHUNK, LANES), 0)
    log_total = jnp.zeros((1, LANES), f32)
    bias_total = jnp.zeros((1, LANES), f32)
    for chunk in range(chunks):
        rows = slice(chunk * CHUNK, (chunk + 1) * CHUNK)
        terms = gather_terms(chunk)
        sums_grad = jnp.zeros((CHUNK, LANES), f32)
        strength_grad = jnp.zeros((CHUNK, LANES), f32)
        for head in range(heads):
            columns = slice(head * value_width, (head + 1) * value_width)
            t = terms[head]
            b, since, remaining, decay = t["b"], t["since"], t["remaining"], t["decay"]
            q, k, v = t["q"], t["k"], t["v"]
            state = states_ref[chunk, head]
            back_now = back_scr[chunk, head]
            carried = carried_ref[rows, columns]
            grad_out = grad_out_scr[rows, columns]
            grad_side = mul(inverse_ref[chunk, head], grad_carried_scr[rows, columns], (0, 0))
            strict = jnp.where(rows_at > cols_at, -mul(grad_side, carried, (1, 1)), 0.0)
            grad_scores = mul(grad_out, carried, (1, 1))
            side_state = mul(grad_side, state, (1, 1))
            out_state = since * mul(grad_out, state, (1, 1))
            carried_back = remaining * mul(carried, back_now, (1, 1))
            key_side = since * row_sum(k * side_state)
            strict_dots = strict * t["dots"]
            grad_strength = row_sum(grad_side * v) - key_side + row_sum(strict_dots)
            pulls = grad_scores * t["scores"] + b * strict_dots
            key_back = row_sum(k * carried_back)
            grad_sums = (
                row_sum(pulls - jnp.transpose(pulls))
                - b * key_side
                + row_sum(q * out_state)
                - key_back
            )
            final = jnp.sum(key_back, axis=0, keepdims=True) + t["through"] * jnp.sum(
                row_sum(back_now * state), axis=0, keepdims=True
            )
            scores_low = (grad_scores * decay).astype(bf16)
            strict_low = (strict * (b * decay)).astype(bf16)
            k_low, q_low = k.astype(bf16), q.astype(bf16)
            grad_q = out_state + mul(scores_low, k_low)
            grad_k = (
                carried_back
                - (b * since) * side_state
                + mul(scores_low, q_low, (0, 0))
                + mul(strict_low, k_low)
                + mul(strict_low, k_low, (0, 0))
            )
            grad_v = b * grad_side
            sums_grad = sums_grad + jnp.where(
                lane == 2 * head, grad_sums + jnp.where(place == CHUNK - 1, final, 0.0), 0.0
            )
            strength_grad = strength_grad + jnp.where(lane == 2 * head + 1, grad_strength, 0.0)
            grad_q = grad_q * key_width ** (-0.5)
            unit = t["unit_q"]
            grad_q = t["q_scale"] * (grad_q - unit * row_sum(grad_q * unit))
            grad_k = t["k_scale"] * (grad_k - k * row_sum(grad_k * k))
            at = head * channels
            for name, grad, size in (
                ("q", grad_q, key_width),
                ("k", grad_k, key_width),
                ("v", grad_v, value_width),
            ):
                pre, sig = t[name + "_slope"]
                mixed_scr[rows, at : at + size] = grad * (sig * (1.0 + pre * (1.0 - sig)))
                at += size
        step = 1
        while step < CHUNK:
            sums_grad = sums_grad + jnp.where(
                place < CHUNK - step, pltpu.roll(sums_grad, CHUNK - step, 0), 0.0
            )
            step *= 2
        rates = rates_ref[rows, :]
        log_decay, _ = decays(rates, log_rates_ref[...], bias_ref[...])
        strength = sigmoid(rates)
        inputs_grad = sums_grad * (-jnp.exp(log_rates_ref[...])) * sigmoid(rates + bias_ref[...])
        log_total = log_total + jnp.sum(sums_grad * log_decay, axis=0, keepdims=True)
        bias_total = bias_total + jnp.sum(inputs_grad, axis=0, keepdims=True)
        grads_ref[rows, heads * width :] = (
            inputs_grad + strength_grad * strength * (1.0 - strength)
        ).astype(bf16)
    grad_lanes_ref[0:1, :] = log_total
    grad_lanes_ref[1:2, :] = bias_total

    mixed_scr[length : length + 8, :] = jnp.zeros((8, mixed_scr.shape[1]), f32)
    for head in range(heads):
        columns = slice(head * channels, (head + 1) * channels)
        source = slice(head * width, head * width + channels)
        taps_here = [jnp.zeros((1, channels), f32) for _ in range(CONV)]
        for chunk in range(chunks):
            start = chunk * CHUNK
            total = None
            now = mixed_scr[start : start + CHUNK, columns]
            for tap in range(CONV):
                ahead = CONV - 1 - tap
                row = tap * heads + head
                term = taps_ref[row : row + 1, :] * (
                    mixed_scr[start + ahead : start + ahead + CHUNK, columns]
                )
                total = term if total is None else total + term
                taps_here[tap] = taps_here[tap] + jnp.sum(
                    now * shifted(project_ref, start, ahead, source), axis=0, keepdims=True
                )
            grads_ref[start : start + CHUNK, source] = total.astype(bf16)
        for tap in range(CONV):
            row = tap * heads + head
            grad_taps_ref[row : row + 1, :] = taps_here[tap]
    half = normed_ref.shape[1] // 2
    send_ref[...] = rows_dot(normed_ref[:, half:], grads_ref[...], bf16)
    if near:
        taps_to_blocks(ids_ref, grad_taps_ref, send_ref, half // LANES)


def fold_blocks(keep, got_ref, own_ref, low_refs):
    size = own_ref.shape[0]
    own_ref[...] = keep[0:size, :] + got_ref[0:size, :].astype(f32)
    for k, ref in enumerate(low_refs):
        here = slice((k + 1) * size, (k + 2) * size)
        ref[...] = (keep[here, :] + got_ref[here, :].astype(f32)).astype(bf16)


def mixer_products(near, refs):
    ids_ref, normed_ref, rows_ref, gated_ref, grads_ref, grad_gate_ref, mix_ref, weights_ref, grad_taps_ref = refs[:9]
    back_send_ref, back_keep_ref, mix_keep_ref = refs[10:13]
    values = grad_gate_ref.shape[1]
    half = normed_ref.shape[1] // 2
    gate_keep_ref = refs[-1]
    gate_keep_ref[:, :values] = rows_dot(normed_ref[:, :half], grad_gate_ref[...])
    gate_keep_ref[:, values:] = rows_dot(rows_ref[:, :half], gated_ref[...])
    if near:
        fold_blocks(gate_keep_ref, refs[9], refs[13], refs[14:-1])
    back = cols_dot(grads_ref[...], mix_ref[...])
    back = back + cols_dot(grad_gate_ref[...], weights_ref[:, :values])
    rows_to_blocks(ids_ref, back, back_send_ref, back_keep_ref)
    mix_keep_ref[...] = rows_dot(normed_ref[:, :half], grads_ref[...])
    if near:
        taps_to_blocks(ids_ref, grad_taps_ref, mix_keep_ref, 0)


def mix_fold(mix_keep_ref, mix_got_ref, gate_ref, gate_got_ref, gate_out_ref, own_ref, *low_refs):
    fold_blocks(mix_keep_ref, mix_got_ref, own_ref, low_refs)
    gate_out_ref[...] = gate_ref[...] + gate_got_ref[...].astype(f32)


def norm_scale(rows):
    return lax.rsqrt(jnp.mean(rows * rows, axis=1, keepdims=True) + NORM_EPS)


def prepare(ids_ref, rows_ref, grad_ref, mixer_gain_ref, ffn_gain_ref, resid_ref, both_ref, gains_ref):
    size = rows_ref.shape[0]
    count = rows_ref.shape[1] // LANES
    for place in range(count):
        at = pl.multiple_of(order_of(ids_ref, place) * LANES, LANES)
        here = slice(place * LANES, (place + 1) * LANES)
        resid_ref[:, here] = rows_ref[:, pl.ds(at, LANES)].astype(f32)
        both_ref[size:, here] = grad_ref[:, pl.ds(at, LANES)]
        gains_ref[0:1, here] = mixer_gain_ref[:, pl.ds(at, LANES)]
        gains_ref[1:2, here] = ffn_gain_ref[:, pl.ds(at, LANES)]
    resid = resid_ref[...]
    both_ref[0:size, :] = (resid * norm_scale(resid) * gains_ref[0:1, :]).astype(bf16)


def fold(keep_ref, got_ref, keep_out_ref, send_ref):
    size = send_ref.shape[0]
    keep_out_ref[...] = keep_ref[0:size, :] + got_ref[0:size, :].astype(f32)
    send_ref[...] = (keep_ref[size:, :] + got_ref[size:, :].astype(f32)).astype(bf16)


def middle_norm(keep_ref, got_ref, resid_in_ref, gains_ref, resid_ref, ffn_in_ref):
    resid = resid_in_ref[...] + keep_ref[...] + got_ref[...].astype(f32)
    resid_ref[...] = resid
    ffn_in_ref[...] = (resid * norm_scale(resid) * gains_ref[1:2, :]).astype(bf16)


def place_of(ids_ref, block, count):
    return ids_ref[1 + count + block]


def feed_forward(ids_ref, refs):
    ffn_refs, grad_refs, (weights_ref,), outs, (ffn_ref, top_ref, weights_scr) = refs
    ffn_out_ref, top_out_ref, hidden_ref, grad_gate_ref, out_send, out_keep, back_send, back_keep = outs
    size = ffn_refs[0].shape[0]
    count = ffn_ref.shape[1] // LANES
    for block in range(count):
        at = pl.multiple_of(order_of(ids_ref, block) * LANES, LANES)
        weights_scr[block * LANES : (block + 1) * LANES, :] = weights_ref[pl.ds(at, LANES), :]
    for k in range(4):
        ffn_ref[k * size : (k + 1) * size, :] = ffn_refs[k][...]
        top_ref[k * size : (k + 1) * size, :] = grad_refs[k][size:, :]
    hidden_size = hidden_ref.shape[1]
    gate_up_w = weights_scr[:, : 2 * hidden_size]
    down_w = weights_scr[:, 2 * hidden_size : 3 * hidden_size]
    gate_up = dot(ffn_ref[...], gate_up_w)
    grad_hidden = dot(top_ref[...], down_w)
    gate, up = gate_up[:, :hidden_size], gate_up[:, hidden_size:]
    sig = sigmoid(gate)
    act = gate * sig
    hidden_ref[...] = (act * up).astype(bf16)
    grad_gate_ref[:, :hidden_size] = (grad_hidden * up * (sig * (1.0 + gate * (1.0 - sig)))).astype(bf16)
    grad_gate_ref[:, hidden_size:] = (grad_hidden * act).astype(bf16)
    back = cols_dot(grad_gate_ref[...], gate_up_w)
    out = cols_dot(hidden_ref[...], down_w)
    for value, send, keep in ((back, back_send, back_keep), (out, out_send, out_keep)):
        for k in range(4):
            target = send if k % 2 else keep
            half = (k // 2) * size
            target[half : half + size, :] = value[k * size : (k + 1) * size, :].astype(target.dtype)
    for block in range(count):
        at = pl.multiple_of(place_of(ids_ref, block, count) * LANES, LANES)
        here = slice(block * LANES, (block + 1) * LANES)
        ffn_out_ref[:, here] = ffn_ref[:, pl.ds(at, LANES)]
        top_out_ref[:, here] = top_ref[:, pl.ds(at, LANES)]


def feed_products(ffn_ref, top_ref, hidden_ref, grad_gate_ref, out_ref):
    hidden_size = hidden_ref.shape[1]
    out_ref[:, : 2 * hidden_size] = rows_dot(ffn_ref[...], grad_gate_ref[...], out_ref.dtype)
    out_ref[:, 2 * hidden_size : 3 * hidden_size] = rows_dot(
        top_ref[...], hidden_ref[...], out_ref.dtype
    )
    rest = out_ref.shape[1] - 3 * hidden_size
    if rest:
        out_ref[:, 3 * hidden_size :] = jnp.zeros((out_ref.shape[0], rest), out_ref.dtype)


def norm_reverse(grad, rows, gain):
    scale = norm_scale(rows)
    unit = rows * scale
    inner = grad * gain
    gain_grad = jnp.sum(grad * unit, axis=0, keepdims=True)
    return scale * (inner - unit * jnp.mean(inner * unit, axis=1, keepdims=True)), gain_grad


def middle_back(
    back_keep_ref, back_got_ref, resid_ref, both_ref, gains_ref, grad_ref, low_ref, gain_grad_ref
):
    grad_ffn_in = back_keep_ref[...] + back_got_ref[...].astype(f32)
    grad, gain_grad = norm_reverse(grad_ffn_in, resid_ref[...], gains_ref[1:2, :])
    grad = grad + both_ref[both_ref.shape[0] // 2 :, :].astype(f32)
    grad_ref[...] = grad
    low_ref[...] = grad.astype(bf16)
    gain_grad_ref[...] = gain_grad


def last_out(ids_ref, keep_ref, got_ref, resid_ref, out_ref, scr):
    scr[...] = resid_ref[...] + keep_ref[...] + got_ref[...].astype(f32)
    count = out_ref.shape[1] // LANES
    for block in range(count):
        at = pl.multiple_of(place_of(ids_ref, block, count) * LANES, LANES)
        out_ref[:, block * LANES : (block + 1) * LANES] = scr[:, pl.ds(at, LANES)].astype(bf16)


def last_grad(
    ids_ref, keep_ref, got_ref, resid_in_ref, gains_ref, grad_ref, gain_grad_ref, out_ref, gains_out_ref, scr, gain_scr
):
    grad_normed = keep_ref[...] + got_ref[...].astype(f32)
    grad, gain_grad = norm_reverse(grad_normed, resid_in_ref[...], gains_ref[0:1, :])
    scr[...] = grad + grad_ref[...]
    gain_scr[0:1, :] = gain_grad
    gain_scr[1:2, :] = gain_grad_ref[...]
    count = out_ref.shape[1] // LANES
    for block in range(count):
        at = pl.multiple_of(place_of(ids_ref, block, count) * LANES, LANES)
        here = slice(block * LANES, (block + 1) * LANES)
        out_ref[:, here] = scr[:, pl.ds(at, LANES)]
        gains_out_ref[:, here] = gain_scr[:, pl.ds(at, LANES)]


def call(kernel, outs, operands, scratch=(), name=None, scalar=True):
    specs = [pl.BlockSpec(memory_space=pltpu.VMEM)] * len(operands)
    if scalar:
        specs[0] = pl.BlockSpec(memory_space=pltpu.SMEM)
    return pl.pallas_call(
        kernel,
        out_shape=tuple(jax.ShapeDtypeStruct(shape, kind) for shape, kind in outs),
        in_specs=specs,
        out_specs=tuple([pl.BlockSpec(memory_space=pltpu.VMEM)] * len(outs)),
        scratch_shapes=[pltpu.VMEM(shape, kind) for shape, kind in scratch],
        compiler_params=pltpu.CompilerParams(vmem_limit_bytes=56 * 2**20),
        name=name,
    )(*operands)


def cut_list(items, sizes):
    parts, at = [], 0
    for size in sizes:
        parts.append(items[at : at + size])
        at += size
    return parts


def run_forward(near, ids, rows, mix, taps, log_rates, bias, value_width):
    length = rows[0].shape[0] // 2 * len(rows)
    model = rows[0].shape[1]
    wide = mix[0].shape[1]
    columns = wide - LANES
    channels = taps.shape[1]
    heads = taps.shape[0] // CONV
    key_width = (channels - value_width) // 2
    pair = (length // CHUNK, heads)
    values = heads * value_width

    def kernel(*refs):
        mixer_forward(near, cut_list(refs, (4, len(rows), len(mix), 9, 5)))

    return call(
        kernel,
        (
            ((length, columns), f32),
            ((length, LANES), f32),
            ((length, values), f32),
            (pair + (key_width, value_width), f32),
            ((length, values), f32),
            (pair + (CHUNK, CHUNK), f32),
            ((length, model), bf16),
            ((model, wide), bf16),
            (taps.shape, f32),
        ),
        (ids, taps, log_rates, bias, *rows, *mix),
        (
            (pair + (CHUNK, key_width), bf16),
            (pair + (CHUNK, key_width), f32),
            (pair + (CHUNK, CHUNK), bf16),
            (pair + (CHUNK, key_width), bf16),
            (pair + (CHUNK, value_width), f32),
        ),
        "mixer_forward",
    )


def run_backward(near, ids, grad_out, log_rates, bias, kept):
    project, _, out, states, _, _, normed, mix, taps = kept
    length, model = normed.shape
    values = out.shape[1]
    wide = mix.shape[1]
    heads, key_width, value_width = states.shape[1:]
    pair = (length // CHUNK, heads)

    def kernel(*refs):
        mixer_backward(near, cut_list(refs, (4, len(kept), 4, 7)))

    return call(
        kernel,
        (
            ((length, wide), bf16),
            (taps.shape, f32),
            ((2, LANES), f32),
            ((model // 2, wide), bf16),
        ),
        (ids, log_rates, bias, grad_out, *kept),
        (
            (pair + (key_width, value_width), f32),
            ((length, values), f32),
            (pair + (CHUNK, key_width), bf16),
            (pair + (CHUNK, key_width), bf16),
            (pair + (CHUNK, CHUNK), bf16),
            (pair + (CHUNK, key_width), bf16),
            ((length + 8, heads * taps.shape[1]), f32),
        ),
        "mixer_backward",
    )


def swap(array, axis, size, offset):
    return lax.ppermute(array, axis, [(i, i ^ offset) for i in range(size)])


def after(arrays, others):
    kept, _ = lax.optimization_barrier((arrays, others))
    return kept


def per_device(
    layer_in,
    mixer_gain,
    w_mix,
    w_rates,
    conv_taps,
    a_log,
    dt_bias,
    head_gain,
    w_out,
    ffn_gain,
    w_gate_up,
    w_down,
    out_grad,
):
    size = lax.axis_size("dp")
    ranks = lax.axis_size("tensor")
    depth, heads, width = w_mix.shape
    model = layer_in.shape[1]
    hidden = w_gate_up.shape[2]
    value_size = w_out.shape[0]
    rows = layer_in.shape[0]
    taps_shape = conv_taps.shape
    part = taps_shape[2]
    near = size == 8 and depth == LANES and 2 * part == LANES
    half = size // 2
    rank, own = lax.axis_index("tensor"), lax.axis_index("dp")
    blocks = model // LANES
    if near:
        offsets = [2 * p for p in range(half)] + [2 * p + 1 for p in range(half)]
        order = own ^ jnp.array(offsets, jnp.int32)
        places = [offsets.index(k) for k in range(size)]
        index = own ^ jnp.arange(size, dtype=jnp.int32)
        place = jnp.where(index % 2 == 0, index // 2, half + index // 2)
        assert places == [k // 2 if k % 2 == 0 else half + k // 2 for k in range(size)]
    else:
        order = place = jnp.arange(blocks, dtype=jnp.int32)
    ids = jnp.concatenate([jnp.full((1,), rank, jnp.int32), order, place])

    def near_z(shard):
        return [shard] + [swap(shard, "dp", size, 2 * p) for p in range(1, half)]

    def near_x(shards, own_side):
        return [own_side, swap(jnp.concatenate(shards[1:], 0), "dp", size, 1)]

    def far(shard):
        return lax.all_gather(shard, "dp", axis=0, tiled=True)

    def rows_y(block):
        return swap(block, "tensor", ranks, 2)

    def rows_core(block):
        return swap(block, "tensor", ranks, 1)

    def gather_rows(block):
        across = rows_y(block)
        return [block, rows_core(block), across, rows_core(across)]

    def sum_rows(send, keep, name):
        got = rows_core(send)
        shape = (rows, model)
        keep, send = call(fold, ((shape, f32), (shape, bf16)), (keep, got), name=name, scalar=False)
        return keep, rows_y(send)

    channels = width - head_gain.shape[0]
    values = value_size
    rates_tile = jnp.pad(w_rates.reshape(depth, 2 * heads), ((0, 0), (0, LANES - 2 * heads)))
    if near:
        taps_tile = conv_taps.reshape(CONV * heads, part)
        taps_tile = jnp.pad(taps_tile, ((0, depth - CONV * heads), (LANES - part, 0)))
        rates_tile = rates_tile + taps_tile
    mix_shard = jnp.concatenate(
        [w_mix[:, :, :channels].reshape(depth, heads * channels), rates_tile], 1
    )
    gate_shard = jnp.concatenate([w_mix[:, :, channels:].reshape(depth, values), w_out.T], 1)
    filler = -3 * hidden % LANES
    ffn_shard = jnp.concatenate(
        [w_gate_up.reshape(depth, 2 * hidden), w_down.T, jnp.zeros((depth, filler), bf16)], 1
    )

    if near:
        mix_z = near_z(mix_shard)
        mix_side = swap(mix_shard, "dp", size, 1)
    square = (rows, model)
    resid_in, both, gains = call(
        prepare,
        ((square, f32), ((2 * rows, model), bf16), ((2, model), f32)),
        (ids, layer_in, out_grad, mixer_gain.reshape(1, -1), ffn_gain.reshape(1, -1)),
        name="prepare",
    )
    ffn_full = far(after(ffn_shard, (mix_z, mix_side)) if near else ffn_shard)
    both_all = gather_rows(both)
    if near:
        gate_shard = after(gate_shard, (mix_z, mix_side))
        gate_z = near_z(gate_shard)
        gate_side = swap(gate_shard, "dp", size, 1)
        mix_slots = mix_z + near_x(mix_z, mix_side)
        taps = jnp.zeros((CONV * heads, part * size), f32)
    else:
        mix_slots = [far(mix_shard)]
        gate_slots = [far(gate_shard)]
        taps = lax.all_gather(conv_taps, "dp", axis=2, tiled=True).astype(f32)
        taps = taps.reshape(CONV * heads, part * size)

    first_head = rank * heads

    def on_lanes(per_head):
        here = lax.dynamic_slice_in_dim(per_head, first_head, heads)
        pairs = jnp.stack([here, jnp.zeros_like(here)], 1).reshape(1, -1)
        return jnp.pad(pairs, ((0, 0), (0, LANES - pairs.shape[1])))

    def off_lanes(row):
        here = row[: 2 * heads : 2]
        return lax.dynamic_update_slice_in_dim(jnp.zeros_like(a_log), here, first_head, 0)

    lanes = (on_lanes(a_log), on_lanes(dt_bias))
    gain_row = head_gain.reshape(1, -1)
    kept = run_forward(near, ids, both_all, mix_slots, taps, *lanes, head_gain.shape[0])
    heads_out, normed_rows, mix_full = kept[2], kept[6], kept[7]
    if near:
        gate_slots = gate_z + near_x(gate_z, gate_side)
    tokens = rows * ranks
    block_pair = (2 * rows, model)
    gated, gate, gate_full, out_send, out_keep = call(
        out_product,
        (
            ((tokens, values), bf16),
            ((tokens, values), f32),
            ((model, 2 * values), bf16),
            (block_pair, bf16),
            (block_pair, f32),
        ),
        (ids, gain_row, normed_rows, heads_out, *gate_slots),
        (),
        "out_product",
    )
    out_keep, out_got = sum_rows(out_send, out_keep, "out_fold")
    resid, ffn_in = call(
        middle_norm, ((square, f32), (square, bf16)), (out_keep, out_got, resid_in, gains), name="middle_norm", scalar=False
    )
    ffn_all = gather_rows(ffn_in)

    def ffn_kernel(ids_ref, *refs):
        feed_forward(ids_ref, cut_list(refs, (4, 4, 1, 8, 3)))

    ffn_rows, top_rows, hidden_low, grad_gate, ffn_send, ffn_keep, back_send, back_keep = call(
        ffn_kernel,
        (
            ((tokens, model), bf16),
            ((tokens, model), bf16),
            ((tokens, hidden), bf16),
            ((tokens, 2 * hidden), bf16),
            (block_pair, bf16),
            (block_pair, f32),
            (block_pair, bf16),
            (block_pair, f32),
        ),
        (ids, *ffn_all, *both_all, ffn_full),
        (((tokens, model), bf16), ((tokens, model), bf16), (ffn_full.shape, bf16)),
        "feed_forward",
    )
    split = model // 2

    def scatter_x(send):
        return swap(send, "dp", size, 1) if near else send

    back_keep, back_got = sum_rows(back_send, back_keep, "back_fold")
    (ffn_grads,) = call(
        feed_products,
        (((model, 3 * hidden + filler), bf16 if near else f32),),
        (ffn_rows, top_rows, hidden_low, grad_gate),
        name="feed_products",
        scalar=False,
    )
    ffn_total = lax.psum_scatter(ffn_grads, "dp", scatter_dimension=0, tiled=True).astype(f32)
    grad_resid, mix_low, ffn_gain_grad = call(
        middle_back,
        ((square, f32), (square, bf16), ((1, model), f32)),
        (back_keep, back_got, resid, both, gains),
        name="middle_back",
        scalar=False,
    )
    mix_all = gather_rows(mix_low)
    ffn_keep, ffn_got = sum_rows(ffn_send, ffn_keep, "ffn_fold")
    (layer_out,) = call(
        last_out, ((square, bf16),), (ids, ffn_keep, ffn_got, resid), ((square, f32),), "last_out"
    )
    grad_rows, grad_out, gate_grad, head_gain_grad, gate_send = call(
        gate_back,
        (
            ((tokens, model), bf16),
            ((tokens, values), f32),
            ((tokens, values), bf16),
            (gain_row.shape, f32),
            ((split, 2 * values), bf16),
        ),
        (ids, gain_row, normed_rows, heads_out, gated, gate, gate_full, *mix_all),
        (),
        "gate_back",
    )
    gate_got = scatter_x(gate_send)
    grads, taps_grad, lanes_grad, mix_send = run_backward(near, ids, grad_out, *lanes, kept)
    mix_got = scatter_x(mix_send)

    def products_kernel(*refs):
        mixer_products(near, refs)

    def blocks_of(send):
        return (((depth, send.shape[1]), f32),) + (((depth, send.shape[1]), bf16),) * (half - 1)

    keep_shape = ((split, 2 * values), f32)
    norm_send, norm_keep, mix_keep, *gate_parts = call(
        products_kernel,
        ((block_pair, bf16), (block_pair, f32), (mix_send.shape, f32))
        + (blocks_of(gate_send) if near else (keep_shape,)),
        (ids, normed_rows, grad_rows, gated, grads, gate_grad, mix_full, gate_full, taps_grad, gate_got),
        (keep_shape,) if near else (),
        "mixer_products",
    )

    def far_sum(parts, got):
        if near:
            own, lows = parts[0], parts[1:]
            return [own] + [swap(low, "dp", size, 2 * (p + 1)) for p, low in enumerate(lows)]
        return [
            lax.psum_scatter(
                jnp.concatenate([parts[0], got.astype(f32)], 0), "dp", scatter_dimension=0, tiled=True
            )
        ]

    def add_up(blocks):
        total = blocks[0]
        for block in blocks[1:]:
            total = total + block.astype(f32)
        return total

    gate_blocks = far_sum(gate_parts, gate_got)
    norm_keep, norm_got = sum_rows(norm_send, norm_keep, "norm_fold")
    in_grad, gains_grad = call(
        last_grad,
        ((square, f32), ((2, model), f32)),
        (ids, norm_keep, norm_got, resid_in, gains, grad_resid, ffn_gain_grad),
        ((square, f32), ((2, model), f32)),
        "last_grad",
    )

    mix_parts = [mix_keep]
    if near:
        gate_sum, *mix_parts = call(
            mix_fold,
            (((depth, 2 * values), f32),) + blocks_of(mix_send),
            (mix_keep, mix_got, gate_blocks[0], gate_blocks[1]),
            name="mix_fold",
            scalar=False,
        )
        gate_blocks = [gate_sum] + gate_blocks[2:]
    mix_blocks = far_sum(mix_parts, mix_got)
    grad_w_gate_up = ffn_total[:, : 2 * hidden].reshape(w_gate_up.shape)
    grad_w_down = ffn_total[:, 2 * hidden : 3 * hidden].T

    small = jnp.concatenate(
        [
            gains_grad.reshape(-1),
            head_gain_grad.reshape(-1),
            off_lanes(lanes_grad[0]),
            off_lanes(lanes_grad[1]),
        ]
    )
    length = small.size
    small = jnp.pad(small, (0, -length % (8 * LANES))).reshape(8, -1)
    for offset in (1, 2):
        small = small + swap(small, "tensor", ranks, offset)
    if near:
        small = small + swap(small, "dp", size, 1)
        small, grad_w_gate_up, grad_w_down = lax.optimization_barrier((small, grad_w_gate_up, grad_w_down))
        small = add_up([small] + [swap(small, "dp", size, 2 * p) for p in range(1, half)])
    else:
        small = lax.psum(small, "dp")
    small = small.reshape(-1)[:length]
    grad_mixer_gain, grad_ffn_gain = small[:model], small[model : 2 * model]
    small = small[2 * model :]
    grad_head_gain, small = small[: head_gain.size], small[head_gain.size :]
    grad_a_log, grad_dt_bias = small[: a_log.size], small[a_log.size :]

    gate_total = add_up(gate_blocks)
    mix_total = add_up(mix_blocks)
    grad_w_mix = jnp.concatenate(
        [
            mix_total[:, : heads * channels].reshape(depth, heads, channels),
            gate_total[:, :values].reshape(depth, heads, -1),
        ],
        2,
    )
    grad_w_rates = mix_total[:, heads * channels : heads * channels + 2 * heads].reshape(w_rates.shape)
    if near:
        grad_taps = mix_total[: CONV * heads, mix_total.shape[1] - part :].reshape(taps_shape)
    else:
        grad_taps = lax.psum_scatter(
            taps_grad.reshape(CONV, heads, -1), "dp", scatter_dimension=2, tiled=True
        )
    return (
        layer_out,
        in_grad,
        grad_mixer_gain,
        grad_w_mix,
        grad_w_rates,
        grad_taps,
        grad_a_log,
        grad_dt_bias,
        grad_head_gain,
        gate_total[:, values:].T,
        grad_ffn_gain,
        grad_w_gate_up,
        grad_w_down,
    )


def solution(mesh):
    return jax.shard_map(
        per_device,
        mesh=mesh,
        in_specs=(
            P(("dp", "tensor"), None),
            P(),
            P("dp", "tensor", None),
            P("dp", "tensor", None),
            P(None, "tensor", "dp"),
            P(),
            P(),
            P(),
            P("tensor", "dp"),
            P(),
            P("dp", None, "tensor"),
            P("tensor", "dp"),
            P(("dp", "tensor"), None),
        ),
        out_specs=(
            P(("dp", "tensor"), None),
            P(("dp", "tensor"), None),
            P(),
            P("dp", "tensor", None),
            P("dp", "tensor", None),
            P(None, "tensor", "dp"),
            P(),
            P(),
            P(),
            P("tensor", "dp"),
            P(),
            P("dp", None, "tensor"),
            P("tensor", "dp"),
        ),
        check_vma=False,
    )
```

```python
import jax
import jax.numpy as jnp
from jax import lax
from jax.experimental import pallas as pl
from jax.experimental.pallas import tpu as pltpu
from jax.sharding import PartitionSpec as P

CONV = 4


highest = lax.Precision.HIGHEST
NORM_EPS = 1e-05
UNIT_EPS = 1e-06
bf16 = jnp.bfloat16
f32 = jnp.float32


def rows_dot(left, right, kind=f32):
    return lax.dot_general(
        left, right, (((0,), (0,)), ((), ())), preferred_element_type=f32
    ).astype(kind)


def cols_dot(left, right):
    return lax.dot_general(left, right, (((1,), (1,)), ((), ())), preferred_element_type=f32)


def dot(left, right):
    return jnp.dot(left, right, preferred_element_type=f32)


CHUNK = 128
LANES = 128


def mul(left, right, over=(1, 0), exact=False):
    dims = (((over[0],), (over[1],)), ((), ()))
    if exact:
        return lax.dot_general(left, right, dims, precision=highest, preferred_element_type=f32)
    return lax.dot_general(left.astype(bf16), right.astype(bf16), dims, preferred_element_type=f32)


def square_ids():
    shape = (CHUNK, CHUNK)
    return lax.broadcasted_iota(jnp.int32, shape, 0), lax.broadcasted_iota(jnp.int32, shape, 1)


def sigmoid(v):
    return 1.0 / (1.0 + jnp.exp(-v))


def softplus(v):
    return jnp.maximum(v, 0.0) + jnp.log1p(jnp.exp(-jnp.abs(v)))


def row_sum(v):
    return jnp.sum(v, axis=1, keepdims=True)


def unit_inverse(lower):
    rows, cols = square_ids()
    inverse = jnp.where(rows == cols, 1.0, 0.0)
    block = 1
    while block < CHUNK:
        corner = (
            (rows // (2 * block) == cols // (2 * block))
            & ((rows // block) % 2 == 1)
            & ((cols // block) % 2 == 0)
        )
        part = jnp.where(corner, lower, 0.0)
        if block == 1:
            inverse = inverse - part
        else:
            inverse = inverse - mul(mul(inverse, part), inverse)
        block *= 2
    return inverse


def shifted(ref, start, back, columns):
    if start == 0 and back:
        rows = lax.broadcasted_iota(jnp.int32, (CHUNK, columns.stop - columns.start), 0)
        return jnp.where(rows >= back, pltpu.roll(ref[0:CHUNK, columns], back, 0), 0.0)
    return ref[start - back : start - back + CHUNK, columns]


def short_conv(project_ref, taps_ref, start, head, heads, columns, tap_columns):
    total = None
    for tap in range(CONV):
        row = tap * heads + head
        term = taps_ref[row : row + 1, tap_columns] * shifted(
            project_ref, start, CONV - 1 - tap, columns
        )
        total = term if total is None else total + term
    return total


def decays(rates, log_rates, bias):
    log_decay = -jnp.exp(log_rates) * softplus(rates + bias)
    place = lax.broadcasted_iota(jnp.int32, rates.shape, 0)
    total = log_decay
    step = 1
    while step < CHUNK:
        total = total + jnp.where(place >= step, pltpu.roll(total, step, 0), 0.0)
        step *= 2
    return log_decay, total


def chunk_terms(head, project_ref, taps_ref, start, total, total_rows, strength, key_width, value_width):
    width = 2 * key_width + value_width
    base = head * width
    heads = project_ref.shape[1] // width
    terms = {}
    parts = (("q", 0, key_width), ("k", key_width, key_width), ("v", 2 * key_width, value_width))
    for name, at, size in parts:
        pre = short_conv(
            project_ref,
            taps_ref,
            start,
            head,
            heads,
            slice(base + at, base + at + size),
            slice(at, at + size),
        )
        gate = sigmoid(pre)
        mixed = pre * gate
        if name != "v":
            scale = lax.rsqrt(row_sum(mixed * mixed) + UNIT_EPS)
            mixed = mixed * scale
            terms[name + "_scale"] = scale
        terms[name + "_slope"] = (pre, gate)
        terms[name] = mixed
    terms["unit_q"] = terms["q"]
    terms["q"] = terms["q"] * key_width ** (-0.5)
    lane = 2 * head
    sums = total[:, lane : lane + 1]
    across = total_rows[lane : lane + 1, :]
    rows, cols = square_ids()
    decay = jnp.where(rows >= cols, jnp.exp(jnp.minimum(sums - across, 0.0)), 0.0)
    final = total[CHUNK - 1 : CHUNK, lane : lane + 1]
    terms["b"] = strength[:, lane + 1 : lane + 2]
    terms["since"] = jnp.exp(sums)
    terms["remaining"] = jnp.exp(final - sums)
    terms["through"] = jnp.exp(final)
    terms["decay"] = decay
    terms["dots"] = mul(terms["k"], terms["k"], (1, 1)) * jnp.where(rows > cols, decay, 0.0)
    terms["scores"] = mul(terms["q"], terms["k"], (1, 1)) * decay
    return terms


def stack_rows(refs, target, column):
    at = 0
    for ref in refs:
        rows = ref.shape[0]
        columns = min(ref.shape[1], target.shape[1] - column)
        target[at : at + rows, column : column + columns] = ref[:, :columns]
        at += rows


def rows_in_time(ids_ref, refs, target):
    size = target.shape[0] // len(refs)
    for k, ref in enumerate(refs):
        at = pl.multiple_of((ids_ref[0] ^ k) * size, size)
        target[pl.ds(at, size), :] = ref[0:size, :]


def order_of(ids_ref, place):
    return ids_ref[1 + place]


def taps_from_blocks(ids_ref, mix_ref, shape):
    rows, channels = shape
    count = mix_ref.shape[0] // LANES
    part = channels // count
    lane = lax.broadcasted_iota(jnp.int32, shape, 1)
    total = jnp.zeros(shape, f32)
    for place in range(count):
        block = mix_ref[place * LANES : place * LANES + 16, mix_ref.shape[1] - LANES :]
        block = block.astype(f32)[0:rows, LANES - part :]
        wide = jnp.concatenate([block] * count, 1)
        total = total + jnp.where(lane // part == order_of(ids_ref, place), wide, 0.0)
    return total


def taps_to_blocks(ids_ref, taps_ref, target, first):
    rows, channels = taps_ref.shape
    count = target.shape[0] // LANES
    part = channels // (2 * count)
    for place in range(count):
        owner = order_of(ids_ref, first + place)
        block = jnp.zeros((rows, part), f32)
        for other in range(2 * count):
            block = block + jnp.where(
                owner == other, taps_ref[:, other * part : (other + 1) * part], 0.0
            )
        block = jnp.concatenate([jnp.zeros((rows, LANES - part), f32), block], 1)
        block = jnp.concatenate([block, jnp.zeros((16 - rows, LANES), f32)], 0)
        at = (slice(place * LANES, place * LANES + 16), slice(target.shape[1] - LANES, target.shape[1]))
        target[at] = (target[at].astype(f32) + block).astype(target.dtype)


def rows_to_blocks(ids_ref, value, send_ref, keep_ref):
    size = value.shape[0] // 4
    for k in range(4):
        target = send_ref if k % 2 else keep_ref
        half = (k // 2) * size
        for block in range(4):

            @pl.when((ids_ref[0] ^ k) == block)
            def _(block=block, half=half, target=target):
                target[half : half + size, :] = value[block * size : (block + 1) * size, :].astype(
                    target.dtype
                )


def mixer_forward(near, refs):
    (ids_ref, taps_in_ref, log_rates_ref, bias_ref), row_refs, mix_refs, outs, scratch = refs
    project_ref, rates_ref, out_ref, states_ref, carried_ref, inverse_ref = outs[:6]
    normed_ref, mix_ref, taps_ref = outs[6:]
    q_scr, kr_scr, p_scr, w_scr, u_scr = scratch
    length = normed_ref.shape[0]
    heads = states_ref.shape[1]
    key_width, value_width = states_ref.shape[2:]
    width = project_ref.shape[1] // heads
    chunks = length // CHUNK
    rows_in_time(ids_ref, row_refs, normed_ref)
    stack_rows(mix_refs, mix_ref, 0)
    if near:
        taps_ref[...] = taps_from_blocks(ids_ref, mix_ref, taps_in_ref.shape)
    else:
        taps_ref[...] = taps_in_ref[...]
    for head in range(heads):
        columns = slice(head * width, (head + 1) * width)
        project_ref[:, columns] = dot(normed_ref[...], mix_ref[:, columns])
    rates_ref[...] = dot(normed_ref[...], mix_ref[:, heads * width :])
    through = {}
    for chunk in range(chunks):
        start = chunk * CHUNK
        rows = slice(start, start + CHUNK)
        rates = rates_ref[rows, :]
        _, total = decays(rates, log_rates_ref[...], bias_ref[...])
        strength = sigmoid(rates)
        total_rows = jnp.transpose(total)
        for head in range(heads):
            t = chunk_terms(
                head, project_ref, taps_ref, start, total, total_rows, strength, key_width, value_width
            )
            inverse = unit_inverse(t["b"] * t["dots"])
            inverse_ref[chunk, head] = inverse
            side = jnp.concatenate([(t["b"] * t["since"]) * t["k"], t["b"] * t["v"]], 1)
            solved = mul(inverse, side)
            w_scr[chunk, head] = solved[:, :key_width].astype(bf16)
            u_scr[chunk, head] = solved[:, key_width:]
            q_scr[chunk, head] = (t["q"] * t["since"]).astype(bf16)
            kr_scr[chunk, head] = t["k"] * t["remaining"]
            p_scr[chunk, head] = t["scores"].astype(bf16)
            through[chunk, head] = t["through"]
    state = [jnp.zeros((key_width, value_width), f32) for _ in range(heads)]
    for chunk in range(chunks):
        rows = slice(chunk * CHUNK, (chunk + 1) * CHUNK)
        for head in range(heads):
            columns = slice(head * value_width, (head + 1) * value_width)
            states_ref[chunk, head] = state[head]
            low = state[head].astype(bf16)
            carried = u_scr[chunk, head] - mul(w_scr[chunk, head], low)
            carried_ref[rows, columns] = carried
            out_ref[rows, columns] = mul(q_scr[chunk, head], low) + mul(p_scr[chunk, head], carried)
            state[head] = through[chunk, head] * state[head] + mul(
                kr_scr[chunk, head], carried, (0, 0), exact=True
            )


def out_product(ids_ref, gain_ref, normed_ref, out_ref, *refs):
    weight_refs, (gated_ref, gate_ref, weights_ref, send_ref, keep_ref) = refs[:-5], refs[-5:]
    value_width = gain_ref.shape[1]
    values = out_ref.shape[1]
    stack_rows(weight_refs, weights_ref, 0)
    for head in range(values // value_width):
        columns = slice(head * value_width, (head + 1) * value_width)
        gate = dot(normed_ref[...], weights_ref[:, columns])
        gate_ref[:, columns] = gate
        out = out_ref[:, columns]
        scale = lax.rsqrt(row_sum(out * out) / value_width + NORM_EPS)
        gated_ref[:, columns] = (out * scale * gain_ref[...] * (gate * sigmoid(gate))).astype(bf16)
    rows_to_blocks(ids_ref, cols_dot(gated_ref[...], weights_ref[:, values:]), send_ref, keep_ref)


def gate_back(ids_ref, gain_ref, normed_ref, out_ref, gated_ref, gate_ref, weights_ref, *refs):
    row_refs, (rows_ref, grad_out_ref, grad_gate_ref, gain_grad_ref, send_ref) = refs[:-5], refs[-5:]
    value_width = gain_ref.shape[1]
    values = out_ref.shape[1]
    rows_in_time(ids_ref, row_refs, rows_ref)
    gain = gain_ref[...]
    gain_total = jnp.zeros((1, value_width), f32)
    for head in range(values // value_width):
        columns = slice(head * value_width, (head + 1) * value_width)
        grad = dot(rows_ref[...], weights_ref[:, values + head * value_width : values + (head + 1) * value_width])
        out, gate = out_ref[:, columns], gate_ref[:, columns]
        scale = lax.rsqrt(row_sum(out * out) / value_width + NORM_EPS)
        unit = out * scale
        sig = sigmoid(gate)
        act = gate * sig
        gain_total = gain_total + jnp.sum(grad * unit * act, axis=0, keepdims=True)
        grad_gate_ref[:, columns] = (
            grad * gain * unit * (sig * (1.0 + gate * (1.0 - sig)))
        ).astype(bf16)
        inner = grad * act * gain
        grad_out_ref[:, columns] = scale * (inner - unit * (row_sum(inner * unit) / value_width))
    gain_grad_ref[...] = gain_total
    half = normed_ref.shape[1] // 2
    send_ref[:, :values] = rows_dot(normed_ref[:, half:], grad_gate_ref[...], bf16)
    send_ref[:, values:] = rows_dot(rows_ref[:, half:], gated_ref[...], bf16)


def mixer_backward(near, refs):
    (ids_ref, log_rates_ref, bias_ref, grad_out_scr), kept, outs, scratch = refs
    (
        project_ref,
        rates_ref,
        out_ref,
        states_ref,
        carried_ref,
        inverse_ref,
        normed_ref,
        _,
        taps_ref,
    ) = kept
    grads_ref, grad_taps_ref, grad_lanes_ref, send_ref = outs
    back_scr, grad_carried_scr, q_scr, kr_scr, p_scr, w_scr, mixed_scr = scratch
    length = normed_ref.shape[0]
    heads = states_ref.shape[1]
    key_width, value_width = states_ref.shape[2:]
    width = channels = project_ref.shape[1] // heads
    chunks = length // CHUNK

    def gather_terms(chunk):
        start = chunk * CHUNK
        rates = rates_ref[start : start + CHUNK, :]
        _, total = decays(rates, log_rates_ref[...], bias_ref[...])
        strength = sigmoid(rates)
        total_rows = jnp.transpose(total)
        return [
            chunk_terms(
                head, project_ref, taps_ref, start, total, total_rows, strength, key_width, value_width
            )
            for head in range(heads)
        ]

    through = {}
    for chunk in range(chunks):
        rows = slice(chunk * CHUNK, (chunk + 1) * CHUNK)
        terms = gather_terms(chunk)
        for head in range(heads):
            columns = slice(head * value_width, (head + 1) * value_width)
            t = terms[head]
            w_scr[chunk, head] = mul(
                inverse_ref[chunk, head], (t["b"] * t["since"]) * t["k"]
            ).astype(bf16)
            q_scr[chunk, head] = (t["q"] * t["since"]).astype(bf16)
            kr_scr[chunk, head] = (t["k"] * t["remaining"]).astype(bf16)
            p_scr[chunk, head] = t["scores"].astype(bf16)
            through[chunk, head] = t["through"]

    back = [jnp.zeros((key_width, value_width), f32) for _ in range(heads)]
    for chunk in reversed(range(chunks)):
        rows = slice(chunk * CHUNK, (chunk + 1) * CHUNK)
        for head in range(heads):
            columns = slice(head * value_width, (head + 1) * value_width)
            back_scr[chunk, head] = back[head]
            grad_out = grad_out_scr[rows, columns].astype(bf16)
            grad_carried = mul(p_scr[chunk, head], grad_out, (0, 0)) + mul(
                kr_scr[chunk, head], back[head]
            )
            grad_carried_scr[rows, columns] = grad_carried
            back[head] = (
                through[chunk, head] * back[head]
                + mul(q_scr[chunk, head], grad_out, (0, 0))
                - mul(w_scr[chunk, head], grad_carried, (0, 0))
            )

    rows_at, cols_at = square_ids()
    lane = lax.broadcasted_iota(jnp.int32, (CHUNK, LANES), 1)
    place = lax.broadcasted_iota(jnp.int32, (CHUNK, LANES), 0)
    log_total = jnp.zeros((1, LANES), f32)
    bias_total = jnp.zeros((1, LANES), f32)
    for chunk in range(chunks):
        rows = slice(chunk * CHUNK, (chunk + 1) * CHUNK)
        terms = gather_terms(chunk)
        sums_grad = jnp.zeros((CHUNK, LANES), f32)
        strength_grad = jnp.zeros((CHUNK, LANES), f32)
        for head in range(heads):
            columns = slice(head * value_width, (head + 1) * value_width)
            t = terms[head]
            b, since, remaining, decay = t["b"], t["since"], t["remaining"], t["decay"]
            q, k, v = t["q"], t["k"], t["v"]
            state = states_ref[chunk, head]
            back_now = back_scr[chunk, head]
            carried = carried_ref[rows, columns]
            grad_out = grad_out_scr[rows, columns]
            grad_side = mul(inverse_ref[chunk, head], grad_carried_scr[rows, columns], (0, 0))
            strict = jnp.where(rows_at > cols_at, -mul(grad_side, carried, (1, 1)), 0.0)
            grad_scores = mul(grad_out, carried, (1, 1))
            side_state = mul(grad_side, state, (1, 1))
            out_state = since * mul(grad_out, state, (1, 1))
            carried_back = remaining * mul(carried, back_now, (1, 1))
            key_side = since * row_sum(k * side_state)
            strict_dots = strict * t["dots"]
            grad_strength = row_sum(grad_side * v) - key_side + row_sum(strict_dots)
            pulls = grad_scores * t["scores"] + b * strict_dots
            key_back = row_sum(k * carried_back)
            grad_sums = (
                row_sum(pulls - jnp.transpose(pulls))
                - b * key_side
                + row_sum(q * out_state)
                - key_back
            )
            final = jnp.sum(key_back, axis=0, keepdims=True) + t["through"] * jnp.sum(
                row_sum(back_now * state), axis=0, keepdims=True
            )
            scores_low = (grad_scores * decay).astype(bf16)
            strict_low = (strict * (b * decay)).astype(bf16)
            k_low, q_low = k.astype(bf16), q.astype(bf16)
            grad_q = out_state + mul(scores_low, k_low)
            grad_k = (
                carried_back
                - (b * since) * side_state
                + mul(scores_low, q_low, (0, 0))
                + mul(strict_low, k_low)
                + mul(strict_low, k_low, (0, 0))
            )
            grad_v = b * grad_side
            sums_grad = sums_grad + jnp.where(
                lane == 2 * head, grad_sums + jnp.where(place == CHUNK - 1, final, 0.0), 0.0
            )
            strength_grad = strength_grad + jnp.where(lane == 2 * head + 1, grad_strength, 0.0)
            grad_q = grad_q * key_width ** (-0.5)
            unit = t["unit_q"]
            grad_q = t["q_scale"] * (grad_q - unit * row_sum(grad_q * unit))
            grad_k = t["k_scale"] * (grad_k - k * row_sum(grad_k * k))
            at = head * channels
            for name, grad, size in (
                ("q", grad_q, key_width),
                ("k", grad_k, key_width),
                ("v", grad_v, value_width),
            ):
                pre, sig = t[name + "_slope"]
                mixed_scr[rows, at : at + size] = grad * (sig * (1.0 + pre * (1.0 - sig)))
                at += size
        step = 1
        while step < CHUNK:
            sums_grad = sums_grad + jnp.where(
                place < CHUNK - step, pltpu.roll(sums_grad, CHUNK - step, 0), 0.0
            )
            step *= 2
        rates = rates_ref[rows, :]
        log_decay, _ = decays(rates, log_rates_ref[...], bias_ref[...])
        strength = sigmoid(rates)
        inputs_grad = sums_grad * (-jnp.exp(log_rates_ref[...])) * sigmoid(rates + bias_ref[...])
        log_total = log_total + jnp.sum(sums_grad * log_decay, axis=0, keepdims=True)
        bias_total = bias_total + jnp.sum(inputs_grad, axis=0, keepdims=True)
        grads_ref[rows, heads * width :] = (
            inputs_grad + strength_grad * strength * (1.0 - strength)
        ).astype(bf16)
    grad_lanes_ref[0:1, :] = log_total
    grad_lanes_ref[1:2, :] = bias_total

    mixed_scr[length : length + 8, :] = jnp.zeros((8, mixed_scr.shape[1]), f32)
    for head in range(heads):
        columns = slice(head * channels, (head + 1) * channels)
        source = slice(head * width, head * width + channels)
        taps_here = [jnp.zeros((1, channels), f32) for _ in range(CONV)]
        for chunk in range(chunks):
            start = chunk * CHUNK
            total = None
            now = mixed_scr[start : start + CHUNK, columns]
            for tap in range(CONV):
                ahead = CONV - 1 - tap
                row = tap * heads + head
                term = taps_ref[row : row + 1, :] * (
                    mixed_scr[start + ahead : start + ahead + CHUNK, columns]
                )
                total = term if total is None else total + term
                taps_here[tap] = taps_here[tap] + jnp.sum(
                    now * shifted(project_ref, start, ahead, source), axis=0, keepdims=True
                )
            grads_ref[start : start + CHUNK, source] = total.astype(bf16)
        for tap in range(CONV):
            row = tap * heads + head
            grad_taps_ref[row : row + 1, :] = taps_here[tap]
    half = normed_ref.shape[1] // 2
    send_ref[...] = rows_dot(normed_ref[:, half:], grads_ref[...], bf16)
    if near:
        taps_to_blocks(ids_ref, grad_taps_ref, send_ref, half // LANES)


def fold_blocks(keep, got_ref, own_ref, low_refs):
    size = own_ref.shape[0]
    own_ref[...] = keep[0:size, :] + got_ref[0:size, :].astype(f32)
    for k, ref in enumerate(low_refs):
        here = slice((k + 1) * size, (k + 2) * size)
        ref[0:size, :] = (keep[here, :] + got_ref[here, :].astype(f32)).astype(bf16)


def mixer_products(near, refs):
    ids_ref, normed_ref, rows_ref, gated_ref, grads_ref, grad_gate_ref, grad_taps_ref, got_ref, mix_keep_ref = refs[:9]
    values = grad_gate_ref.shape[1]
    half = normed_ref.shape[1] // 2
    gate_keep_ref = refs[-1]
    gate_keep_ref[:, :values] = rows_dot(normed_ref[:, :half], grad_gate_ref[...])
    gate_keep_ref[:, values:] = rows_dot(rows_ref[:, :half], gated_ref[...])
    if near:
        fold_blocks(gate_keep_ref, got_ref, refs[9], refs[10:-1])
    mix_keep_ref[...] = rows_dot(normed_ref[:, :half], grads_ref[...])
    if near:
        taps_to_blocks(ids_ref, grad_taps_ref, mix_keep_ref, 0)


def mixer_rows(ids_ref, grads_ref, grad_gate_ref, mix_ref, weights_ref, send_ref, keep_ref):
    values = grad_gate_ref.shape[1]
    back = cols_dot(grads_ref[...], mix_ref[...])
    back = back + cols_dot(grad_gate_ref[...], weights_ref[:, :values])
    rows_to_blocks(ids_ref, back, send_ref, keep_ref)


def mix_fold(mix_keep_ref, mix_got_ref, gate_ref, gate_got_ref, small_ref, gate_out_ref, own_ref, *low_refs):
    fold_blocks(mix_keep_ref, mix_got_ref, own_ref, low_refs)
    size = own_ref.shape[0]
    rows, columns = small_ref.shape
    for ref in low_refs:
        ref[size:, :] = jnp.zeros((ref.shape[0] - size, ref.shape[1]), ref.dtype)
        tail = jnp.concatenate([small_ref[...], jnp.zeros((ref.shape[0] - size - rows, columns), f32)], 0)
        ref[size:, :columns] = tail.astype(ref.dtype)
    gate_out_ref[...] = gate_ref[...] + gate_got_ref[...].astype(f32)


def norm_scale(rows):
    return lax.rsqrt(jnp.mean(rows * rows, axis=1, keepdims=True) + NORM_EPS)


def prepare(ids_ref, rows_ref, grad_ref, mixer_gain_ref, ffn_gain_ref, resid_ref, both_ref, gains_ref):
    size = rows_ref.shape[0]
    count = rows_ref.shape[1] // LANES
    for place in range(count):
        at = pl.multiple_of(order_of(ids_ref, place) * LANES, LANES)
        here = slice(place * LANES, (place + 1) * LANES)
        resid_ref[:, here] = rows_ref[:, pl.ds(at, LANES)].astype(f32)
        both_ref[size:, here] = grad_ref[:, pl.ds(at, LANES)]
        gains_ref[0:1, here] = mixer_gain_ref[:, pl.ds(at, LANES)]
        gains_ref[1:2, here] = ffn_gain_ref[:, pl.ds(at, LANES)]
    resid = resid_ref[...]
    both_ref[0:size, :] = (resid * norm_scale(resid) * gains_ref[0:1, :]).astype(bf16)


def fold(keep_ref, got_ref, keep_out_ref, send_ref):
    size = send_ref.shape[0]
    keep_out_ref[...] = keep_ref[0:size, :] + got_ref[0:size, :].astype(f32)
    send_ref[...] = (keep_ref[size:, :] + got_ref[size:, :].astype(f32)).astype(bf16)


def middle_norm(keep_ref, got_ref, resid_in_ref, gains_ref, resid_ref, ffn_in_ref):
    resid = resid_in_ref[...] + keep_ref[...] + got_ref[...].astype(f32)
    resid_ref[...] = resid
    ffn_in_ref[...] = (resid * norm_scale(resid) * gains_ref[1:2, :]).astype(bf16)


def place_of(ids_ref, block, count):
    return ids_ref[1 + count + block]


def feed_forward(ids_ref, refs):
    ffn_refs, grad_refs, (weights_ref,), outs, (ffn_ref, top_ref, weights_scr) = refs
    ffn_out_ref, top_out_ref, hidden_ref, grad_gate_ref, out_send, out_keep, back_send, back_keep = outs
    size = ffn_refs[0].shape[0]
    count = ffn_ref.shape[1] // LANES
    for block in range(count):
        at = pl.multiple_of(order_of(ids_ref, block) * LANES, LANES)
        weights_scr[block * LANES : (block + 1) * LANES, :] = weights_ref[pl.ds(at, LANES), :]
    for k in range(4):
        ffn_ref[k * size : (k + 1) * size, :] = ffn_refs[k][...]
        top_ref[k * size : (k + 1) * size, :] = grad_refs[k][size:, :]
    hidden_size = hidden_ref.shape[1]
    gate_up_w = weights_scr[:, : 2 * hidden_size]
    down_w = weights_scr[:, 2 * hidden_size : 3 * hidden_size]
    gate_up = dot(ffn_ref[...], gate_up_w)
    grad_hidden = dot(top_ref[...], down_w)
    gate, up = gate_up[:, :hidden_size], gate_up[:, hidden_size:]
    sig = sigmoid(gate)
    act = gate * sig
    hidden_ref[...] = (act * up).astype(bf16)
    grad_gate_ref[:, :hidden_size] = (grad_hidden * up * (sig * (1.0 + gate * (1.0 - sig)))).astype(bf16)
    grad_gate_ref[:, hidden_size:] = (grad_hidden * act).astype(bf16)
    back = cols_dot(grad_gate_ref[...], gate_up_w)
    out = cols_dot(hidden_ref[...], down_w)
    for value, send, keep in ((back, back_send, back_keep), (out, out_send, out_keep)):
        for k in range(4):
            target = send if k % 2 else keep
            half = (k // 2) * size
            target[half : half + size, :] = value[k * size : (k + 1) * size, :].astype(target.dtype)
    for block in range(count):
        at = pl.multiple_of(place_of(ids_ref, block, count) * LANES, LANES)
        here = slice(block * LANES, (block + 1) * LANES)
        ffn_out_ref[:, here] = ffn_ref[:, pl.ds(at, LANES)]
        top_out_ref[:, here] = top_ref[:, pl.ds(at, LANES)]


def feed_finish(total_ref, gate_up_ref, down_ref):
    hidden_size = down_ref.shape[0]
    for part in range(2):
        gate_up_ref[:, part, :] = total_ref[:, part * hidden_size : (part + 1) * hidden_size].astype(f32)
    down_ref[...] = jnp.transpose(total_ref[:, 2 * hidden_size : 3 * hidden_size].astype(f32))


def feed_products(ffn_ref, top_ref, hidden_ref, grad_gate_ref, out_ref):
    hidden_size = hidden_ref.shape[1]
    out_ref[:, : 2 * hidden_size] = rows_dot(ffn_ref[...], grad_gate_ref[...], out_ref.dtype)
    out_ref[:, 2 * hidden_size : 3 * hidden_size] = rows_dot(
        top_ref[...], hidden_ref[...], out_ref.dtype
    )
    rest = out_ref.shape[1] - 3 * hidden_size
    if rest:
        out_ref[:, 3 * hidden_size :] = jnp.zeros((out_ref.shape[0], rest), out_ref.dtype)


def norm_reverse(grad, rows, gain):
    scale = norm_scale(rows)
    unit = rows * scale
    inner = grad * gain
    gain_grad = jnp.sum(grad * unit, axis=0, keepdims=True)
    return scale * (inner - unit * jnp.mean(inner * unit, axis=1, keepdims=True)), gain_grad


def middle_back(
    back_keep_ref, back_got_ref, resid_ref, both_ref, gains_ref, grad_ref, low_ref, gain_grad_ref
):
    grad_ffn_in = back_keep_ref[...] + back_got_ref[...].astype(f32)
    grad, gain_grad = norm_reverse(grad_ffn_in, resid_ref[...], gains_ref[1:2, :])
    grad = grad + both_ref[both_ref.shape[0] // 2 :, :].astype(f32)
    grad_ref[...] = grad
    low_ref[...] = grad.astype(bf16)
    gain_grad_ref[...] = gain_grad


def last_out(ids_ref, keep_ref, got_ref, resid_ref, out_ref, scr):
    scr[...] = resid_ref[...] + keep_ref[...] + got_ref[...].astype(f32)
    count = out_ref.shape[1] // LANES
    for block in range(count):
        at = pl.multiple_of(place_of(ids_ref, block, count) * LANES, LANES)
        out_ref[:, block * LANES : (block + 1) * LANES] = scr[:, pl.ds(at, LANES)].astype(bf16)


def last_grad(
    ids_ref, keep_ref, got_ref, resid_in_ref, gains_ref, grad_ref, gain_grad_ref, out_ref, gains_out_ref, scr, gain_scr
):
    grad_normed = keep_ref[...] + got_ref[...].astype(f32)
    grad, gain_grad = norm_reverse(grad_normed, resid_in_ref[...], gains_ref[0:1, :])
    scr[...] = grad + grad_ref[...]
    gain_scr[0:1, :] = gain_grad
    gain_scr[1:2, :] = gain_grad_ref[...]
    count = out_ref.shape[1] // LANES
    for block in range(count):
        at = pl.multiple_of(place_of(ids_ref, block, count) * LANES, LANES)
        here = slice(block * LANES, (block + 1) * LANES)
        out_ref[:, here] = scr[:, pl.ds(at, LANES)]
        gains_out_ref[:, here] = gain_scr[:, pl.ds(at, LANES)]


def call(kernel, outs, operands, scratch=(), name=None, scalar=True):
    specs = [pl.BlockSpec(memory_space=pltpu.VMEM)] * len(operands)
    if scalar:
        specs[0] = pl.BlockSpec(memory_space=pltpu.SMEM)
    return pl.pallas_call(
        kernel,
        out_shape=tuple(jax.ShapeDtypeStruct(shape, kind) for shape, kind in outs),
        in_specs=specs,
        out_specs=tuple([pl.BlockSpec(memory_space=pltpu.VMEM)] * len(outs)),
        scratch_shapes=[pltpu.VMEM(shape, kind) for shape, kind in scratch],
        compiler_params=pltpu.CompilerParams(vmem_limit_bytes=56 * 2**20),
        name=name,
    )(*operands)


def cut_list(items, sizes):
    parts, at = [], 0
    for size in sizes:
        parts.append(items[at : at + size])
        at += size
    return parts


def run_forward(near, ids, rows, mix, taps, log_rates, bias, value_width):
    length = rows[0].shape[0] // 2 * len(rows)
    model = rows[0].shape[1]
    wide = mix[0].shape[1]
    columns = wide - LANES
    channels = taps.shape[1]
    heads = taps.shape[0] // CONV
    key_width = (channels - value_width) // 2
    pair = (length // CHUNK, heads)
    values = heads * value_width

    def kernel(*refs):
        mixer_forward(near, cut_list(refs, (4, len(rows), len(mix), 9, 5)))

    return call(
        kernel,
        (
            ((length, columns), f32),
            ((length, LANES), f32),
            ((length, values), f32),
            (pair + (key_width, value_width), f32),
            ((length, values), f32),
            (pair + (CHUNK, CHUNK), f32),
            ((length, model), bf16),
            ((model, wide), bf16),
            (taps.shape, f32),
        ),
        (ids, taps, log_rates, bias, *rows, *mix),
        (
            (pair + (CHUNK, key_width), bf16),
            (pair + (CHUNK, key_width), f32),
            (pair + (CHUNK, CHUNK), bf16),
            (pair + (CHUNK, key_width), bf16),
            (pair + (CHUNK, value_width), f32),
        ),
        "mixer_forward",
    )


def run_backward(near, ids, grad_out, log_rates, bias, kept):
    project, _, out, states, _, _, normed, mix, taps = kept
    length, model = normed.shape
    values = out.shape[1]
    wide = mix.shape[1]
    heads, key_width, value_width = states.shape[1:]
    pair = (length // CHUNK, heads)

    def kernel(*refs):
        mixer_backward(near, cut_list(refs, (4, len(kept), 4, 7)))

    return call(
        kernel,
        (
            ((length, wide), bf16),
            (taps.shape, f32),
            ((2, LANES), f32),
            ((model // 2, wide), bf16),
        ),
        (ids, log_rates, bias, grad_out, *kept),
        (
            (pair + (key_width, value_width), f32),
            ((length, values), f32),
            (pair + (CHUNK, key_width), bf16),
            (pair + (CHUNK, key_width), bf16),
            (pair + (CHUNK, CHUNK), bf16),
            (pair + (CHUNK, key_width), bf16),
            ((length + 8, heads * taps.shape[1]), f32),
        ),
        "mixer_backward",
    )


def swap(array, axis, size, offset):
    return lax.ppermute(array, axis, [(i, i ^ offset) for i in range(size)])


def after(arrays, others):
    kept, _ = lax.optimization_barrier((arrays, others))
    return kept


def per_device(
    layer_in,
    mixer_gain,
    w_mix,
    w_rates,
    conv_taps,
    a_log,
    dt_bias,
    head_gain,
    w_out,
    ffn_gain,
    w_gate_up,
    w_down,
    out_grad,
):
    size = lax.axis_size("dp")
    ranks = lax.axis_size("tensor")
    depth, heads, width = w_mix.shape
    model = layer_in.shape[1]
    hidden = w_gate_up.shape[2]
    value_size = w_out.shape[0]
    rows = layer_in.shape[0]
    taps_shape = conv_taps.shape
    part = taps_shape[2]
    near = size == 8 and depth == LANES and 2 * part == LANES
    half = size // 2
    rank, own = lax.axis_index("tensor"), lax.axis_index("dp")
    blocks = model // LANES
    if near:
        offsets = [2 * p for p in range(half)] + [2 * p + 1 for p in range(half)]
        order = own ^ jnp.array(offsets, jnp.int32)
        places = [offsets.index(k) for k in range(size)]
        index = own ^ jnp.arange(size, dtype=jnp.int32)
        place = jnp.where(index % 2 == 0, index // 2, half + index // 2)
        assert places == [k // 2 if k % 2 == 0 else half + k // 2 for k in range(size)]
    else:
        order = place = jnp.arange(blocks, dtype=jnp.int32)
    ids = jnp.concatenate([jnp.full((1,), rank, jnp.int32), order, place])

    def near_z(shard):
        return [shard] + [swap(shard, "dp", size, 2 * p) for p in range(1, half)]

    def near_x(shards, own_side):
        return [own_side, swap(jnp.concatenate(shards[1:], 0), "dp", size, 1)]

    def far(shard):
        return lax.all_gather(shard, "dp", axis=0, tiled=True)

    def rows_y(block):
        return swap(block, "tensor", ranks, 2)

    def rows_core(block):
        return swap(block, "tensor", ranks, 1)

    def gather_rows(block):
        across = rows_y(block)
        return [block, rows_core(block), across, rows_core(across)]

    def sum_rows(send, keep, name):
        got = rows_core(send)
        shape = (rows, model)
        keep, send = call(fold, ((shape, f32), (shape, bf16)), (keep, got), name=name, scalar=False)
        return keep, rows_y(send)

    channels = width - head_gain.shape[0]
    values = value_size
    rates_tile = jnp.pad(w_rates.reshape(depth, 2 * heads), ((0, 0), (0, LANES - 2 * heads)))
    if near:
        taps_tile = conv_taps.reshape(CONV * heads, part)
        taps_tile = jnp.pad(taps_tile, ((0, depth - CONV * heads), (LANES - part, 0)))
        rates_tile = rates_tile + taps_tile
    mix_shard = jnp.concatenate(
        [w_mix[:, :, :channels].reshape(depth, heads * channels), rates_tile], 1
    )
    gate_shard = jnp.concatenate([w_mix[:, :, channels:].reshape(depth, values), w_out.T], 1)
    filler = -3 * hidden % LANES
    ffn_shard = jnp.concatenate(
        [w_gate_up.reshape(depth, 2 * hidden), w_down.T, jnp.zeros((depth, filler), bf16)], 1
    )

    if near:
        mix_z = near_z(mix_shard)
        mix_side = swap(mix_shard, "dp", size, 1)
    square = (rows, model)
    resid_in, both, gains = call(
        prepare,
        ((square, f32), ((2 * rows, model), bf16), ((2, model), f32)),
        (ids, layer_in, out_grad, mixer_gain.reshape(1, -1), ffn_gain.reshape(1, -1)),
        name="prepare",
    )
    ffn_full = far(after(ffn_shard, (mix_z, mix_side)) if near else ffn_shard)
    both_all = gather_rows(both)
    if near:
        gate_shard = after(gate_shard, (mix_z, mix_side, both))
        gate_z = near_z(gate_shard)
        gate_side = swap(gate_shard, "dp", size, 1)
        mix_slots = mix_z + near_x(mix_z, mix_side)
        taps = jnp.zeros((CONV * heads, part * size), f32)
    else:
        mix_slots = [far(mix_shard)]
        gate_slots = [far(gate_shard)]
        taps = lax.all_gather(conv_taps, "dp", axis=2, tiled=True).astype(f32)
        taps = taps.reshape(CONV * heads, part * size)

    first_head = rank * heads

    def on_lanes(per_head):
        here = lax.dynamic_slice_in_dim(per_head, first_head, heads)
        pairs = jnp.stack([here, jnp.zeros_like(here)], 1).reshape(1, -1)
        return jnp.pad(pairs, ((0, 0), (0, LANES - pairs.shape[1])))

    def off_lanes(row):
        here = row[: 2 * heads : 2]
        return lax.dynamic_update_slice_in_dim(jnp.zeros_like(a_log), here, first_head, 0)

    lanes = (on_lanes(a_log), on_lanes(dt_bias))
    gain_row = head_gain.reshape(1, -1)
    kept = run_forward(near, ids, both_all, mix_slots, taps, *lanes, head_gain.shape[0])
    heads_out, normed_rows, mix_full = kept[2], kept[6], kept[7]
    if near:
        gate_slots = gate_z + near_x(gate_z, gate_side)
    tokens = rows * ranks
    block_pair = (2 * rows, model)
    gated, gate, gate_full, out_send, out_keep = call(
        out_product,
        (
            ((tokens, values), bf16),
            ((tokens, values), f32),
            ((model, 2 * values), bf16),
            (block_pair, bf16),
            (block_pair, f32),
        ),
        (ids, gain_row, normed_rows, heads_out, *gate_slots),
        (),
        "out_product",
    )
    out_keep, out_got = sum_rows(out_send, out_keep, "out_fold")
    resid, ffn_in = call(
        middle_norm, ((square, f32), (square, bf16)), (out_keep, out_got, resid_in, gains), name="middle_norm", scalar=False
    )
    ffn_all = gather_rows(ffn_in)

    def ffn_kernel(ids_ref, *refs):
        feed_forward(ids_ref, cut_list(refs, (4, 4, 1, 8, 3)))

    ffn_rows, top_rows, hidden_low, grad_gate, ffn_send, ffn_keep, back_send, back_keep = call(
        ffn_kernel,
        (
            ((tokens, model), bf16),
            ((tokens, model), bf16),
            ((tokens, hidden), bf16),
            ((tokens, 2 * hidden), bf16),
            (block_pair, bf16),
            (block_pair, f32),
            (block_pair, bf16),
            (block_pair, f32),
        ),
        (ids, *ffn_all, *both_all, ffn_full),
        (((tokens, model), bf16), ((tokens, model), bf16), (ffn_full.shape, bf16)),
        "feed_forward",
    )
    split = model // 2

    def scatter_x(send):
        return swap(send, "dp", size, 1) if near else send

    back_keep, back_got = sum_rows(back_send, back_keep, "back_fold")
    (ffn_grads,) = call(
        feed_products,
        (((model, 3 * hidden + filler), bf16 if near else f32),),
        (ffn_rows, top_rows, hidden_low, grad_gate),
        name="feed_products",
        scalar=False,
    )
    ffn_total = lax.psum_scatter(ffn_grads, "dp", scatter_dimension=0, tiled=True)
    grad_resid, mix_low, ffn_gain_grad = call(
        middle_back,
        ((square, f32), (square, bf16), ((1, model), f32)),
        (back_keep, back_got, resid, both, gains),
        name="middle_back",
        scalar=False,
    )
    mix_all = gather_rows(mix_low)
    ffn_keep, ffn_got = sum_rows(ffn_send, ffn_keep, "ffn_fold")
    (layer_out,) = call(
        last_out, ((square, bf16),), (ids, ffn_keep, ffn_got, resid), ((square, f32),), "last_out"
    )
    mix_all, layer_out = lax.optimization_barrier((mix_all, layer_out))
    grad_rows, grad_out, gate_grad, head_gain_grad, gate_send = call(
        gate_back,
        (
            ((tokens, model), bf16),
            ((tokens, values), f32),
            ((tokens, values), bf16),
            (gain_row.shape, f32),
            ((split, 2 * values), bf16),
        ),
        (ids, gain_row, normed_rows, heads_out, gated, gate, gate_full, *mix_all),
        (),
        "gate_back",
    )
    gate_got = scatter_x(gate_send)
    grads, taps_grad, lanes_grad, mix_send = run_backward(near, ids, grad_out, *lanes, kept)
    mix_got = scatter_x(mix_send)

    def products_kernel(*refs):
        mixer_products(near, refs)

    def blocks_of(send, more=0):
        columns = send.shape[1]
        return (((depth, columns), f32),) + (((depth + more, columns), bf16),) * (half - 1)

    keep_shape = ((split, 2 * values), f32)
    norm_send, norm_keep = call(
        mixer_rows,
        ((block_pair, bf16), (block_pair, f32)),
        (ids, grads, gate_grad, mix_full, gate_full),
        name="mixer_rows",
    )
    norm_got = rows_core(norm_send)
    norm_keep, norm_send = call(
        fold, ((square, f32), (square, bf16)), (norm_keep, norm_got), name="norm_fold", scalar=False
    )
    gate_got, norm_send = lax.optimization_barrier((gate_got, norm_send))
    norm_got = rows_y(norm_send)
    mix_keep, *gate_parts = call(
        products_kernel,
        ((mix_send.shape, f32),) + (blocks_of(gate_send) if near else (keep_shape,)),
        (ids, normed_rows, grad_rows, gated, grads, gate_grad, taps_grad, gate_got),
        (keep_shape,) if near else (),
        "mixer_products",
    )

    def far_sum(parts, got):
        if near:
            own, lows = parts[0], parts[1:]
            return [own] + [swap(low, "dp", size, 2 * (p + 1)) for p, low in enumerate(lows)]
        return [
            lax.psum_scatter(
                jnp.concatenate([parts[0], got.astype(f32)], 0), "dp", scatter_dimension=0, tiled=True
            )
        ]

    def add_up(blocks):
        total = blocks[0]
        for block in blocks[1:]:
            total = total + block.astype(f32)
        return total

    gate_blocks = far_sum(gate_parts, gate_got)
    in_grad, gains_grad = call(
        last_grad,
        ((square, f32), ((2, model), f32)),
        (ids, norm_keep, norm_got, resid_in, gains, grad_resid, ffn_gain_grad),
        ((square, f32), ((2, model), f32)),
        "last_grad",
    )

    small = jnp.concatenate(
        [
            gains_grad.reshape(-1),
            head_gain_grad.reshape(-1),
            off_lanes(lanes_grad[0]),
            off_lanes(lanes_grad[1]),
        ]
    )
    length = small.size
    small = jnp.pad(small, (0, -length % (8 * LANES))).reshape(8, -1)
    mix_parts = [mix_keep]
    for offset in (1, 2):
        small = small + swap(small, "tensor", ranks, offset)
    mix_parts = [mix_keep]
    if near:
        small = small + swap(small, "dp", size, 1)
        gate_sum, *mix_parts = call(
            mix_fold,
            (((depth, 2 * values), f32),) + blocks_of(mix_send, 16),
            (mix_keep, mix_got, gate_blocks[0], gate_blocks[1], small),
            name="mix_fold",
            scalar=False,
        )
        gate_blocks = [gate_sum] + gate_blocks[2:]
    mix_blocks = far_sum(mix_parts, mix_got)
    grad_w_gate_up, grad_w_down = call(
        feed_finish,
        ((w_gate_up.shape, f32), (w_down.shape, f32)),
        (ffn_total,),
        name="feed_finish",
        scalar=False,
    )
    own_block, grad_w_gate_up, grad_w_down = lax.optimization_barrier(
        (mix_blocks[0], grad_w_gate_up, grad_w_down)
    )
    mix_blocks = [own_block] + mix_blocks[1:]

    if near:
        small = add_up([small] + [got[depth : depth + 8, : small.shape[1]] for got in mix_blocks[1:]])
        mix_blocks = [mix_blocks[0]] + [got[:depth] for got in mix_blocks[1:]]
    else:
        small = lax.psum(small, "dp")
    small = small.reshape(-1)[:length]
    grad_mixer_gain, grad_ffn_gain = small[:model], small[model : 2 * model]
    small = small[2 * model :]
    grad_head_gain, small = small[: head_gain.size], small[head_gain.size :]
    grad_a_log, grad_dt_bias = small[: a_log.size], small[a_log.size :]

    gate_total = add_up(gate_blocks)
    mix_total = add_up(mix_blocks)
    grad_w_mix = jnp.concatenate(
        [
            mix_total[:, : heads * channels].reshape(depth, heads, channels),
            gate_total[:, :values].reshape(depth, heads, -1),
        ],
        2,
    )
    grad_w_rates = mix_total[:, heads * channels : heads * channels + 2 * heads].reshape(w_rates.shape)
    if near:
        grad_taps = mix_total[: CONV * heads, mix_total.shape[1] - part :].reshape(taps_shape)
    else:
        grad_taps = lax.psum_scatter(
            taps_grad.reshape(CONV, heads, -1), "dp", scatter_dimension=2, tiled=True
        )
    return (
        layer_out,
        in_grad,
        grad_mixer_gain,
        grad_w_mix,
        grad_w_rates,
        grad_taps,
        grad_a_log,
        grad_dt_bias,
        grad_head_gain,
        gate_total[:, values:].T,
        grad_ffn_gain,
        grad_w_gate_up,
        grad_w_down,
    )


def solution(mesh):
    return jax.shard_map(
        per_device,
        mesh=mesh,
        in_specs=(
            P(("dp", "tensor"), None),
            P(),
            P("dp", "tensor", None),
            P("dp", "tensor", None),
            P(None, "tensor", "dp"),
            P(),
            P(),
            P(),
            P("tensor", "dp"),
            P(),
            P("dp", None, "tensor"),
            P("tensor", "dp"),
            P(("dp", "tensor"), None),
        ),
        out_specs=(
            P(("dp", "tensor"), None),
            P(("dp", "tensor"), None),
            P(),
            P("dp", "tensor", None),
            P("dp", "tensor", None),
            P(None, "tensor", "dp"),
            P(),
            P(),
            P(),
            P("tensor", "dp"),
            P(),
            P("dp", None, "tensor"),
            P("tensor", "dp"),
        ),
        check_vma=False,
    )
```

```python
import jax
import jax.numpy as jnp
from jax import lax
from jax.experimental import pallas as pl
from jax.experimental.pallas import tpu as pltpu
from jax.sharding import PartitionSpec as P

CONV = 4


highest = lax.Precision.HIGHEST
NORM_EPS = 1e-05
UNIT_EPS = 1e-06
bf16 = jnp.bfloat16
f32 = jnp.float32


def rows_dot(left, right, kind=f32):
    return lax.dot_general(
        left, right, (((0,), (0,)), ((), ())), preferred_element_type=f32
    ).astype(kind)


def cols_dot(left, right):
    return lax.dot_general(left, right, (((1,), (1,)), ((), ())), preferred_element_type=f32)


def dot(left, right):
    return jnp.dot(left, right, preferred_element_type=f32)


CHUNK = 128
LANES = 128


def mul(left, right, over=(1, 0), exact=False):
    dims = (((over[0],), (over[1],)), ((), ()))
    if exact:
        return lax.dot_general(left, right, dims, precision=highest, preferred_element_type=f32)
    return lax.dot_general(left.astype(bf16), right.astype(bf16), dims, preferred_element_type=f32)


def square_ids():
    shape = (CHUNK, CHUNK)
    return lax.broadcasted_iota(jnp.int32, shape, 0), lax.broadcasted_iota(jnp.int32, shape, 1)


def sigmoid(v):
    return 1.0 / (1.0 + jnp.exp(-v))


def softplus(v):
    return jnp.maximum(v, 0.0) + jnp.log1p(jnp.exp(-jnp.abs(v)))


def row_sum(v):
    return jnp.sum(v, axis=1, keepdims=True)


def unit_inverse(lower):
    rows, cols = square_ids()
    inverse = jnp.where(rows == cols, 1.0, 0.0)
    block = 1
    while block < CHUNK:
        corner = (
            (rows // (2 * block) == cols // (2 * block))
            & ((rows // block) % 2 == 1)
            & ((cols // block) % 2 == 0)
        )
        part = jnp.where(corner, lower, 0.0)
        if block == 1:
            inverse = inverse - part
        else:
            inverse = inverse - mul(mul(inverse, part), inverse)
        block *= 2
    return inverse


def shifted(ref, start, back, columns):
    if start == 0 and back:
        rows = lax.broadcasted_iota(jnp.int32, (CHUNK, columns.stop - columns.start), 0)
        return jnp.where(rows >= back, pltpu.roll(ref[0:CHUNK, columns], back, 0), 0.0)
    return ref[start - back : start - back + CHUNK, columns]


def short_conv(project_ref, taps_ref, start, head, heads, columns, tap_columns):
    total = None
    for tap in range(CONV):
        row = tap * heads + head
        term = taps_ref[row : row + 1, tap_columns] * shifted(
            project_ref, start, CONV - 1 - tap, columns
        )
        total = term if total is None else total + term
    return total


def decays(rates, log_rates, bias):
    log_decay = -jnp.exp(log_rates) * softplus(rates + bias)
    place = lax.broadcasted_iota(jnp.int32, rates.shape, 0)
    total = log_decay
    step = 1
    while step < CHUNK:
        total = total + jnp.where(place >= step, pltpu.roll(total, step, 0), 0.0)
        step *= 2
    return log_decay, total


def chunk_terms(head, project_ref, taps_ref, start, total, total_rows, strength, key_width, value_width):
    width = 2 * key_width + value_width
    base = head * width
    heads = project_ref.shape[1] // width
    terms = {}
    parts = (("q", 0, key_width), ("k", key_width, key_width), ("v", 2 * key_width, value_width))
    for name, at, size in parts:
        pre = short_conv(
            project_ref,
            taps_ref,
            start,
            head,
            heads,
            slice(base + at, base + at + size),
            slice(at, at + size),
        )
        gate = sigmoid(pre)
        mixed = pre * gate
        if name != "v":
            scale = lax.rsqrt(row_sum(mixed * mixed) + UNIT_EPS)
            mixed = mixed * scale
            terms[name + "_scale"] = scale
        terms[name + "_slope"] = (pre, gate)
        terms[name] = mixed
    terms["unit_q"] = terms["q"]
    terms["q"] = terms["q"] * key_width ** (-0.5)
    lane = 2 * head
    sums = total[:, lane : lane + 1]
    across = total_rows[lane : lane + 1, :]
    rows, cols = square_ids()
    decay = jnp.where(rows >= cols, jnp.exp(jnp.minimum(sums - across, 0.0)), 0.0)
    final = total[CHUNK - 1 : CHUNK, lane : lane + 1]
    terms["b"] = strength[:, lane + 1 : lane + 2]
    terms["since"] = jnp.exp(sums)
    terms["remaining"] = jnp.exp(final - sums)
    terms["through"] = jnp.exp(final)
    terms["decay"] = decay
    terms["dots"] = mul(terms["k"], terms["k"], (1, 1)) * jnp.where(rows > cols, decay, 0.0)
    terms["scores"] = mul(terms["q"], terms["k"], (1, 1)) * decay
    return terms


def stack_rows(refs, target, column):
    at = 0
    for ref in refs:
        rows = ref.shape[0]
        columns = min(ref.shape[1], target.shape[1] - column)
        target[at : at + rows, column : column + columns] = ref[:, :columns]
        at += rows


def rows_in_time(ids_ref, refs, target):
    size = target.shape[0] // len(refs)
    for k, ref in enumerate(refs):
        at = pl.multiple_of((ids_ref[0] ^ k) * size, size)
        target[pl.ds(at, size), :] = ref[0:size, :]


def order_of(ids_ref, place):
    return ids_ref[1 + place]


def taps_from_blocks(ids_ref, mix_ref, shape):
    rows, channels = shape
    count = mix_ref.shape[0] // LANES
    part = channels // count
    lane = lax.broadcasted_iota(jnp.int32, shape, 1)
    total = jnp.zeros(shape, f32)
    for place in range(count):
        block = mix_ref[place * LANES : place * LANES + 16, mix_ref.shape[1] - LANES :]
        block = block.astype(f32)[0:rows, LANES - part :]
        wide = jnp.concatenate([block] * count, 1)
        total = total + jnp.where(lane // part == order_of(ids_ref, place), wide, 0.0)
    return total


def taps_to_blocks(ids_ref, taps_ref, target, first):
    rows, channels = taps_ref.shape
    count = target.shape[0] // LANES
    part = channels // (2 * count)
    for place in range(count):
        owner = order_of(ids_ref, first + place)
        block = jnp.zeros((rows, part), f32)
        for other in range(2 * count):
            block = block + jnp.where(
                owner == other, taps_ref[:, other * part : (other + 1) * part], 0.0
            )
        block = jnp.concatenate([jnp.zeros((rows, LANES - part), f32), block], 1)
        block = jnp.concatenate([block, jnp.zeros((16 - rows, LANES), f32)], 0)
        at = (slice(place * LANES, place * LANES + 16), slice(target.shape[1] - LANES, target.shape[1]))
        target[at] = (target[at].astype(f32) + block).astype(target.dtype)


def rows_to_blocks(ids_ref, value, send_ref, keep_ref):
    size = value.shape[0] // 4
    for k in range(4):
        target = send_ref if k % 2 else keep_ref
        half = (k // 2) * size
        for block in range(4):

            @pl.when((ids_ref[0] ^ k) == block)
            def _(block=block, half=half, target=target):
                target[half : half + size, :] = value[block * size : (block + 1) * size, :].astype(
                    target.dtype
                )


def mixer_forward(near, refs):
    (ids_ref, taps_in_ref, log_rates_ref, bias_ref), row_refs, mix_refs, outs, scratch = refs
    project_ref, rates_ref, out_ref, states_ref, carried_ref, inverse_ref = outs[:6]
    normed_ref, mix_ref, taps_ref = outs[6:]
    q_scr, kr_scr, p_scr, w_scr, u_scr = scratch
    length = normed_ref.shape[0]
    heads = states_ref.shape[1]
    key_width, value_width = states_ref.shape[2:]
    width = project_ref.shape[1] // heads
    chunks = length // CHUNK
    rows_in_time(ids_ref, row_refs, normed_ref)
    stack_rows(mix_refs, mix_ref, 0)
    if near:
        taps_ref[...] = taps_from_blocks(ids_ref, mix_ref, taps_in_ref.shape)
    else:
        taps_ref[...] = taps_in_ref[...]
    for head in range(heads):
        columns = slice(head * width, (head + 1) * width)
        project_ref[:, columns] = dot(normed_ref[...], mix_ref[:, columns])
    rates_ref[...] = dot(normed_ref[...], mix_ref[:, heads * width :])
    through = {}
    for chunk in range(chunks):
        start = chunk * CHUNK
        rows = slice(start, start + CHUNK)
        rates = rates_ref[rows, :]
        _, total = decays(rates, log_rates_ref[...], bias_ref[...])
        strength = sigmoid(rates)
        total_rows = jnp.transpose(total)
        for head in range(heads):
            t = chunk_terms(
                head, project_ref, taps_ref, start, total, total_rows, strength, key_width, value_width
            )
            inverse = unit_inverse(t["b"] * t["dots"])
            inverse_ref[chunk, head] = inverse
            side = jnp.concatenate([(t["b"] * t["since"]) * t["k"], t["b"] * t["v"]], 1)
            solved = mul(inverse, side)
            w_scr[chunk, head] = solved[:, :key_width].astype(bf16)
            u_scr[chunk, head] = solved[:, key_width:]
            q_scr[chunk, head] = (t["q"] * t["since"]).astype(bf16)
            kr_scr[chunk, head] = t["k"] * t["remaining"]
            p_scr[chunk, head] = t["scores"].astype(bf16)
            through[chunk, head] = t["through"]
    state = [jnp.zeros((key_width, value_width), f32) for _ in range(heads)]
    for chunk in range(chunks):
        rows = slice(chunk * CHUNK, (chunk + 1) * CHUNK)
        for head in range(heads):
            columns = slice(head * value_width, (head + 1) * value_width)
            states_ref[chunk, head] = state[head]
            low = state[head].astype(bf16)
            carried = u_scr[chunk, head] - mul(w_scr[chunk, head], low)
            carried_ref[rows, columns] = carried
            out_ref[rows, columns] = mul(q_scr[chunk, head], low) + mul(p_scr[chunk, head], carried)
            state[head] = through[chunk, head] * state[head] + mul(
                kr_scr[chunk, head], carried, (0, 0), exact=True
            )


def out_product(ids_ref, gain_ref, normed_ref, out_ref, *refs):
    weight_refs, (gated_ref, gate_ref, weights_ref, send_ref, keep_ref) = refs[:-5], refs[-5:]
    value_width = gain_ref.shape[1]
    values = out_ref.shape[1]
    stack_rows(weight_refs, weights_ref, 0)
    for head in range(values // value_width):
        columns = slice(head * value_width, (head + 1) * value_width)
        gate = dot(normed_ref[...], weights_ref[:, columns])
        gate_ref[:, columns] = gate
        out = out_ref[:, columns]
        scale = lax.rsqrt(row_sum(out * out) / value_width + NORM_EPS)
        gated_ref[:, columns] = (out * scale * gain_ref[...] * (gate * sigmoid(gate))).astype(bf16)
    rows_to_blocks(ids_ref, cols_dot(gated_ref[...], weights_ref[:, values:]), send_ref, keep_ref)


def gate_back(ids_ref, gain_ref, normed_ref, out_ref, gated_ref, gate_ref, weights_ref, *refs):
    row_refs, (rows_ref, grad_out_ref, grad_gate_ref, gain_grad_ref, send_ref) = refs[:-5], refs[-5:]
    value_width = gain_ref.shape[1]
    values = out_ref.shape[1]
    rows_in_time(ids_ref, row_refs, rows_ref)
    gain = gain_ref[...]
    gain_total = jnp.zeros((1, value_width), f32)
    for head in range(values // value_width):
        columns = slice(head * value_width, (head + 1) * value_width)
        grad = dot(rows_ref[...], weights_ref[:, values + head * value_width : values + (head + 1) * value_width])
        out, gate = out_ref[:, columns], gate_ref[:, columns]
        scale = lax.rsqrt(row_sum(out * out) / value_width + NORM_EPS)
        unit = out * scale
        sig = sigmoid(gate)
        act = gate * sig
        gain_total = gain_total + jnp.sum(grad * unit * act, axis=0, keepdims=True)
        grad_gate_ref[:, columns] = (
            grad * gain * unit * (sig * (1.0 + gate * (1.0 - sig)))
        ).astype(bf16)
        inner = grad * act * gain
        grad_out_ref[:, columns] = scale * (inner - unit * (row_sum(inner * unit) / value_width))
    gain_grad_ref[...] = gain_total
    half = normed_ref.shape[1] // 2
    send_ref[:, :values] = rows_dot(normed_ref[:, half:], grad_gate_ref[...], bf16)
    send_ref[:, values:] = rows_dot(rows_ref[:, half:], gated_ref[...], bf16)


def mixer_backward(near, refs):
    (ids_ref, log_rates_ref, bias_ref, grad_out_scr), kept, outs, scratch = refs
    (
        project_ref,
        rates_ref,
        out_ref,
        states_ref,
        carried_ref,
        inverse_ref,
        normed_ref,
        _,
        taps_ref,
    ) = kept
    grads_ref, grad_taps_ref, grad_lanes_ref, send_ref = outs
    back_scr, grad_carried_scr, q_scr, kr_scr, p_scr, w_scr, mixed_scr = scratch
    length = normed_ref.shape[0]
    heads = states_ref.shape[1]
    key_width, value_width = states_ref.shape[2:]
    width = channels = project_ref.shape[1] // heads
    chunks = length // CHUNK

    def gather_terms(chunk):
        start = chunk * CHUNK
        rates = rates_ref[start : start + CHUNK, :]
        _, total = decays(rates, log_rates_ref[...], bias_ref[...])
        strength = sigmoid(rates)
        total_rows = jnp.transpose(total)
        return [
            chunk_terms(
                head, project_ref, taps_ref, start, total, total_rows, strength, key_width, value_width
            )
            for head in range(heads)
        ]

    through = {}
    for chunk in range(chunks):
        rows = slice(chunk * CHUNK, (chunk + 1) * CHUNK)
        terms = gather_terms(chunk)
        for head in range(heads):
            columns = slice(head * value_width, (head + 1) * value_width)
            t = terms[head]
            w_scr[chunk, head] = mul(
                inverse_ref[chunk, head], (t["b"] * t["since"]) * t["k"]
            ).astype(bf16)
            q_scr[chunk, head] = (t["q"] * t["since"]).astype(bf16)
            kr_scr[chunk, head] = (t["k"] * t["remaining"]).astype(bf16)
            p_scr[chunk, head] = t["scores"].astype(bf16)
            through[chunk, head] = t["through"]

    back = [jnp.zeros((key_width, value_width), f32) for _ in range(heads)]
    for chunk in reversed(range(chunks)):
        rows = slice(chunk * CHUNK, (chunk + 1) * CHUNK)
        for head in range(heads):
            columns = slice(head * value_width, (head + 1) * value_width)
            back_scr[chunk, head] = back[head]
            grad_out = grad_out_scr[rows, columns].astype(bf16)
            grad_carried = mul(p_scr[chunk, head], grad_out, (0, 0)) + mul(
                kr_scr[chunk, head], back[head]
            )
            grad_carried_scr[rows, columns] = grad_carried
            back[head] = (
                through[chunk, head] * back[head]
                + mul(q_scr[chunk, head], grad_out, (0, 0))
                - mul(w_scr[chunk, head], grad_carried, (0, 0))
            )

    rows_at, cols_at = square_ids()
    lane = lax.broadcasted_iota(jnp.int32, (CHUNK, LANES), 1)
    place = lax.broadcasted_iota(jnp.int32, (CHUNK, LANES), 0)
    log_total = jnp.zeros((1, LANES), f32)
    bias_total = jnp.zeros((1, LANES), f32)
    for chunk in range(chunks):
        rows = slice(chunk * CHUNK, (chunk + 1) * CHUNK)
        terms = gather_terms(chunk)
        sums_grad = jnp.zeros((CHUNK, LANES), f32)
        strength_grad = jnp.zeros((CHUNK, LANES), f32)
        for head in range(heads):
            columns = slice(head * value_width, (head + 1) * value_width)
            t = terms[head]
            b, since, remaining, decay = t["b"], t["since"], t["remaining"], t["decay"]
            q, k, v = t["q"], t["k"], t["v"]
            state = states_ref[chunk, head]
            back_now = back_scr[chunk, head]
            carried = carried_ref[rows, columns]
            grad_out = grad_out_scr[rows, columns]
            grad_side = mul(inverse_ref[chunk, head], grad_carried_scr[rows, columns], (0, 0))
            strict = jnp.where(rows_at > cols_at, -mul(grad_side, carried, (1, 1)), 0.0)
            grad_scores = mul(grad_out, carried, (1, 1))
            side_state = mul(grad_side, state, (1, 1))
            out_state = since * mul(grad_out, state, (1, 1))
            carried_back = remaining * mul(carried, back_now, (1, 1))
            key_side = since * row_sum(k * side_state)
            strict_dots = strict * t["dots"]
            grad_strength = row_sum(grad_side * v) - key_side + row_sum(strict_dots)
            pulls = grad_scores * t["scores"] + b * strict_dots
            key_back = row_sum(k * carried_back)
            grad_sums = (
                row_sum(pulls - jnp.transpose(pulls))
                - b * key_side
                + row_sum(q * out_state)
                - key_back
            )
            final = jnp.sum(key_back, axis=0, keepdims=True) + t["through"] * jnp.sum(
                row_sum(back_now * state), axis=0, keepdims=True
            )
            scores_low = (grad_scores * decay).astype(bf16)
            strict_low = (strict * (b * decay)).astype(bf16)
            k_low, q_low = k.astype(bf16), q.astype(bf16)
            grad_q = out_state + mul(scores_low, k_low)
            grad_k = (
                carried_back
                - (b * since) * side_state
                + mul(scores_low, q_low, (0, 0))
                + mul(strict_low, k_low)
                + mul(strict_low, k_low, (0, 0))
            )
            grad_v = b * grad_side
            sums_grad = sums_grad + jnp.where(
                lane == 2 * head, grad_sums + jnp.where(place == CHUNK - 1, final, 0.0), 0.0
            )
            strength_grad = strength_grad + jnp.where(lane == 2 * head + 1, grad_strength, 0.0)
            grad_q = grad_q * key_width ** (-0.5)
            unit = t["unit_q"]
            grad_q = t["q_scale"] * (grad_q - unit * row_sum(grad_q * unit))
            grad_k = t["k_scale"] * (grad_k - k * row_sum(grad_k * k))
            at = head * channels
            for name, grad, size in (
                ("q", grad_q, key_width),
                ("k", grad_k, key_width),
                ("v", grad_v, value_width),
            ):
                pre, sig = t[name + "_slope"]
                mixed_scr[rows, at : at + size] = grad * (sig * (1.0 + pre * (1.0 - sig)))
                at += size
        step = 1
        while step < CHUNK:
            sums_grad = sums_grad + jnp.where(
                place < CHUNK - step, pltpu.roll(sums_grad, CHUNK - step, 0), 0.0
            )
            step *= 2
        rates = rates_ref[rows, :]
        log_decay, _ = decays(rates, log_rates_ref[...], bias_ref[...])
        strength = sigmoid(rates)
        inputs_grad = sums_grad * (-jnp.exp(log_rates_ref[...])) * sigmoid(rates + bias_ref[...])
        log_total = log_total + jnp.sum(sums_grad * log_decay, axis=0, keepdims=True)
        bias_total = bias_total + jnp.sum(inputs_grad, axis=0, keepdims=True)
        grads_ref[rows, heads * width :] = (
            inputs_grad + strength_grad * strength * (1.0 - strength)
        ).astype(bf16)
    grad_lanes_ref[0:1, :] = log_total
    grad_lanes_ref[1:2, :] = bias_total

    mixed_scr[length : length + 8, :] = jnp.zeros((8, mixed_scr.shape[1]), f32)
    for head in range(heads):
        columns = slice(head * channels, (head + 1) * channels)
        source = slice(head * width, head * width + channels)
        taps_here = [jnp.zeros((1, channels), f32) for _ in range(CONV)]
        for chunk in range(chunks):
            start = chunk * CHUNK
            total = None
            now = mixed_scr[start : start + CHUNK, columns]
            for tap in range(CONV):
                ahead = CONV - 1 - tap
                row = tap * heads + head
                term = taps_ref[row : row + 1, :] * (
                    mixed_scr[start + ahead : start + ahead + CHUNK, columns]
                )
                total = term if total is None else total + term
                taps_here[tap] = taps_here[tap] + jnp.sum(
                    now * shifted(project_ref, start, ahead, source), axis=0, keepdims=True
                )
            grads_ref[start : start + CHUNK, source] = total.astype(bf16)
        for tap in range(CONV):
            row = tap * heads + head
            grad_taps_ref[row : row + 1, :] = taps_here[tap]
    half = normed_ref.shape[1] // 2
    send_ref[...] = rows_dot(normed_ref[:, half:], grads_ref[...], bf16)
    if near:
        taps_to_blocks(ids_ref, grad_taps_ref, send_ref, half // LANES)


def fold_blocks(keep, got_ref, own_ref, low_refs):
    size = own_ref.shape[0]
    own_ref[...] = keep[0:size, :] + got_ref[0:size, :].astype(f32)
    for k, ref in enumerate(low_refs):
        here = slice((k + 1) * size, (k + 2) * size)
        ref[0:size, :] = (keep[here, :] + got_ref[here, :].astype(f32)).astype(bf16)


def mixer_products(near, refs):
    ids_ref, normed_ref, rows_ref, gated_ref, grads_ref, grad_gate_ref, grad_taps_ref, got_ref, mix_keep_ref = refs[:9]
    values = grad_gate_ref.shape[1]
    half = normed_ref.shape[1] // 2
    gate_keep_ref = refs[-1]
    gate_keep_ref[:, :values] = rows_dot(normed_ref[:, :half], grad_gate_ref[...])
    gate_keep_ref[:, values:] = rows_dot(rows_ref[:, :half], gated_ref[...])
    if near:
        fold_blocks(gate_keep_ref, got_ref, refs[9], refs[10:-1])
    mix_keep_ref[...] = rows_dot(normed_ref[:, :half], grads_ref[...])
    if near:
        taps_to_blocks(ids_ref, grad_taps_ref, mix_keep_ref, 0)


def mixer_rows(ids_ref, grads_ref, grad_gate_ref, mix_ref, weights_ref, send_ref, keep_ref):
    values = grad_gate_ref.shape[1]
    back = cols_dot(grads_ref[...], mix_ref[...])
    back = back + cols_dot(grad_gate_ref[...], weights_ref[:, :values])
    rows_to_blocks(ids_ref, back, send_ref, keep_ref)


def mix_fold(mix_keep_ref, mix_got_ref, gate_ref, gate_got_ref, small_ref, gate_out_ref, own_ref, *low_refs):
    fold_blocks(mix_keep_ref, mix_got_ref, own_ref, low_refs)
    size = own_ref.shape[0]
    rows, columns = small_ref.shape
    for ref in low_refs:
        ref[size:, :] = jnp.zeros((ref.shape[0] - size, ref.shape[1]), ref.dtype)
        tail = jnp.concatenate([small_ref[...], jnp.zeros((ref.shape[0] - size - rows, columns), f32)], 0)
        ref[size:, :columns] = tail.astype(ref.dtype)
    gate_out_ref[...] = gate_ref[...] + gate_got_ref[...].astype(f32)


def norm_scale(rows):
    return lax.rsqrt(jnp.mean(rows * rows, axis=1, keepdims=True) + NORM_EPS)


def prepare(ids_ref, rows_ref, grad_ref, mixer_gain_ref, ffn_gain_ref, resid_ref, both_ref, gains_ref):
    size = rows_ref.shape[0]
    count = rows_ref.shape[1] // LANES
    for place in range(count):
        at = pl.multiple_of(order_of(ids_ref, place) * LANES, LANES)
        here = slice(place * LANES, (place + 1) * LANES)
        resid_ref[:, here] = rows_ref[:, pl.ds(at, LANES)].astype(f32)
        both_ref[size:, here] = grad_ref[:, pl.ds(at, LANES)]
        gains_ref[0:1, here] = mixer_gain_ref[:, pl.ds(at, LANES)]
        gains_ref[1:2, here] = ffn_gain_ref[:, pl.ds(at, LANES)]
    resid = resid_ref[...]
    both_ref[0:size, :] = (resid * norm_scale(resid) * gains_ref[0:1, :]).astype(bf16)


def fold(keep_ref, got_ref, keep_out_ref, send_ref):
    size = send_ref.shape[0]
    keep_out_ref[...] = keep_ref[0:size, :] + got_ref[0:size, :].astype(f32)
    send_ref[...] = (keep_ref[size:, :] + got_ref[size:, :].astype(f32)).astype(bf16)


def middle_norm(keep_ref, got_ref, resid_in_ref, gains_ref, resid_ref, ffn_in_ref):
    resid = resid_in_ref[...] + keep_ref[...] + got_ref[...].astype(f32)
    resid_ref[...] = resid
    ffn_in_ref[...] = (resid * norm_scale(resid) * gains_ref[1:2, :]).astype(bf16)


def place_of(ids_ref, block, count):
    return ids_ref[1 + count + block]


def feed_forward(ids_ref, refs):
    ffn_refs, grad_refs, (weights_ref,), outs, (ffn_ref, top_ref, weights_scr) = refs
    ffn_out_ref, top_out_ref, hidden_ref, grad_gate_ref, out_send, out_keep, back_send, back_keep = outs
    size = ffn_refs[0].shape[0]
    count = ffn_ref.shape[1] // LANES
    for block in range(count):
        at = pl.multiple_of(order_of(ids_ref, block) * LANES, LANES)
        weights_scr[block * LANES : (block + 1) * LANES, :] = weights_ref[pl.ds(at, LANES), :]
    for k in range(4):
        ffn_ref[k * size : (k + 1) * size, :] = ffn_refs[k][...]
        top_ref[k * size : (k + 1) * size, :] = grad_refs[k][size:, :]
    hidden_size = hidden_ref.shape[1]
    gate_up_w = weights_scr[:, : 2 * hidden_size]
    down_w = weights_scr[:, 2 * hidden_size : 3 * hidden_size]
    gate_up = dot(ffn_ref[...], gate_up_w)
    grad_hidden = dot(top_ref[...], down_w)
    gate, up = gate_up[:, :hidden_size], gate_up[:, hidden_size:]
    sig = sigmoid(gate)
    act = gate * sig
    hidden_ref[...] = (act * up).astype(bf16)
    grad_gate_ref[:, :hidden_size] = (grad_hidden * up * (sig * (1.0 + gate * (1.0 - sig)))).astype(bf16)
    grad_gate_ref[:, hidden_size:] = (grad_hidden * act).astype(bf16)
    back = cols_dot(grad_gate_ref[...], gate_up_w)
    out = cols_dot(hidden_ref[...], down_w)
    for value, send, keep in ((back, back_send, back_keep), (out, out_send, out_keep)):
        for k in range(4):
            target = send if k % 2 else keep
            half = (k // 2) * size
            target[half : half + size, :] = value[k * size : (k + 1) * size, :].astype(target.dtype)
    for block in range(count):
        at = pl.multiple_of(place_of(ids_ref, block, count) * LANES, LANES)
        here = slice(block * LANES, (block + 1) * LANES)
        ffn_out_ref[:, here] = ffn_ref[:, pl.ds(at, LANES)]
        top_out_ref[:, here] = top_ref[:, pl.ds(at, LANES)]


def feed_finish(total_ref, gate_up_ref, down_ref):
    hidden_size = down_ref.shape[0]
    for part in range(2):
        gate_up_ref[:, part, :] = total_ref[:, part * hidden_size : (part + 1) * hidden_size].astype(f32)
    down_ref[...] = jnp.transpose(total_ref[:, 2 * hidden_size : 3 * hidden_size].astype(f32))


def feed_products(ffn_ref, top_ref, hidden_ref, grad_gate_ref, out_ref):
    hidden_size = hidden_ref.shape[1]
    out_ref[:, : 2 * hidden_size] = rows_dot(ffn_ref[...], grad_gate_ref[...], out_ref.dtype)
    out_ref[:, 2 * hidden_size : 3 * hidden_size] = rows_dot(
        top_ref[...], hidden_ref[...], out_ref.dtype
    )
    rest = out_ref.shape[1] - 3 * hidden_size
    if rest:
        out_ref[:, 3 * hidden_size :] = jnp.zeros((out_ref.shape[0], rest), out_ref.dtype)


def norm_reverse(grad, rows, gain):
    scale = norm_scale(rows)
    unit = rows * scale
    inner = grad * gain
    gain_grad = jnp.sum(grad * unit, axis=0, keepdims=True)
    return scale * (inner - unit * jnp.mean(inner * unit, axis=1, keepdims=True)), gain_grad


def middle_back(
    back_keep_ref, back_got_ref, resid_ref, both_ref, gains_ref, grad_ref, low_ref, gain_grad_ref
):
    grad_ffn_in = back_keep_ref[...] + back_got_ref[...].astype(f32)
    grad, gain_grad = norm_reverse(grad_ffn_in, resid_ref[...], gains_ref[1:2, :])
    grad = grad + both_ref[both_ref.shape[0] // 2 :, :].astype(f32)
    grad_ref[...] = grad
    low_ref[...] = grad.astype(bf16)
    gain_grad_ref[...] = gain_grad


def last_out(ids_ref, keep_ref, got_ref, resid_ref, out_ref, scr):
    scr[...] = resid_ref[...] + keep_ref[...] + got_ref[...].astype(f32)
    count = out_ref.shape[1] // LANES
    for block in range(count):
        at = pl.multiple_of(place_of(ids_ref, block, count) * LANES, LANES)
        out_ref[:, block * LANES : (block + 1) * LANES] = scr[:, pl.ds(at, LANES)].astype(bf16)


def last_grad(
    ids_ref, keep_ref, got_ref, resid_in_ref, gains_ref, grad_ref, gain_grad_ref, out_ref, gains_out_ref, scr, gain_scr
):
    grad_normed = keep_ref[...] + got_ref[...].astype(f32)
    grad, gain_grad = norm_reverse(grad_normed, resid_in_ref[...], gains_ref[0:1, :])
    scr[...] = grad + grad_ref[...]
    gain_scr[0:1, :] = gain_grad
    gain_scr[1:2, :] = gain_grad_ref[...]
    count = out_ref.shape[1] // LANES
    for block in range(count):
        at = pl.multiple_of(place_of(ids_ref, block, count) * LANES, LANES)
        here = slice(block * LANES, (block + 1) * LANES)
        out_ref[:, here] = scr[:, pl.ds(at, LANES)]
        gains_out_ref[:, here] = gain_scr[:, pl.ds(at, LANES)]


def call(kernel, outs, operands, scratch=(), name=None, scalar=True):
    specs = [pl.BlockSpec(memory_space=pltpu.VMEM)] * len(operands)
    if scalar:
        specs[0] = pl.BlockSpec(memory_space=pltpu.SMEM)
    return pl.pallas_call(
        kernel,
        out_shape=tuple(jax.ShapeDtypeStruct(shape, kind) for shape, kind in outs),
        in_specs=specs,
        out_specs=tuple([pl.BlockSpec(memory_space=pltpu.VMEM)] * len(outs)),
        scratch_shapes=[pltpu.VMEM(shape, kind) for shape, kind in scratch],
        compiler_params=pltpu.CompilerParams(vmem_limit_bytes=56 * 2**20),
        name=name,
    )(*operands)


def cut_list(items, sizes):
    parts, at = [], 0
    for size in sizes:
        parts.append(items[at : at + size])
        at += size
    return parts


def run_forward(near, ids, rows, mix, taps, log_rates, bias, value_width):
    length = rows[0].shape[0] // 2 * len(rows)
    model = rows[0].shape[1]
    wide = mix[0].shape[1]
    columns = wide - LANES
    channels = taps.shape[1]
    heads = taps.shape[0] // CONV
    key_width = (channels - value_width) // 2
    pair = (length // CHUNK, heads)
    values = heads * value_width

    def kernel(*refs):
        mixer_forward(near, cut_list(refs, (4, len(rows), len(mix), 9, 5)))

    return call(
        kernel,
        (
            ((length, columns), f32),
            ((length, LANES), f32),
            ((length, values), f32),
            (pair + (key_width, value_width), f32),
            ((length, values), f32),
            (pair + (CHUNK, CHUNK), f32),
            ((length, model), bf16),
            ((model, wide), bf16),
            (taps.shape, f32),
        ),
        (ids, taps, log_rates, bias, *rows, *mix),
        (
            (pair + (CHUNK, key_width), bf16),
            (pair + (CHUNK, key_width), f32),
            (pair + (CHUNK, CHUNK), bf16),
            (pair + (CHUNK, key_width), bf16),
            (pair + (CHUNK, value_width), f32),
        ),
        "mixer_forward",
    )


def run_backward(near, ids, grad_out, log_rates, bias, kept):
    project, _, out, states, _, _, normed, mix, taps = kept
    length, model = normed.shape
    values = out.shape[1]
    wide = mix.shape[1]
    heads, key_width, value_width = states.shape[1:]
    pair = (length // CHUNK, heads)

    def kernel(*refs):
        mixer_backward(near, cut_list(refs, (4, len(kept), 4, 7)))

    return call(
        kernel,
        (
            ((length, wide), bf16),
            (taps.shape, f32),
            ((2, LANES), f32),
            ((model // 2, wide), bf16),
        ),
        (ids, log_rates, bias, grad_out, *kept),
        (
            (pair + (key_width, value_width), f32),
            ((length, values), f32),
            (pair + (CHUNK, key_width), bf16),
            (pair + (CHUNK, key_width), bf16),
            (pair + (CHUNK, CHUNK), bf16),
            (pair + (CHUNK, key_width), bf16),
            ((length + 8, heads * taps.shape[1]), f32),
        ),
        "mixer_backward",
    )


def swap(array, axis, size, offset):
    return lax.ppermute(array, axis, [(i, i ^ offset) for i in range(size)])


def after(arrays, others):
    kept, _ = lax.optimization_barrier((arrays, others))
    return kept


def per_device(
    layer_in,
    mixer_gain,
    w_mix,
    w_rates,
    conv_taps,
    a_log,
    dt_bias,
    head_gain,
    w_out,
    ffn_gain,
    w_gate_up,
    w_down,
    out_grad,
):
    size = lax.axis_size("dp")
    ranks = lax.axis_size("tensor")
    depth, heads, width = w_mix.shape
    model = layer_in.shape[1]
    hidden = w_gate_up.shape[2]
    value_size = w_out.shape[0]
    rows = layer_in.shape[0]
    taps_shape = conv_taps.shape
    part = taps_shape[2]
    near = size == 8 and depth == LANES and 2 * part == LANES
    half = size // 2
    rank, own = lax.axis_index("tensor"), lax.axis_index("dp")
    blocks = model // LANES
    if near:
        offsets = [2 * p for p in range(half)] + [2 * p + 1 for p in range(half)]
        order = own ^ jnp.array(offsets, jnp.int32)
        places = [offsets.index(k) for k in range(size)]
        index = own ^ jnp.arange(size, dtype=jnp.int32)
        place = jnp.where(index % 2 == 0, index // 2, half + index // 2)
        assert places == [k // 2 if k % 2 == 0 else half + k // 2 for k in range(size)]
    else:
        order = place = jnp.arange(blocks, dtype=jnp.int32)
    ids = jnp.concatenate([jnp.full((1,), rank, jnp.int32), order, place])

    def near_z(shard):
        return [shard] + [swap(shard, "dp", size, 2 * p) for p in range(1, half)]

    def near_x(shards, own_side):
        return [own_side, swap(jnp.concatenate(shards[1:], 0), "dp", size, 1)]

    def far(shard):
        return lax.all_gather(shard, "dp", axis=0, tiled=True)

    def rows_y(block):
        return swap(block, "tensor", ranks, 2)

    def rows_core(block):
        return swap(block, "tensor", ranks, 1)

    def gather_rows(block):
        across = rows_y(block)
        return [block, rows_core(block), across, rows_core(across)]

    def sum_rows(send, keep, name):
        got = rows_core(send)
        shape = (rows, model)
        keep, send = call(fold, ((shape, f32), (shape, bf16)), (keep, got), name=name, scalar=False)
        return keep, rows_y(send)

    channels = width - head_gain.shape[0]
    values = value_size
    rates_tile = jnp.pad(w_rates.reshape(depth, 2 * heads), ((0, 0), (0, LANES - 2 * heads)))
    if near:
        taps_tile = conv_taps.reshape(CONV * heads, part)
        taps_tile = jnp.pad(taps_tile, ((0, depth - CONV * heads), (LANES - part, 0)))
        rates_tile = rates_tile + taps_tile
    mix_shard = jnp.concatenate(
        [w_mix[:, :, :channels].reshape(depth, heads * channels), rates_tile], 1
    )
    gate_shard = jnp.concatenate([w_mix[:, :, channels:].reshape(depth, values), w_out.T], 1)
    filler = -3 * hidden % LANES
    ffn_shard = jnp.concatenate(
        [w_gate_up.reshape(depth, 2 * hidden), w_down.T, jnp.zeros((depth, filler), bf16)], 1
    )

    if near:
        mix_z = near_z(mix_shard)
        mix_side = swap(mix_shard, "dp", size, 1)
    square = (rows, model)
    resid_in, both, gains = call(
        prepare,
        ((square, f32), ((2 * rows, model), bf16), ((2, model), f32)),
        (ids, layer_in, out_grad, mixer_gain.reshape(1, -1), ffn_gain.reshape(1, -1)),
        name="prepare",
    )
    both_all = gather_rows(both)
    ffn_full = far(after(ffn_shard, (mix_z, mix_side, both_all[2])) if near else ffn_shard)
    if near:
        gate_shard = after(gate_shard, (mix_z, mix_side, both))
        gate_z = near_z(gate_shard)
        gate_side = swap(gate_shard, "dp", size, 1)
        mix_slots = mix_z + near_x(mix_z, mix_side)
        taps = jnp.zeros((CONV * heads, part * size), f32)
    else:
        mix_slots = [far(mix_shard)]
        gate_slots = [far(gate_shard)]
        taps = lax.all_gather(conv_taps, "dp", axis=2, tiled=True).astype(f32)
        taps = taps.reshape(CONV * heads, part * size)

    first_head = rank * heads

    def on_lanes(per_head):
        here = lax.dynamic_slice_in_dim(per_head, first_head, heads)
        pairs = jnp.stack([here, jnp.zeros_like(here)], 1).reshape(1, -1)
        return jnp.pad(pairs, ((0, 0), (0, LANES - pairs.shape[1])))

    def off_lanes(row):
        here = row[: 2 * heads : 2]
        return lax.dynamic_update_slice_in_dim(jnp.zeros_like(a_log), here, first_head, 0)

    lanes = (on_lanes(a_log), on_lanes(dt_bias))
    gain_row = head_gain.reshape(1, -1)
    kept = run_forward(near, ids, both_all, mix_slots, taps, *lanes, head_gain.shape[0])
    heads_out, normed_rows, mix_full = kept[2], kept[6], kept[7]
    if near:
        gate_slots = gate_z + near_x(gate_z, gate_side)
    tokens = rows * ranks
    block_pair = (2 * rows, model)
    gated, gate, gate_full, out_send, out_keep = call(
        out_product,
        (
            ((tokens, values), bf16),
            ((tokens, values), f32),
            ((model, 2 * values), bf16),
            (block_pair, bf16),
            (block_pair, f32),
        ),
        (ids, gain_row, normed_rows, heads_out, *gate_slots),
        (),
        "out_product",
    )
    out_keep, out_got = sum_rows(out_send, out_keep, "out_fold")
    resid, ffn_in = call(
        middle_norm, ((square, f32), (square, bf16)), (out_keep, out_got, resid_in, gains), name="middle_norm", scalar=False
    )
    ffn_all = gather_rows(ffn_in)

    def ffn_kernel(ids_ref, *refs):
        feed_forward(ids_ref, cut_list(refs, (4, 4, 1, 8, 3)))

    ffn_rows, top_rows, hidden_low, grad_gate, ffn_send, ffn_keep, back_send, back_keep = call(
        ffn_kernel,
        (
            ((tokens, model), bf16),
            ((tokens, model), bf16),
            ((tokens, hidden), bf16),
            ((tokens, 2 * hidden), bf16),
            (block_pair, bf16),
            (block_pair, f32),
            (block_pair, bf16),
            (block_pair, f32),
        ),
        (ids, *ffn_all, *both_all, ffn_full),
        (((tokens, model), bf16), ((tokens, model), bf16), (ffn_full.shape, bf16)),
        "feed_forward",
    )
    split = model // 2

    def scatter_x(send):
        return swap(send, "dp", size, 1) if near else send

    back_keep, back_got = sum_rows(back_send, back_keep, "back_fold")
    (ffn_grads,) = call(
        feed_products,
        (((model, 3 * hidden + filler), bf16 if near else f32),),
        (ffn_rows, top_rows, hidden_low, grad_gate),
        name="feed_products",
        scalar=False,
    )
    ffn_total = lax.psum_scatter(ffn_grads, "dp", scatter_dimension=0, tiled=True)
    grad_resid, mix_low, ffn_gain_grad = call(
        middle_back,
        ((square, f32), (square, bf16), ((1, model), f32)),
        (back_keep, back_got, resid, both, gains),
        name="middle_back",
        scalar=False,
    )
    mix_all = gather_rows(mix_low)
    ffn_keep, ffn_got = sum_rows(ffn_send, ffn_keep, "ffn_fold")
    (layer_out,) = call(
        last_out, ((square, bf16),), (ids, ffn_keep, ffn_got, resid), ((square, f32),), "last_out"
    )
    mix_all, layer_out = lax.optimization_barrier((mix_all, layer_out))
    grad_rows, grad_out, gate_grad, head_gain_grad, gate_send = call(
        gate_back,
        (
            ((tokens, model), bf16),
            ((tokens, values), f32),
            ((tokens, values), bf16),
            (gain_row.shape, f32),
            ((split, 2 * values), bf16),
        ),
        (ids, gain_row, normed_rows, heads_out, gated, gate, gate_full, *mix_all),
        (),
        "gate_back",
    )
    gate_got = scatter_x(gate_send)
    grads, taps_grad, lanes_grad, mix_send = run_backward(near, ids, grad_out, *lanes, kept)
    mix_got = scatter_x(mix_send)

    def products_kernel(*refs):
        mixer_products(near, refs)

    def blocks_of(send, more=0):
        columns = send.shape[1]
        return (((depth, columns), f32),) + (((depth + more, columns), bf16),) * (half - 1)

    keep_shape = ((split, 2 * values), f32)
    norm_send, norm_keep = call(
        mixer_rows,
        ((block_pair, bf16), (block_pair, f32)),
        (ids, grads, gate_grad, mix_full, gate_full),
        name="mixer_rows",
    )
    norm_got = rows_core(norm_send)
    norm_keep, norm_send = call(
        fold, ((square, f32), (square, bf16)), (norm_keep, norm_got), name="norm_fold", scalar=False
    )
    gate_got, norm_send = lax.optimization_barrier((gate_got, norm_send))
    norm_got = rows_y(norm_send)
    mix_keep, *gate_parts = call(
        products_kernel,
        ((mix_send.shape, f32),) + (blocks_of(gate_send) if near else (keep_shape,)),
        (ids, normed_rows, grad_rows, gated, grads, gate_grad, taps_grad, gate_got),
        (keep_shape,) if near else (),
        "mixer_products",
    )

    def far_sum(parts, got):
        if near:
            own, lows = parts[0], parts[1:]
            return [own] + [swap(low, "dp", size, 2 * (p + 1)) for p, low in enumerate(lows)]
        return [
            lax.psum_scatter(
                jnp.concatenate([parts[0], got.astype(f32)], 0), "dp", scatter_dimension=0, tiled=True
            )
        ]

    def add_up(blocks):
        total = blocks[0]
        for block in blocks[1:]:
            total = total + block.astype(f32)
        return total

    gate_blocks = far_sum(gate_parts, gate_got)
    in_grad, gains_grad = call(
        last_grad,
        ((square, f32), ((2, model), f32)),
        (ids, norm_keep, norm_got, resid_in, gains, grad_resid, ffn_gain_grad),
        ((square, f32), ((2, model), f32)),
        "last_grad",
    )

    small = jnp.concatenate(
        [
            gains_grad.reshape(-1),
            head_gain_grad.reshape(-1),
            off_lanes(lanes_grad[0]),
            off_lanes(lanes_grad[1]),
        ]
    )
    length = small.size
    small = jnp.pad(small, (0, -length % (8 * LANES))).reshape(8, -1)
    mix_parts = [mix_keep]
    for offset in (1, 2):
        small = small + swap(small, "tensor", ranks, offset)
    mix_parts = [mix_keep]
    if near:
        small = small + swap(small, "dp", size, 1)
        gate_sum, *mix_parts = call(
            mix_fold,
            (((depth, 2 * values), f32),) + blocks_of(mix_send, 16),
            (mix_keep, mix_got, gate_blocks[0], gate_blocks[1], small),
            name="mix_fold",
            scalar=False,
        )
        gate_blocks = [gate_sum] + gate_blocks[2:]
    mix_blocks = far_sum(mix_parts, mix_got)
    grad_w_gate_up, grad_w_down = call(
        feed_finish,
        ((w_gate_up.shape, f32), (w_down.shape, f32)),
        (ffn_total,),
        name="feed_finish",
        scalar=False,
    )
    own_block, grad_w_gate_up, grad_w_down = lax.optimization_barrier(
        (mix_blocks[0], grad_w_gate_up, grad_w_down)
    )
    mix_blocks = [own_block] + mix_blocks[1:]

    if near:
        small = add_up([small] + [got[depth : depth + 8, : small.shape[1]] for got in mix_blocks[1:]])
        mix_blocks = [mix_blocks[0]] + [got[:depth] for got in mix_blocks[1:]]
    else:
        small = lax.psum(small, "dp")
    small = small.reshape(-1)[:length]
    grad_mixer_gain, grad_ffn_gain = small[:model], small[model : 2 * model]
    small = small[2 * model :]
    grad_head_gain, small = small[: head_gain.size], small[head_gain.size :]
    grad_a_log, grad_dt_bias = small[: a_log.size], small[a_log.size :]

    gate_total = add_up(gate_blocks)
    mix_total = add_up(mix_blocks)
    grad_w_mix = jnp.concatenate(
        [
            mix_total[:, : heads * channels].reshape(depth, heads, channels),
            gate_total[:, :values].reshape(depth, heads, -1),
        ],
        2,
    )
    grad_w_rates = mix_total[:, heads * channels : heads * channels + 2 * heads].reshape(w_rates.shape)
    if near:
        grad_taps = mix_total[: CONV * heads, mix_total.shape[1] - part :].reshape(taps_shape)
    else:
        grad_taps = lax.psum_scatter(
            taps_grad.reshape(CONV, heads, -1), "dp", scatter_dimension=2, tiled=True
        )
    return (
        layer_out,
        in_grad,
        grad_mixer_gain,
        grad_w_mix,
        grad_w_rates,
        grad_taps,
        grad_a_log,
        grad_dt_bias,
        grad_head_gain,
        gate_total[:, values:].T,
        grad_ffn_gain,
        grad_w_gate_up,
        grad_w_down,
    )


def solution(mesh):
    return jax.shard_map(
        per_device,
        mesh=mesh,
        in_specs=(
            P(("dp", "tensor"), None),
            P(),
            P("dp", "tensor", None),
            P("dp", "tensor", None),
            P(None, "tensor", "dp"),
            P(),
            P(),
            P(),
            P("tensor", "dp"),
            P(),
            P("dp", None, "tensor"),
            P("tensor", "dp"),
            P(("dp", "tensor"), None),
        ),
        out_specs=(
            P(("dp", "tensor"), None),
            P(("dp", "tensor"), None),
            P(),
            P("dp", "tensor", None),
            P("dp", "tensor", None),
            P(None, "tensor", "dp"),
            P(),
            P(),
            P(),
            P("tensor", "dp"),
            P(),
            P("dp", None, "tensor"),
            P("tensor", "dp"),
        ),
        check_vma=False,
    )
```
